32 devices in a mesh: fsdp: 8 (over z, x), ctx: 2 (over y), tp: 2 (over core).
Axes of the slice: x: 2, y: 2, z: 4, core: 2. Of those that a mesh axis runs over, the one named last changes fastest.
Arguments:
- latents: float32 [64, 256, 16], P(('fsdp', 'ctx')), may hold values from -6 to 6
- noise: float32 [64, 256, 16], P(('fsdp', 'ctx')), may hold values from -6 to 6
- timesteps: int32 [64], P(('fsdp', 'ctx')), may hold values from 0 to 999
- labels: int32 [64], P(('fsdp', 'ctx')), may hold values from 0 to 999
- owners: int32 [1152], replicated, may hold values from 0 to 15, as said below
- tiles_low: bfloat16 [2, 1152, 128, 128], P('tp', ('fsdp', 'ctx')), may hold values from -0.5 to 0.5
- tiles_master: float32 [2, 1152, 128, 128], P('tp', ('fsdp', 'ctx')), may hold values from -0.5 to 0.5
- tiles_first: float32 [2, 1152, 128, 128], P('tp', ('fsdp', 'ctx')), may hold values from -0.0024414062 to 0.0024414062
- tiles_second: float32 [2, 1152, 128, 128], P('tp', ('fsdp', 'ctx')), may hold values from 2.3689173e-08 to 9.475669e-08
- bases: float32 [2, 1152, 2, 128], P('tp', ('fsdp', 'ctx')), may hold values from -5 to 5
- else_low: bfloat16 [4464640], P(('fsdp', 'ctx', 'tp')), may hold values from -1 to 1
- else_master: float32 [4464640], P(('fsdp', 'ctx', 'tp')), may hold values from -1 to 1
- else_first: float32 [4464640], P(('fsdp', 'ctx', 'tp')), may hold values from -0.0036939091 to 0.0036939091
- else_second: float32 [4464640], P(('fsdp', 'ctx', 'tp')), may hold values from 2.3689174e-08 to 3.0322142e-06
Outputs:
- loss: float32 [], replicated
- grad_norm: float32 [], replicated
- tiles_master_new: float32 [2, 1152, 128, 128], P('tp', ('fsdp', 'ctx'))
- tiles_first_new: float32 [2, 1152, 128, 128], P('tp', ('fsdp', 'ctx'))
- tiles_second_new: float32 [2, 1152, 128, 128], P('tp', ('fsdp', 'ctx'))
- tiles_low_new: bfloat16 [2, 1152, 128, 128], P('tp', ('fsdp', 'ctx'))
- else_master_new: float32 [4464640], P(('fsdp', 'ctx', 'tp'))
- else_first_new: float32 [4464640], P(('fsdp', 'ctx', 'tp'))
- else_second_new: float32 [4464640], P(('fsdp', 'ctx', 'tp'))
- else_low_new: bfloat16 [4464640], P(('fsdp', 'ctx', 'tp'))
The draws below stay inside these ranges and needn't reach their ends.
Inputs may be any that keep to these rules, and one draw needn't show every extreme that they name: `owners`: each owner is named by exactly 72 tiles.
All inputs are finite; a program needn't handle non-finite values.
Results may differ from the reference program's by a relative error of at most 0.0034.
Values may be sent and summed in bfloat16 or wider, within the bound.
No kernel may reach another device: no remote copies, remote signals or barrier semaphores. Data moves between devices by JAX's collectives and lax.ppermute only.
A program may use at most 448 MiB of HBM per device.

```python
import math
import jax
import jax.numpy as jnp
from jax import lax

D = 1024
H = 16
HD = 64
F = 4096
P_SIZE = 16
TFREQ = 256
NCLS = 1000
GRID = 16
L = 2
B = 128
IMAGES = 64
S = 256
TILES = 1152
SLOT_DEV = 72
ELSE_N = 4464640
P_ALL = 42213376
N_TP = 2


def slot_order(key):
    owner_list = (jax.random.permutation(jax.random.fold_in(key, 7), TILES) // SLOT_DEV).astype(jnp.int32)
    return (owner_list, jnp.argsort(owner_list, stable=True))


def draw_owners(key, part):
    return slot_order(key)[0]


def tile_scales():
    head_width = D // N_TP
    hidden_width = F // N_TP
    area = B * B
    amounts = [D * 3 * head_width // area, head_width * D // area, D * hidden_width // area, hidden_width * D // area, D * 6 * head_width // area]
    factors = [D ** (-0.5), 4.0 * D ** (-0.5), D ** (-0.5), F ** (-0.5), D ** (-0.5)]
    within = jnp.arange(TILES) % (TILES // L)
    scaling = jnp.zeros((TILES,), jnp.float32)
    border = 0
    for amount, factor in zip(amounts, factors):
        scaling = jnp.where((within >= border) & (within < border + amount), factor, scaling)
        border += amount
    return scaling


def tile_draw(key, salt):
    ordering = slot_order(key)[1]
    scaling = tile_scales()[ordering]
    values = jax.random.truncated_normal(jax.random.fold_in(key, salt), -4.0, 4.0, (N_TP, TILES, B, B), jnp.float32)
    return values * scaling[None, :, None, None]


def draw_tiles_low(key, part):
    return tile_draw(key, 11).astype(jnp.bfloat16)


def draw_tiles_master(key, part):
    return tile_draw(key, 13)


def else_draw(key, salt):
    pieces = [(P_SIZE * D, P_SIZE ** (-0.5)), (NCLS * D, 2.0 * D ** (-0.5)), (TFREQ * D, TFREQ ** (-0.5)), (D * D, D ** (-0.5)), (2 * D * D, D ** (-0.5)), (D * P_SIZE, D ** (-0.5))]
    position = jnp.arange(ELSE_N)
    scaling = jnp.zeros((ELSE_N,), jnp.float32)
    border = 0
    for amount, factor in pieces:
        scaling = jnp.where((position >= border) & (position < border + amount), factor, scaling)
        border += amount
    values = jax.random.truncated_normal(jax.random.fold_in(key, salt), -4.0, 4.0, (ELSE_N,), jnp.float32)
    return values * scaling


def draw_else_low(key, part):
    return else_draw(key, 17).astype(jnp.bfloat16)


def draw_else_master(key, part):
    return else_draw(key, 19)


def draw_else_first(key, part):
    key = jax.random.fold_in(key, 23)
    values = jax.random.truncated_normal(key, -4.0, 4.0, (ELSE_N,), jnp.float32)
    return values * P_ALL ** (-0.5)


def draw_else_second(key, part):
    key = jax.random.fold_in(key, 29)
    lowest, highest = (1.0, 4.0)
    spread = jax.random.uniform(key, (ELSE_N,), jnp.float32)
    return jnp.exp(math.log(lowest / P_ALL) + spread * math.log(highest))


def touch_ends(drawn, key, low, top_value):
    place = [jax.random.randint(jax.random.fold_in(key, axis), (), 0, length) for axis, length in enumerate(drawn.shape)]
    widest = drawn.shape.index(max(drawn.shape))
    next_to = place[:widest] + [(place[widest] + 1) % drawn.shape[widest]] + place[widest + 1:]
    return drawn.at[tuple(place)].set(low).at[tuple(next_to)].set(top_value)


def levels(rng, extent, cuts, smallest, high):
    gain = 1.0
    for axis_at, parts in cuts:
        draws = jax.random.uniform(jax.random.fold_in(jax.random.fold_in(rng, 6), axis_at), (parts,), jnp.float32, smallest / len(cuts), high / len(cuts))
        gain = gain * jnp.repeat(jnp.exp(draws), extent[axis_at] // parts).reshape((-1,) + (1,) * (len(extent) - 1 - axis_at))
    return gain


def bell_draw(rng, dims, width, reach, cuts=(), held_as=jnp.bfloat16):
    array = jax.random.normal(rng, dims, jnp.float32) * width
    if len(cuts) > 0:
        array = levels(rng, dims, cuts, -0.22, 0.18) * array
    return jnp.clip(array, min=-reach, max=reach).astype(held_as)


def setup_inputs(seed: int = 0) -> dict:
    splits = jax.random.split(jax.random.key(seed), 15)
    latents = bell_draw(splits[0], (IMAGES, S, P_SIZE), 1.0, 6.0, ((0, 16),), jnp.float32)
    noise = bell_draw(splits[1], (IMAGES, S, P_SIZE), 1.0, 6.0, ((0, 16),), jnp.float32)
    timesteps = touch_ends(jax.random.randint(splits[2], (IMAGES,), 0, 1000), jax.random.fold_in(splits[2], 1), 0, 999).astype(jnp.int32)
    labels = touch_ends(jax.random.randint(splits[3], (IMAGES,), 0, NCLS), jax.random.fold_in(splits[3], 1), 0, NCLS - 1).astype(jnp.int32)
    owners = draw_owners(jax.random.fold_in(splits[14], 71), 0)
    tiles_low = draw_tiles_low(jax.random.fold_in(splits[14], 71), 0)
    tiles_master = draw_tiles_master(jax.random.fold_in(splits[14], 71), 0)
    tiles_first = bell_draw(splits[7], (N_TP, TILES, B, B), (P_ALL ** -0.5), 0.0024414062, ((0, 2), (1, 16)), jnp.float32)
    tiles_second = jnp.clip(jnp.exp(math.log(9.475669315861524e-08) - 1.3862944 * jax.random.uniform(splits[8], (N_TP, TILES, B, B), jnp.float32) ** levels(splits[8], (N_TP, TILES, B, B), ((0, 2), (1, 16)), -0.2, 0.2)), 2.368917328965381e-08, 9.475669315861524e-08)
    bases = bell_draw(splits[9], (N_TP, TILES, 2, B), 1.0, 5.0, ((0, 2), (1, 16)), jnp.float32)
    else_low = draw_else_low(jax.random.fold_in(splits[14], 71), 0)
    else_master = draw_else_master(jax.random.fold_in(splits[14], 71), 0)
    else_first = draw_else_first(jax.random.fold_in(splits[14], 71), 0)
    else_second = draw_else_second(jax.random.fold_in(splits[14], 71), 0)
    return {"latents": latents, "noise": noise, "timesteps": timesteps, "labels": labels, "owners": owners, "tiles_low": tiles_low, "tiles_master": tiles_master, "tiles_first": tiles_first, "tiles_second": tiles_second, "bases": bases, "else_low": else_low, "else_master": else_master, "else_first": else_first, "else_second": else_second}


@jax.custom_vjp
def low(v):
    return lax.optimization_barrier(v.astype(jnp.bfloat16)).astype(jnp.float32)

@jax.custom_vjp
def low_back(v):
    return v

def low_keep(v):
    return (low(v), None)

def low_pass(kept, grad):
    return (grad,)

def back_keep(v):
    return (v, None)

def back_low(kept, grad):
    return (low(grad),)
low.defvjp(low_keep, low_pass)
low_back.defvjp(back_keep, back_low)
HIGHEST = lax.Precision.HIGHEST
EPS_NORM = 1e-06
RATE = 0.02
DECAY = 0.1

def matmul(left_op, right_op):
    return jnp.dot(left_op, right_op, precision=HIGHEST)

def contract(formula, left_op, right_op):
    return jnp.einsum(formula, left_op, right_op, precision=HIGHEST)

def normed(stream):
    centred = stream - lax.optimization_barrier(jnp.mean(stream, -1, keepdims=True))
    return centred * lax.rsqrt(lax.optimization_barrier(jnp.mean(centred * centred, -1, keepdims=True)) + EPS_NORM)

def modulate(stream, offset, factor):
    return normed(stream) * (1.0 + factor) + offset

def time_features(time_steps):
    half_count = TFREQ // 2
    freqs = jnp.exp(-math.log(10000.0) * jnp.arange(half_count, dtype=jnp.float32) / half_count)
    angles = time_steps.astype(jnp.float32)[:, None] * freqs[None, :]
    return jnp.concatenate([jnp.cos(angles), jnp.sin(angles)], -1)

def position_table(token_ids):
    quarter = D // 4
    omegas = 1.0 / 10000.0 ** (jnp.arange(quarter, dtype=jnp.float32) / quarter)
    row_angle = (token_ids // GRID).astype(jnp.float32)[:, None] * omegas[None, :]
    col_angle = (token_ids % GRID).astype(jnp.float32)[:, None] * omegas[None, :]
    return jnp.concatenate([jnp.sin(row_angle), jnp.cos(row_angle), jnp.sin(col_angle), jnp.cos(col_angle)], -1)

def signal_level(time_steps):
    phase = (time_steps.astype(jnp.float32) / 1000.0 + 0.008) / 1.008 * (math.pi / 2)
    return jnp.cos(phase) ** 2

def shard_shapes(tp_parts):
    head_width = D // tp_parts
    hidden_width = F // tp_parts
    return [(D, 3 * head_width), (head_width, D), (D, hidden_width), (hidden_width, D), (D, 6 * head_width)]

def untile(tile_set, height, breadth):
    block = tile_set.shape[-1]
    return tile_set.reshape(height // block, breadth // block, block, block).transpose(0, 2, 1, 3).reshape(height, breadth)

def retile(matrix):
    height, breadth = matrix.shape
    return matrix.reshape(height // B, B, breadth // B, B).transpose(0, 2, 1, 3).reshape(-1, B, B)

def unpack_layers(tile_set, tp_parts):
    layer_list = []
    cursor = 0
    for layer_no in range(L):
        matrices = []
        for height, breadth in shard_shapes(tp_parts):
            amount = height * breadth // (B * B)
            matrices.append(untile(tile_set[cursor:cursor + amount], height, breadth))
            cursor += amount
        layer_list.append(matrices)
    return layer_list

def pack_layers(layer_list):
    return jnp.concatenate([retile(matrix) for matrices in layer_list for matrix in matrices], 0)

def else_shapes():
    return [(P_SIZE, D), (NCLS, D), (TFREQ, D), (D, D), (D, 2 * D), (D, P_SIZE)]

def split_else(flat_params):
    components = []
    cursor = 0
    for height, breadth in else_shapes():
        components.append(flat_params[cursor:cursor + height * breadth].reshape(height, breadth))
        cursor += height * breadth
    return components

def reflection(vectors):
    outer_prod = vectors[..., :, None] * vectors[..., None, :]
    return jnp.eye(vectors.shape[-1], dtype=jnp.float32) - 2.0 * outer_prod / lax.optimization_barrier(jnp.sum(vectors * vectors, -1))[..., None, None]

def rotate(left_basis, middle, right_basis):
    return contract('...ab,...bc->...ac', contract('...ab,...bc->...ac', left_basis, middle), right_basis)

def adam_finish(turned, master_state, first_state, second_state, left_basis, right_basis):
    first_new = 0.5 * first_state + 0.5 * turned
    second_new = 0.5 * second_state + 0.5 * turned * turned
    direction = first_new / (jnp.sqrt(second_new) + 1e-08)
    return (master_state - RATE * rotate(left_basis, direction, right_basis), first_new, second_new)

def adamw_flat(grad_clipped, master_state, first_state, second_state):
    first_new = 0.5 * first_state + 0.5 * grad_clipped
    second_new = 0.5 * second_state + 0.5 * grad_clipped * grad_clipped
    master_new = master_state - RATE * (first_new / (jnp.sqrt(second_new) + 1e-08) + DECAY * master_state)
    return (master_new, first_new, second_new)

def group_loss(params, noisy_input, target, features, onehot, positions):
    patch_weight, class_table, time_first, time_second, final_weight, head_weight = params[0]
    w_query, w_key, w_value, w_proj, w_up, w_down, w_mod = params[1]
    images = noisy_input.shape[0]
    time_hidden = matmul(low(features), time_first)
    condition = matmul(low(jax.nn.silu(time_hidden)), time_second) + matmul(onehot, class_table)
    cond_act = low(jax.nn.silu(condition))
    stream = low_back(contract('gsp,pd->gsd', low(noisy_input), patch_weight)) + positions[None]
    for layer_no in range(L):
        modes = matmul(cond_act, w_mod[layer_no])[:, None, :]
        shift_attn, scale_attn, gate_attn, shift_mlp, scale_mlp, gate_mlp = jnp.split(modes, 6, -1)
        normed_in = low(modulate(stream, shift_attn, scale_attn))
        queries = low_back(low(contract('gsd,de->gse', normed_in, w_query[layer_no]))).reshape(images, S, H, HD)
        key_rows = low_back(low(contract('gsd,de->gse', normed_in, w_key[layer_no]))).reshape(images, S, H, HD)
        value_rows = low_back(low(contract('gsd,de->gse', normed_in, w_value[layer_no]))).reshape(images, S, H, HD)
        scores = low_back(contract('gqhe,gkhe->ghqk', queries, key_rows) * HD ** (-0.5))
        exponent = jnp.exp(scores - lax.optimization_barrier(jnp.max(scores, -1, keepdims=True)))
        probabilities = low(exponent / lax.optimization_barrier(jnp.sum(exponent, -1, keepdims=True)))
        attended = low_back(low(contract('ghqk,gkhe->gqhe', probabilities, value_rows))).reshape(images, S, D)
        stream = stream + gate_attn * low_back(contract('gse,ed->gsd', attended, w_proj[layer_no]))
        normed_mid = low(modulate(stream, shift_mlp, scale_mlp))
        hidden = low_back(contract('gsd,df->gsf', normed_mid, w_up[layer_no]))
        activation = low(jax.nn.gelu(hidden, approximate=True))
        stream = stream + gate_mlp * low_back(contract('gsf,fd->gsd', activation, w_down[layer_no]))
    final_modes = matmul(cond_act, final_weight)[:, None, :]
    shift_out, scale_out = jnp.split(final_modes, 2, -1)
    predicted = low_back(contract('gsd,dp->gsp', low(modulate(stream, shift_out, scale_out)), head_weight))
    return jnp.sum((predicted - target) ** 2) / (IMAGES * S * P_SIZE)

def reference(latents, noise, timesteps, labels, owners, tiles_low, tiles_master, tiles_first, tiles_second, bases, else_low, else_master, else_first, else_second):
    ordering = jnp.argsort(owners, stable=True).astype(jnp.int32)
    inverse = jnp.argsort(ordering).astype(jnp.int32)
    head_width = D // N_TP
    hidden_width = F // N_TP
    shards = [unpack_layers(tiles_low[tp_no].astype(jnp.float32)[inverse], N_TP) for tp_no in range(N_TP)]
    layer_sets = [[], [], [], [], [], [], []]
    for layer_no in range(L):
        here = [shards[tp_no][layer_no] for tp_no in range(N_TP)]
        layer_sets[0].append(jnp.concatenate([matrices[0][:, :head_width] for matrices in here], 1))
        layer_sets[1].append(jnp.concatenate([matrices[0][:, head_width:2 * head_width] for matrices in here], 1))
        layer_sets[2].append(jnp.concatenate([matrices[0][:, 2 * head_width:] for matrices in here], 1))
        layer_sets[3].append(jnp.concatenate([matrices[1] for matrices in here], 0))
        layer_sets[4].append(jnp.concatenate([matrices[2] for matrices in here], 1))
        layer_sets[5].append(jnp.concatenate([matrices[3] for matrices in here], 0))
        layer_sets[6].append(jnp.concatenate([matrices[4] for matrices in here], 1))
    params = (split_else(else_low.astype(jnp.float32)), [jnp.stack(entries) for entries in layer_sets])
    signal = signal_level(timesteps)
    noisy_input = jnp.sqrt(signal)[:, None, None] * latents + jnp.sqrt(1.0 - signal)[:, None, None] * noise
    features = time_features(timesteps)
    onehot = (labels[:, None] == jnp.arange(NCLS)[None, :]).astype(jnp.float32)
    positions = position_table(jnp.arange(S))
    group_size = math.gcd(IMAGES, 16)

    def grouped(tensor):
        return tensor.reshape((IMAGES // group_size, group_size) + tensor.shape[1:])

    def accumulate(running, batch_set):

        def loss_of(weights):
            return group_loss(weights, batch_set[0], batch_set[1], batch_set[2], batch_set[3], positions)
        loss_value, pullback = jax.vjp(loss_of, params)
        gradients = pullback(jnp.ones((), jnp.float32))[0]
        return ((running[0] + loss_value, jax.tree.map(jnp.add, running[1], gradients)), None)
    zero_tree = jax.tree.map(jnp.zeros_like, params)
    final_state, unused_out = lax.scan(accumulate, (jnp.zeros((), jnp.float32), zero_tree), (grouped(noisy_input), grouped(noise), grouped(features), grouped(onehot)))
    loss_total, gradients = final_state
    grad_else = jnp.concatenate([component.reshape(-1) for component in gradients[0]])
    grad_query, grad_key, grad_value, grad_proj, grad_up, grad_down, grad_mod = gradients[1]
    tile_list = []
    for tp_no in range(N_TP):
        head_begin, head_end = (tp_no * head_width, (tp_no + 1) * head_width)
        hidden_begin, hidden_end = (tp_no * hidden_width, (tp_no + 1) * hidden_width)
        layer_list = []
        for layer_no in range(L):
            layer_list.append([jnp.concatenate([grad_query[layer_no][:, head_begin:head_end], grad_key[layer_no][:, head_begin:head_end], grad_value[layer_no][:, head_begin:head_end]], 1), grad_proj[layer_no][head_begin:head_end], grad_up[layer_no][:, hidden_begin:hidden_end], grad_down[layer_no][hidden_begin:hidden_end], grad_mod[layer_no][:, 6 * head_begin:6 * head_end]])
        tile_list.append(pack_layers(layer_list)[ordering])
    tile_grads = jnp.stack(tile_list)
    grad_norm = jnp.sqrt(jnp.sum(tile_grads * tile_grads) + jnp.sum(grad_else * grad_else))
    clip_factor = jnp.minimum(1.0, 1.0 / grad_norm)
    left_basis = reflection(bases[:, :, 0, :])
    right_basis = reflection(bases[:, :, 1, :])
    turned = rotate(left_basis, clip_factor * tile_grads, right_basis)
    master_new, first_new, second_new = adam_finish(turned, tiles_master, tiles_first, tiles_second, left_basis, right_basis)
    else_master_new, else_first_new, else_second_new = adamw_flat(clip_factor * grad_else, else_master, else_first, else_second)
    return (loss_total, grad_norm, master_new, first_new, second_new, master_new.astype(jnp.bfloat16), else_master_new, else_first_new, else_second_new, else_master_new.astype(jnp.bfloat16))
```

```python
import math

import jax
import jax.numpy as jnp
from jax import lax
from jax.experimental import pallas as pl
from jax.experimental.pallas import tpu as pltpu
from jax.sharding import PartitionSpec as P

D = 1024
HD = 64
F = 4096
P_SIZE = 16
TFREQ = 256
NCLS = 1000
GRID = 16
L = 2
B = 128


HIGHEST = lax.Precision.HIGHEST
EPS_NORM = 1e-06
RATE = 0.02
DECAY = 0.1


def matmul(left_op, right_op):
    return jnp.dot(left_op, right_op, precision=HIGHEST)


def contract(formula, left_op, right_op):
    return jnp.einsum(formula, left_op, right_op, precision=HIGHEST)


def product(left_op, right_op):
    return jnp.dot(left_op, right_op, preferred_element_type=jnp.float32)


def over_rows(left_op, right_op):
    return lax.dot_general(
        left_op, right_op, (((0,), (0,)), ((), ())), preferred_element_type=jnp.float32
    )


def against(left_op, right_op):
    return lax.dot_general(
        left_op, right_op, (((1,), (1,)), ((), ())), preferred_element_type=jnp.float32
    )


def normed(stream):
    centred = stream - jnp.mean(stream, -1, keepdims=True)
    return centred * lax.rsqrt(jnp.mean(centred * centred, -1, keepdims=True) + EPS_NORM)


def modulate(stream, offset, factor):
    return normed(stream) * (1.0 + factor) + offset


def gelu_tanh(values):
    return jax.nn.gelu(values, approximate=True)


def time_features(time_steps):
    half_count = TFREQ // 2
    freqs = jnp.exp(-math.log(10000.0) * jnp.arange(half_count, dtype=jnp.float32) / half_count)
    angles = time_steps.astype(jnp.float32)[:, None] * freqs[None, :]
    return jnp.concatenate([jnp.cos(angles), jnp.sin(angles)], -1)


def position_table(token_ids):
    quarter = D // 4
    omegas = 1.0 / 10000.0 ** (jnp.arange(quarter, dtype=jnp.float32) / quarter)
    row_angle = (token_ids // GRID).astype(jnp.float32)[:, None] * omegas[None, :]
    col_angle = (token_ids % GRID).astype(jnp.float32)[:, None] * omegas[None, :]
    return jnp.concatenate(
        [jnp.sin(row_angle), jnp.cos(row_angle), jnp.sin(col_angle), jnp.cos(col_angle)], -1
    )


def signal_level(time_steps):
    phase = (time_steps.astype(jnp.float32) / 1000.0 + 0.008) / 1.008 * (math.pi / 2)
    return jnp.cos(phase) ** 2


def shard_shapes(tp_parts):
    head_width = D // tp_parts
    hidden_width = F // tp_parts
    return [
        (D, 3 * head_width),
        (head_width, D),
        (D, hidden_width),
        (hidden_width, D),
        (D, 6 * head_width),
    ]


def untile(tile_set, height, breadth):
    block = tile_set.shape[-1]
    return (
        tile_set.reshape(height // block, breadth // block, block, block)
        .transpose(0, 2, 1, 3)
        .reshape(height, breadth)
    )


def retile(matrix):
    height, breadth = matrix.shape
    return matrix.reshape(height // B, B, breadth // B, B).transpose(0, 2, 1, 3).reshape(-1, B, B)


def unpack_layers(tile_set, tp_parts):
    layer_list = []
    cursor = 0
    for layer_no in range(L):
        matrices = []
        for height, breadth in shard_shapes(tp_parts):
            amount = height * breadth // (B * B)
            matrices.append(untile(tile_set[cursor : cursor + amount], height, breadth))
            cursor += amount
        layer_list.append(matrices)
    return layer_list


def pack_layers(layer_list):
    return jnp.concatenate([retile(matrix) for matrices in layer_list for matrix in matrices], 0)


def else_shapes():
    return [(P_SIZE, D), (NCLS, D), (TFREQ, D), (D, D), (D, 2 * D), (D, P_SIZE)]


def split_else(flat_params):
    components = []
    cursor = 0
    for height, breadth in else_shapes():
        components.append(flat_params[cursor : cursor + height * breadth].reshape(height, breadth))
        cursor += height * breadth
    return components


def reflection(vectors):
    outer_prod = vectors[..., :, None] * vectors[..., None, :]
    return (
        jnp.eye(vectors.shape[-1], dtype=jnp.float32)
        - 2.0 * outer_prod / jnp.sum(vectors * vectors, -1)[..., None, None]
    )


def rotate(left_basis, middle, right_basis):
    return contract(
        "...ab,...bc->...ac", contract("...ab,...bc->...ac", left_basis, middle), right_basis
    )


def adam_finish(turned, master_state, first_state, second_state, left_basis, right_basis):
    first_new = 0.5 * first_state + 0.5 * turned
    second_new = 0.5 * second_state + 0.5 * turned * turned
    direction = first_new / (jnp.sqrt(second_new) + 1e-08)
    return (master_state - RATE * rotate(left_basis, direction, right_basis), first_new, second_new)


def adamw_flat(grad_clipped, master_state, first_state, second_state):
    first_new = 0.5 * first_state + 0.5 * grad_clipped
    second_new = 0.5 * second_state + 0.5 * grad_clipped * grad_clipped
    master_new = master_state - RATE * (
        first_new / (jnp.sqrt(second_new) + 1e-08) + DECAY * master_state
    )
    return (master_new, first_new, second_new)


def is_box():
    return (lax.axis_size("fsdp"), lax.axis_size("ctx"), lax.axis_size("tp")) == (8, 2, 2)


def swap_tp(value):
    return lax.ppermute(value, "tp", [(0, 1), (1, 0)])


def swap_y(value):
    return lax.ppermute(value, "ctx", [(0, 1), (1, 0)])


def swap_f(value, bit):
    return lax.ppermute(value, "fsdp", [(place, place ^ bit) for place in range(8)])


def swap_x(value):
    return swap_f(value, 1)


def move_z(value, step, sources):
    return lax.ppermute(
        value,
        "fsdp",
        [(2 * from_z + x, 2 * (from_z + step) + x) for from_z in sources for x in range(2)],
    )


def place_z():
    return lax.axis_index("fsdp") // 2


def low(value):
    return value.astype(jnp.bfloat16)


def wide(value):
    return value.astype(jnp.float32)


def along_z(own):
    z = place_z()
    above, below = [own], [own]
    for hop in range(1, 4):
        above.append(move_z(above[-1], 1, range(hop - 1, 3)))
        below.append(move_z(below[-1], -1, range(1, 5 - hop)))
    return [
        own,
        jnp.where(z % 2 == 1, above[1], below[1]),
        jnp.where(z >= 2, above[2], below[2]),
        jnp.where(
            z == 0, below[3], jnp.where(z == 3, above[3], jnp.where(z == 1, below[1], above[1]))
        ),
    ]


def sum_z(blocks):
    z = place_z()
    up = move_z(low(blocks[3]), 1, range(0, 1))
    down = move_z(low(blocks[3]), -1, range(3, 4))
    up = move_z(low(blocks[2] + up), 1, range(0, 2))
    down = move_z(low(blocks[2] + down), -1, range(2, 4))
    up = move_z(low(jnp.where(z == 1, blocks[3], blocks[1]) + up), 1, range(0, 3))
    down = move_z(low(jnp.where(z == 2, blocks[3], blocks[1]) + down), -1, range(1, 4))
    return blocks[0] + up + down


def slot_ranges(slots):
    side = slots * 5 // 18
    return slots - 2 * side, side


def gather_tiles(own):
    main, side = slot_ranges(own.shape[0])
    half = main // 2
    first, second, third = own[:main], own[main : main + side], own[main + side :]
    second = jnp.concatenate([second, swap_x(second)], 0)
    third = jnp.concatenate([third, swap_y(third)], 0)
    pieces = []
    for block in along_z(first):
        by_x, by_y = swap_x(block), swap_y(block)
        pieces += [block, by_y, by_x, swap_y(by_x[:half]), swap_x(by_y[half:])]
    for block in along_z(second):
        pieces += [block, swap_y(block)]
    for block in along_z(third):
        pieces += [block, swap_x(block)]
    return jnp.concatenate(pieces, 0)


def place_of_slot(owner, slot, slots):
    main, side = slot_ranges(slots)
    rel_f = jnp.bitwise_xor(owner // 2, lax.axis_index("fsdp"))
    rel_y = jnp.bitwise_xor(owner % 2, lax.axis_index("ctx"))
    rel_z, rel_x = rel_f // 2, rel_f % 2
    one = ((rel_z * 2 + rel_x) * 2 + rel_y) * main + slot
    two = 16 * main + ((rel_z * 2 + rel_y) * 2 + rel_x) * side + slot - main
    three = 16 * (main + side) + ((rel_z * 2 + rel_x) * 2 + rel_y) * side + slot - main - side
    return jnp.where(slot < main, one, jnp.where(slot < main + side, two, three))


def scatter_tiles(parts, slots):
    main, side = slot_ranges(slots)
    half = main // 2
    first = parts[: 16 * main].reshape(4, 2, 2, main, B, B)
    second = parts[16 * main : 16 * (main + side)].reshape(4, 2, 2, side, B, B)
    third = parts[16 * (main + side) :].reshape(4, 2, 2, side, B, B)
    blocks = [None] * 4
    two = [None] * 4
    three = [None] * 4
    for rel in (3, 2, 1, 0):
        two[rel] = wide(second[rel, 0]) + swap_y(second[rel, 1])
        three[rel] = wide(third[rel, 0]) + swap_x(third[rel, 1])
    for rel in (3, 2, 1, 0):
        by_y = swap_y(first[rel, 1, 1, :half])
        by_x = swap_x(first[rel, 1, 1, half:])
        from_x = jnp.concatenate(
            [
                swap_x(low(wide(first[rel, 1, 0, :half]) + by_y)),
                swap_x(first[rel, 1, 0, half:]),
            ],
            0,
        )
        from_y = jnp.concatenate(
            [
                swap_y(first[rel, 0, 1, :half]),
                swap_y(low(wide(first[rel, 0, 1, half:]) + by_x)),
            ],
            0,
        )
        blocks[rel] = wide(first[rel, 0, 0]) + from_x + from_y
    two = sum_z(two)
    three = sum_z(three)
    two = two[0] + swap_x(low(two[1]))
    three = three[0] + swap_y(low(three[1]))
    return jnp.concatenate([sum_z(blocks), two, three], 0)


def gather_images(value):
    if not is_box():
        return lax.all_gather(value, ("fsdp", "ctx"), axis=0, tiled=True)
    value = jnp.concatenate(along_z(value), 0)
    by_x, by_y = swap_x(value), swap_y(value)
    return jnp.concatenate([value, by_x, by_y, swap_x(by_y)], 0)


def gather_else(flat):
    if not is_box():
        return lax.all_gather(flat, ("fsdp", "ctx", "tp"), axis=0, tiled=True)
    z, x = place_z(), lax.axis_index("fsdp") % 2
    y, core = lax.axis_index("ctx"), lax.axis_index("tp")
    own = flat.reshape(1, -1, 128)
    line = along_z(own)
    line = [
        jnp.where(
            z == place,
            line[0],
            jnp.where(z == place ^ 1, line[1], jnp.where(z == place ^ 2, line[2], line[3])),
        )
        for place in range(4)
    ]
    line = jnp.concatenate(line, 0)
    by_x, by_y = swap_x(line), swap_y(line)
    half = line.shape[1] // 2
    both = jnp.concatenate([swap_y(by_x[:, :half]), swap_x(by_y[:, half:])], 1)
    y_low = [jnp.where(y == 0, line, by_y), jnp.where(y == 0, by_x, both)]
    y_high = [jnp.where(y == 0, by_y, line), jnp.where(y == 0, both, by_x)]
    chip = jnp.stack(
        [
            jnp.stack([jnp.where(x == 0, y_low[0], y_low[1]), jnp.where(x == 0, y_high[0], y_high[1])], 1),
            jnp.stack([jnp.where(x == 0, y_low[1], y_low[0]), jnp.where(x == 0, y_high[1], y_high[0])], 1),
        ],
        1,
    )
    other = swap_tp(chip)
    return jnp.stack(
        [jnp.where(core == 0, chip, other), jnp.where(core == 0, other, chip)], 3
    ).reshape(-1)


def total(value):
    if not is_box():
        return lax.psum(value, ("fsdp", "ctx", "tp"))
    value = value + swap_tp(value)
    value = value + swap_y(value)
    for bit in (1, 2, 4):
        value = value + swap_f(value, bit)
    return value


def tp_sum(value):
    if lax.axis_size("tp") == 2:
        return value + swap_tp(value)
    return lax.psum(value, "tp")


def columns_in(value):
    if lax.axis_size("tp") == 2:
        other = swap_tp(value)
        at_zero = lax.axis_index("tp") == 0
        return jnp.concatenate(
            [jnp.where(at_zero, value, other), jnp.where(at_zero, other, value)], -1
        )
    return lax.all_gather(value, "tp", axis=value.ndim - 1, tiled=True)


def rows_in(value_low):
    if lax.axis_size("tp") == 2:
        return jnp.concatenate([value_low, swap_tp(value_low)], 0)
    return lax.all_gather(value_low, "tp", axis=0, tiled=True)


def rows_out(left_op, weight, contract_dim):
    partial = lax.dot_general(
        left_op, weight, (((1,), (contract_dim,)), ((), ())), preferred_element_type=jnp.float32
    )
    if lax.axis_size("tp") == 2:
        half = partial.shape[0] // 2
        return partial[:half] + swap_tp(partial[half:])
    return lax.psum_scatter(partial, "tp", scatter_dimension=0, tiled=True)


def attend(queries, key_rows, value_rows):
    scores = jnp.einsum(
        "iqhe,ikhe->ihqk", queries, key_rows, preferred_element_type=jnp.float32
    ) * HD ** (-0.5)
    highest_score = jnp.max(scores, -1, keepdims=True)
    exponent = jnp.exp(scores - highest_score)
    row_total = jnp.sum(exponent, -1, keepdims=True)
    probabilities = (exponent / row_total).astype(jnp.bfloat16)
    attended = jnp.einsum(
        "ihqk,ikhe->iqhe", probabilities, value_rows, preferred_element_type=jnp.float32
    )
    return (attended, highest_score + jnp.log(row_total))


def attend_back(queries, key_rows, value_rows, log_total, grad_attended):
    scores = jnp.einsum(
        "iqhe,ikhe->ihqk", queries, key_rows, preferred_element_type=jnp.float32
    ) * HD ** (-0.5)
    probabilities = jnp.exp(scores - log_total)
    grad_prob = jnp.einsum(
        "iqhe,ikhe->ihqk", grad_attended, value_rows, preferred_element_type=jnp.float32
    )
    grad_scores = (
        probabilities * (grad_prob - jnp.sum(probabilities * grad_prob, -1, keepdims=True))
    ).astype(jnp.bfloat16)
    grad_queries = jnp.einsum(
        "ihqk,ikhe->iqhe", grad_scores, key_rows, preferred_element_type=jnp.float32
    ) * HD ** (-0.5)
    grad_keys = jnp.einsum(
        "ihqk,iqhe->ikhe", grad_scores, queries, preferred_element_type=jnp.float32
    ) * HD ** (-0.5)
    grad_values = jnp.einsum(
        "ihqk,iqhe->ikhe",
        probabilities.astype(jnp.bfloat16),
        grad_attended,
        preferred_element_type=jnp.float32,
    )
    return (grad_queries, grad_keys, grad_values)


def layer_forward(stream, modes, matrices, images, local_len):
    w_qkv, w_proj, w_up, w_down = matrices[:4]
    own, group = stream.shape[:2]
    rows = own * group
    shift_attn, scale_attn, gate_attn, shift_mlp, scale_mlp, gate_mlp = jnp.split(
        modes[:, None, :], 6, -1
    )
    normed_in = rows_in(low(modulate(stream, shift_attn, scale_attn)).reshape(rows, D))
    projected = low(product(normed_in, w_qkv))
    head_width = w_proj.shape[0]
    head_count = head_width // HD
    queries = projected[:, :head_width].reshape(images, local_len, head_count, HD)
    key_rows = projected[:, head_width : 2 * head_width].reshape(images, local_len, head_count, HD)
    value_rows = projected[:, 2 * head_width :].reshape(images, local_len, head_count, HD)
    attended, log_total = attend(queries, key_rows, value_rows)
    attended = low(attended.reshape(images * local_len, head_width))
    branch = rows_out(attended, w_proj, 0).reshape(own, group, D)
    middle = stream + gate_attn * branch
    normed_mid = rows_in(low(modulate(middle, shift_mlp, scale_mlp)).reshape(rows, D))
    hidden = product(normed_mid, w_up)
    activation = low(gelu_tanh(hidden))
    mlp_out = rows_out(activation, w_down, 0).reshape(own, group, D)
    kept_state = (
        stream,
        normed_in,
        queries,
        key_rows,
        value_rows,
        log_total,
        attended,
        branch,
        middle,
        normed_mid,
        hidden,
        mlp_out,
    )
    return (middle + gate_mlp * mlp_out, kept_state)


def layer_backward(upstream, kept_state, modes, matrices, images, local_len):
    w_qkv, w_proj, w_up, w_down = matrices[:4]
    (
        stream,
        normed_in,
        queries,
        key_rows,
        value_rows,
        log_total,
        attended,
        branch,
        middle,
        normed_mid,
        hidden,
        mlp_out,
    ) = kept_state
    own, group = stream.shape[:2]
    rows = own * group
    shift_attn, scale_attn, gate_attn, shift_mlp, scale_mlp, gate_mlp = jnp.split(
        modes[:, None, :], 6, -1
    )
    grad_mlp = rows_in(low(gate_mlp * upstream).reshape(rows, D))
    activation, gelu_back = jax.vjp(gelu_tanh, hidden)
    grad_down = low(over_rows(low(activation), grad_mlp))
    grad_hidden = low(gelu_back(against(grad_mlp, w_down))[0])
    grad_up = low(over_rows(normed_mid, grad_hidden))
    grad_normed_mid = rows_out(grad_hidden, w_up, 1).reshape(own, group, D)
    grad_middle, grad_shift_mlp, grad_scale_mlp = jax.vjp(modulate, middle, shift_mlp, scale_mlp)[
        1
    ](grad_normed_mid)
    grad_middle = grad_middle + upstream
    grad_branch = rows_in(low(gate_attn * grad_middle).reshape(rows, D))
    grad_proj = low(over_rows(attended, grad_branch))
    head_width = w_proj.shape[0]
    head_count = head_width // HD
    grad_attended = low(against(grad_branch, w_proj)).reshape(images, local_len, head_count, HD)
    grad_queries, grad_keys, grad_values = attend_back(
        queries, key_rows, value_rows, log_total, grad_attended
    )
    rows_here = images * local_len
    grad_qkv = low(
        jnp.concatenate(
            [
                grad_queries.reshape(rows_here, head_width),
                grad_keys.reshape(rows_here, head_width),
                grad_values.reshape(rows_here, head_width),
            ],
            1,
        )
    )
    grad_w_qkv = low(over_rows(normed_in, grad_qkv))
    grad_normed_in = rows_out(grad_qkv, w_qkv, 1).reshape(own, group, D)
    grad_stream, grad_shift_attn, grad_scale_attn = jax.vjp(
        modulate, stream, shift_attn, scale_attn
    )[1](grad_normed_in)
    grad_modes = jnp.concatenate(
        [
            grad_shift_attn,
            grad_scale_attn,
            jnp.sum(grad_middle * branch, 1, keepdims=True),
            grad_shift_mlp,
            grad_scale_mlp,
            jnp.sum(upstream * mlp_out, 1, keepdims=True),
        ],
        -1,
    )[:, 0]
    return (grad_stream + grad_middle, [grad_w_qkv, grad_proj, grad_up, grad_down], grad_modes)


def update_kernel(clip, grad, master, first, second, bases, master_out, first_out, second_out, low_out):
    eye = lax.broadcasted_iota(jnp.int32, (B, B), 0) == lax.broadcasted_iota(jnp.int32, (B, B), 1)
    for tile in range(grad.shape[0]):
        left_row = bases[tile, 0:1, :]
        right_row = bases[tile, 1:2, :]
        left_col = jnp.sum(jnp.where(eye, left_row, 0.0), 1, keepdims=True)
        left_rate = 2.0 / jnp.sum(left_row * left_row, 1, keepdims=True)
        right_rate = 2.0 / jnp.sum(right_row * right_row, 1, keepdims=True)
        left_scaled = left_col * left_rate
        right_scaled = right_row * right_rate

        def turn(middle):
            middle = middle - left_scaled * jnp.sum(left_col * middle, 0, keepdims=True)
            return middle - jnp.sum(middle * right_row, 1, keepdims=True) * right_scaled

        turned = turn(clip[0, 0] * grad[tile])
        first_new = 0.5 * first[tile] + 0.5 * turned
        second_new = 0.5 * second[tile] + 0.5 * turned * turned
        direction = first_new / (jnp.sqrt(second_new) + 1e-08)
        master_new = master[tile] - RATE * turn(direction)
        master_out[tile] = master_new
        first_out[tile] = first_new
        second_out[tile] = second_new
        low_out[tile] = master_new.astype(jnp.bfloat16)


def update_tiles(clip_factor, grad, master, first, second, bases):
    slots = grad.shape[0]
    amount = 3
    tile_spec = pl.BlockSpec((amount, B, B), lambda step: (step, 0, 0))
    whole = jax.ShapeDtypeStruct(grad.shape, jnp.float32)
    return pl.pallas_call(
        update_kernel,
        grid=(slots // amount,),
        in_specs=[pl.BlockSpec(memory_space=pltpu.SMEM)]
        + [tile_spec] * 4
        + [pl.BlockSpec((amount, 2, B), lambda step: (step, 0, 0))],
        out_specs=[tile_spec] * 4,
        out_shape=[whole, whole, whole, jax.ShapeDtypeStruct(grad.shape, jnp.bfloat16)],
        compiler_params=pltpu.CompilerParams(vmem_limit_bytes=32 * 1024 * 1024),
        cost_estimate=pl.CostEstimate(
            flops=slots * B * B * 30, bytes_accessed=slots * B * B * 30, transcendentals=slots * B * B
        ),
    )(clip_factor.reshape(1, 1), grad, master, first, second, bases)


def on_device(
    latents,
    noise,
    timesteps,
    labels,
    owners,
    tiles_low,
    tiles_master,
    tiles_first,
    tiles_second,
    bases,
    else_low,
    else_master,
    else_first,
    else_second,
):
    box = is_box()
    tp_parts = lax.axis_size("tp")
    tp_index = lax.axis_index("tp")
    ctx_parts = lax.axis_size("ctx")
    fsdp_parts = lax.axis_size("fsdp")
    images = latents.shape[0]
    local_len = latents.shape[1]
    slots = tiles_low.shape[1]
    sp_rows = images * local_len // tp_parts
    first_row = tp_index * sp_rows
    own = max(1, sp_rows // local_len)
    group = sp_rows // own
    first_image = first_row // local_len
    element_count = images * fsdp_parts * ctx_parts * local_len * P_SIZE
    ordering = jnp.argsort(owners, stable=True)
    inverse = jnp.argsort(ordering)
    patch_weight, class_table, time_first, time_second, final_weight, head_weight = split_else(
        gather_else(else_low)
    )
    if box:
        places = place_of_slot(inverse // slots, inverse % slots, slots)
        tile_at = jnp.argsort(places)
        gathered = gather_tiles(tiles_low[0])[places]
    else:
        gathered = lax.all_gather(tiles_low, ("fsdp", "ctx"), axis=1, tiled=True)[0][inverse]
    layer_list = unpack_layers(gathered, tp_parts)
    features_low = low(time_features(timesteps))
    onehot = low(labels[:, None] == jnp.arange(NCLS)[None, :])
    time_hidden = product(features_low, time_first)
    time_act = low(jax.nn.silu(time_hidden))
    condition = product(time_act, time_second) + product(onehot, class_table)
    cond_act = low(jax.nn.silu(condition))
    mod_full = columns_in(
        jnp.stack([product(cond_act, matrices[4]) for matrices in layer_list])
    )
    mode_rows = lax.dynamic_slice_in_dim(mod_full, first_image, own, 1)
    final_rows = lax.dynamic_slice_in_dim(product(cond_act, final_weight), first_image, own, 0)
    row_index = first_row + jnp.arange(sp_rows)
    signal = signal_level(timesteps)
    noisy_input = (
        jnp.sqrt(signal)[:, None, None] * latents + jnp.sqrt(1.0 - signal)[:, None, None] * noise
    )
    noisy_rows = low(
        lax.dynamic_slice_in_dim(
            noisy_input.reshape(images * local_len, P_SIZE), first_row, sp_rows, 0
        )
    )
    target = lax.dynamic_slice_in_dim(
        noise.reshape(images * local_len, P_SIZE), first_row, sp_rows, 0
    )
    stream = (product(noisy_rows, patch_weight) + position_table(row_index % local_len)).reshape(
        own, group, D
    )
    kept_list = []
    for layer_no in range(L):
        stream, kept_state = layer_forward(
            stream, mode_rows[layer_no], layer_list[layer_no], images, local_len
        )
        kept_list.append(kept_state)
    shift_out, scale_out = jnp.split(final_rows[:, None, :], 2, -1)
    head_in, head_back = jax.vjp(modulate, stream, shift_out, scale_out)
    head_low = low(head_in).reshape(sp_rows, D)
    mismatch = product(head_low, head_weight) - target
    loss_part = jnp.sum(mismatch * mismatch) / element_count
    grad_pred = low(2.0 * mismatch / element_count)
    grad_head = over_rows(head_low, grad_pred)
    upstream, grad_shift_out, grad_scale_out = head_back(
        against(grad_pred, head_weight).reshape(own, group, D)
    )
    grad_final = jnp.concatenate([grad_shift_out, grad_scale_out], -1)[:, 0]
    grad_layers = [None] * L
    grad_modes = [None] * L
    for layer_no in reversed(range(L)):
        upstream, grad_layers[layer_no], grad_modes[layer_no] = layer_backward(
            upstream,
            kept_list[layer_no],
            mode_rows[layer_no],
            layer_list[layer_no],
            images,
            local_len,
        )
    grad_patch = over_rows(noisy_rows, low(upstream).reshape(sp_rows, D))
    own_modes = jnp.concatenate(grad_modes + [grad_final], -1)
    image_grads = tp_sum(
        lax.dynamic_update_slice_in_dim(
            jnp.zeros((images, own_modes.shape[1]), jnp.float32), own_modes, first_image, 0
        )
    )
    grad_final = image_grads[:, 12 * D :]
    mode_width = 6 * D // tp_parts
    mode_image = [
        lax.dynamic_slice_in_dim(
            image_grads, layer_no * 6 * D + tp_index * mode_width, mode_width, 1
        )
        for layer_no in range(L)
    ]
    cond_wide = wide(cond_act)
    grad_cond_act = 0.0
    for layer_no in range(L):
        grad_layers[layer_no].append(low(contract("id,ie->de", cond_wide, mode_image[layer_no])))
        grad_cond_act = grad_cond_act + matmul(
            mode_image[layer_no], wide(layer_list[layer_no][4]).T
        )
    grad_cond_act = tp_sum(grad_cond_act) + matmul(grad_final, wide(final_weight).T)
    grad_condition = jax.vjp(jax.nn.silu, condition)[1](grad_cond_act)[0]
    grad_time_hidden = jax.vjp(jax.nn.silu, time_hidden)[1](
        matmul(grad_condition, wide(time_second).T)
    )[0]
    if box:
        tile_grads = pack_layers(grad_layers)[tile_at]
        owned = scatter_tiles(tile_grads, slots)
    else:
        tile_grads = wide(pack_layers(grad_layers))[ordering]
        owned = lax.psum_scatter(tile_grads, ("fsdp", "ctx"), scatter_dimension=0, tiled=True)
    label_column = jnp.broadcast_to(wide(labels)[:, None], (images, 128))
    every = gather_images(
        jnp.concatenate(
            [
                label_column,
                wide(features_low),
                grad_time_hidden,
                grad_condition,
                wide(time_act),
                cond_wide,
                grad_final,
            ],
            1,
        )
    )
    cuts = [128, 128 + TFREQ]
    for length in (D, D, D, D):
        cuts.append(cuts[-1] + length)
    all_labels, all_features, all_hidden, all_condition, all_time, all_cond, all_final = jnp.split(
        every, cuts, 1
    )
    all_onehot = wide(all_labels[:, :1] == jnp.arange(NCLS, dtype=jnp.float32)[None, :])
    token_grads = total(jnp.concatenate([grad_patch, grad_head.reshape(P_SIZE, D)], 0))
    row_grads = jnp.concatenate(
        [
            token_grads[:P_SIZE],
            contract("ic,id->cd", all_onehot, all_condition),
            contract("ic,id->cd", all_features, all_hidden),
            contract("ic,id->cd", all_time, all_condition),
            contract("ic,id->cd", all_cond, all_final).reshape(2 * D, D),
            token_grads[P_SIZE:],
        ],
        0,
    )
    share = else_low.shape[0]
    device = (lax.axis_index("fsdp") * ctx_parts + lax.axis_index("ctx")) * tp_parts + tp_index
    begin = device * share
    row_count = min(share // D + 2, row_grads.shape[0])
    begin_row = jnp.minimum(begin // D, row_grads.shape[0] - row_count)
    near = lax.dynamic_slice_in_dim(row_grads, begin_row, row_count, 0).reshape(-1)
    else_grad = lax.dynamic_slice_in_dim(near, begin - begin_row * D, share, 0)
    squares = jnp.sum(owned * owned) + jnp.sum(else_grad * else_grad)
    totals = total(jnp.stack([loss_part, squares]))
    loss_total = totals[0]
    grad_norm = jnp.sqrt(totals[1])
    clip_factor = jnp.minimum(1.0, 1.0 / grad_norm)
    master_new, first_new, second_new, low_new = update_tiles(
        clip_factor, owned, tiles_master[0], tiles_first[0], tiles_second[0], bases[0]
    )
    else_master_new, else_first_new, else_second_new = adamw_flat(
        clip_factor * else_grad, else_master, else_first, else_second
    )
    return (
        loss_total,
        grad_norm,
        master_new[None],
        first_new[None],
        second_new[None],
        low_new[None],
        else_master_new,
        else_first_new,
        else_second_new,
        low(else_master_new),
    )


def solution(mesh):
    return jax.shard_map(
        on_device,
        mesh=mesh,
        in_specs=(
            P(("fsdp", "ctx"), None, None),
            P(("fsdp", "ctx"), None, None),
            P(("fsdp", "ctx")),
            P(("fsdp", "ctx")),
            P(),
            P("tp", ("fsdp", "ctx"), None, None),
            P("tp", ("fsdp", "ctx"), None, None),
            P("tp", ("fsdp", "ctx"), None, None),
            P("tp", ("fsdp", "ctx"), None, None),
            P("tp", ("fsdp", "ctx"), None, None),
            P(("fsdp", "ctx", "tp")),
            P(("fsdp", "ctx", "tp")),
            P(("fsdp", "ctx", "tp")),
            P(("fsdp", "ctx", "tp")),
        ),
        out_specs=(
            P(),
            P(),
            P("tp", ("fsdp", "ctx"), None, None),
            P("tp", ("fsdp", "ctx"), None, None),
            P("tp", ("fsdp", "ctx"), None, None),
            P("tp", ("fsdp", "ctx"), None, None),
            P(("fsdp", "ctx", "tp")),
            P(("fsdp", "ctx", "tp")),
            P(("fsdp", "ctx", "tp")),
            P(("fsdp", "ctx", "tp")),
        ),
        check_vma=False,
    )
```

```python
import math

import jax
import jax.numpy as jnp
from jax import lax
from jax.experimental import pallas as pl
from jax.experimental.pallas import tpu as pltpu
from jax.sharding import PartitionSpec as P

D = 1024
HD = 64
F = 4096
P_SIZE = 16
TFREQ = 256
NCLS = 1000
GRID = 16
L = 2
B = 128


HIGHEST = lax.Precision.HIGHEST
EPS_NORM = 1e-06
RATE = 0.02
DECAY = 0.1


def matmul(left_op, right_op):
    return jnp.dot(left_op, right_op, precision=HIGHEST)


def contract(formula, left_op, right_op):
    return jnp.einsum(formula, left_op, right_op, precision=HIGHEST)


def product(left_op, right_op):
    return jnp.dot(left_op, right_op, preferred_element_type=jnp.float32)


def over_rows(left_op, right_op):
    return lax.dot_general(
        left_op, right_op, (((0,), (0,)), ((), ())), preferred_element_type=jnp.float32
    )


def against(left_op, right_op):
    return lax.dot_general(
        left_op, right_op, (((1,), (1,)), ((), ())), preferred_element_type=jnp.float32
    )


def normed(stream):
    centred = stream - jnp.mean(stream, -1, keepdims=True)
    return centred * lax.rsqrt(jnp.mean(centred * centred, -1, keepdims=True) + EPS_NORM)


def modulate(stream, offset, factor):
    return normed(stream) * (1.0 + factor) + offset


def gelu_tanh(values):
    return jax.nn.gelu(values, approximate=True)


def time_features(time_steps):
    half_count = TFREQ // 2
    freqs = jnp.exp(-math.log(10000.0) * jnp.arange(half_count, dtype=jnp.float32) / half_count)
    angles = time_steps.astype(jnp.float32)[:, None] * freqs[None, :]
    return jnp.concatenate([jnp.cos(angles), jnp.sin(angles)], -1)


def position_table(token_ids):
    quarter = D // 4
    omegas = 1.0 / 10000.0 ** (jnp.arange(quarter, dtype=jnp.float32) / quarter)
    row_angle = (token_ids // GRID).astype(jnp.float32)[:, None] * omegas[None, :]
    col_angle = (token_ids % GRID).astype(jnp.float32)[:, None] * omegas[None, :]
    return jnp.concatenate(
        [jnp.sin(row_angle), jnp.cos(row_angle), jnp.sin(col_angle), jnp.cos(col_angle)], -1
    )


def signal_level(time_steps):
    phase = (time_steps.astype(jnp.float32) / 1000.0 + 0.008) / 1.008 * (math.pi / 2)
    return jnp.cos(phase) ** 2


def shard_shapes(tp_parts):
    head_width = D // tp_parts
    hidden_width = F // tp_parts
    return [
        (D, 3 * head_width),
        (head_width, D),
        (D, hidden_width),
        (hidden_width, D),
        (D, 6 * head_width),
    ]


def untile(tile_set, height, breadth):
    block = tile_set.shape[-1]
    return (
        tile_set.reshape(height // block, breadth // block, block, block)
        .transpose(0, 2, 1, 3)
        .reshape(height, breadth)
    )


def retile(matrix):
    height, breadth = matrix.shape
    return matrix.reshape(height // B, B, breadth // B, B).transpose(0, 2, 1, 3).reshape(-1, B, B)


def unpack_layers(tile_set, tp_parts):
    layer_list = []
    cursor = 0
    for layer_no in range(L):
        matrices = []
        for height, breadth in shard_shapes(tp_parts):
            amount = height * breadth // (B * B)
            matrices.append(untile(tile_set[cursor : cursor + amount], height, breadth))
            cursor += amount
        layer_list.append(matrices)
    return layer_list


def pack_layers(layer_list):
    return jnp.concatenate([retile(matrix) for matrices in layer_list for matrix in matrices], 0)


def else_shapes():
    return [(P_SIZE, D), (NCLS, D), (TFREQ, D), (D, D), (D, 2 * D), (D, P_SIZE)]


def split_else(flat_params):
    components = []
    cursor = 0
    for height, breadth in else_shapes():
        components.append(flat_params[cursor : cursor + height * breadth].reshape(height, breadth))
        cursor += height * breadth
    return components


def reflection(vectors):
    outer_prod = vectors[..., :, None] * vectors[..., None, :]
    return (
        jnp.eye(vectors.shape[-1], dtype=jnp.float32)
        - 2.0 * outer_prod / jnp.sum(vectors * vectors, -1)[..., None, None]
    )


def rotate(left_basis, middle, right_basis):
    return contract(
        "...ab,...bc->...ac", contract("...ab,...bc->...ac", left_basis, middle), right_basis
    )


def adam_finish(turned, master_state, first_state, second_state, left_basis, right_basis):
    first_new = 0.5 * first_state + 0.5 * turned
    second_new = 0.5 * second_state + 0.5 * turned * turned
    direction = first_new / (jnp.sqrt(second_new) + 1e-08)
    return (master_state - RATE * rotate(left_basis, direction, right_basis), first_new, second_new)


def adamw_flat(grad_clipped, master_state, first_state, second_state):
    first_new = 0.5 * first_state + 0.5 * grad_clipped
    second_new = 0.5 * second_state + 0.5 * grad_clipped * grad_clipped
    master_new = master_state - RATE * (
        first_new / (jnp.sqrt(second_new) + 1e-08) + DECAY * master_state
    )
    return (master_new, first_new, second_new)


def is_box():
    return (lax.axis_size("fsdp"), lax.axis_size("ctx"), lax.axis_size("tp")) == (8, 2, 2)


def swap_tp(value):
    return lax.ppermute(value, "tp", [(0, 1), (1, 0)])


def swap_y(value):
    return lax.ppermute(value, "ctx", [(0, 1), (1, 0)])


def swap_f(value, bit):
    return lax.ppermute(value, "fsdp", [(place, place ^ bit) for place in range(8)])


def swap_x(value):
    return swap_f(value, 1)


def place_z():
    return lax.axis_index("fsdp") // 2


def low(value):
    return value.astype(jnp.bfloat16)


def wide(value):
    return value.astype(jnp.float32)


def after(value, *earlier):
    return lax.optimization_barrier((value, *earlier))[0]


class Lanes:
    def __init__(self):
        self.done = ()

    def step(self, sends, *earlier):
        values = lax.optimization_barrier(tuple(value for _, value in sends) + self.done + earlier)
        self.done = tuple(swap(value) for (swap, _), value in zip(sends, values))
        return list(self.done)


def move_z(step, sources):
    pairs = [(2 * z + x, 2 * (z + step) + x) for z in sources for x in range(2)]
    return lambda value: lax.ppermute(value, "fsdp", pairs)


def to_z(rel):
    return lambda value: swap_f(value, 2 * rel)


class ZLine:
    def __init__(self, own):
        self.above, self.below = [own], [own]

    def sends(self):
        hop = len(self.above)
        return [
            (move_z(1, range(hop - 1, 3)), self.above[-1]),
            (move_z(-1, range(1, 5 - hop)), self.below[-1]),
        ]

    def take(self, arrived):
        self.above.append(arrived[0])
        self.below.append(arrived[1])

    def block(self, rel):
        z = place_z()
        above, below = self.above, self.below
        if rel == 0:
            return above[0]
        if rel == 1:
            return jnp.where(z % 2 == 1, above[1], below[1])
        if rel == 2:
            return jnp.where(z >= 2, above[2], below[2])
        return jnp.where(
            z == 0, below[3], jnp.where(z == 3, above[3], jnp.where(z == 1, below[1], above[1]))
        )


class ZSum:
    def __init__(self):
        self.last = None
        self.up = self.down = None

    def sends(self, rel, block):
        z = place_z()
        if rel == 3:
            self.last = block
            up, down = block, block
        elif rel == 2:
            up, down = block + self.up, block + self.down
        else:
            up = jnp.where(z == 1, self.last, block) + self.up
            down = jnp.where(z == 2, self.last, block) + self.down
        return [
            (move_z(1, range(0, 4 - rel)), low(up)),
            (move_z(-1, range(rel, 4)), low(down)),
        ]

    def take(self, arrived):
        self.up, self.down = arrived

    def total(self, block):
        return block + self.up + self.down


def early_slots(slots):
    return slots - slots * 13 // 36


def gather_tiles(own, early, place_early, place_late, else_low, targets):
    half = early // 2
    lanes = Lanes()
    line, late_line = ZLine(own[:early]), ZLine(own[early:])
    rest = None
    token = ()
    for rel in range(4):
        block = line.block(rel)
        sends = [(swap_x, block), (swap_y, block)]
        waits = token
        if rel == 2:
            waits += (flat,)
        elif rel == 3:
            waits += rest
        if rel < 3:
            by_x, by_y, *arrived = lanes.step(sends + line.sends(), *waits)
            line.take(arrived)
        else:
            by_x, by_y, *arrived = lanes.step(sends + late_line.sends(), *waits)
            late_line.take(arrived)
        sends = [(swap_y, by_x[:half]), (swap_x, by_y[half:])]
        if rel == 0:
            first, second, *arrived = lanes.step(
                sends + [(to_z(other), else_low.reshape(1, -1, 128)) for other in (1, 2, 3)],
                targets,
            )
            flat = gather_else(else_low, lanes, arrived)
            rest = cut_else(flat)
        elif rel == 1:
            first, second = lanes.step(sends)
        else:
            first, second, *arrived = lanes.step(sends + late_line.sends())
            late_line.take(arrived)
        at = 4 * rel * early
        group = [
            (block, at),
            (by_y, at + early),
            (by_x, at + 2 * early),
            (first, at + 3 * early),
            (second, at + 3 * early + half),
        ]
        token = (place_early(group),)
    line = jnp.concatenate([late_line.block(rel) for rel in range(4)], 0)
    count = line.shape[0]
    half = count // 2
    by_x, by_y = lanes.step([(swap_x, line), (swap_y, line)])
    token = place_late([(line, 0)])
    first, second = lanes.step([(swap_y, by_x[:half]), (swap_x, by_y[half:])], token)
    place_late([(by_y, count), (by_x, 2 * count)])
    place_late([(first, 3 * count), (second, 3 * count + half)])
    return rest


def relative(owner):
    rel_f = jnp.bitwise_xor(owner // 2, lax.axis_index("fsdp"))
    return rel_f // 2, rel_f % 2, jnp.bitwise_xor(owner % 2, lax.axis_index("ctx"))


def early_place(owner, slot, slots):
    rel_z, rel_x, rel_y = relative(owner)
    return ((rel_z * 2 + rel_x) * 2 + rel_y) * slots + slot


def late_place(owner, slot, slots):
    rel_z, rel_x, rel_y = relative(owner)
    return ((rel_x * 2 + rel_y) * 4 + rel_z) * slots + slot


def scatter_late(parts, slots, lanes):
    count = 4 * slots
    half = count // 2
    keep, to_y, to_x, both = (parts[part * count : (part + 1) * count] for part in range(4))
    by_y, by_x = lanes.step([(swap_y, both[:half]), (swap_x, both[half:])])
    to_x = jnp.concatenate([low(wide(to_x[:half]) + by_y), to_x[half:]], 0)
    to_y = jnp.concatenate([to_y[:half], low(wide(to_y[half:]) + by_x)], 0)
    from_x, from_y = lanes.step([(swap_x, to_x), (swap_y, to_y)])
    keep = wide(keep) + from_x + from_y
    return [keep[rel * slots : (rel + 1) * slots] for rel in range(4)]


def scatter_early(parts, slots, lanes, late, images_part):
    half = slots // 2

    def block(part, begin, end):
        return parts[part * slots + begin : part * slots + end]

    def diagonal(rel):
        return [
            (swap_y, block(4 * rel + 3, 0, half)),
            (swap_x, block(4 * rel + 3, half, slots)),
        ]

    def sides(rel, arrived):
        by_y, by_x = arrived
        return [
            (
                swap_x,
                jnp.concatenate(
                    [
                        low(wide(block(4 * rel + 2, 0, half)) + by_y),
                        block(4 * rel + 2, half, slots),
                    ],
                    0,
                ),
            ),
            (
                swap_y,
                jnp.concatenate(
                    [
                        block(4 * rel + 1, 0, half),
                        low(wide(block(4 * rel + 1, half, slots)) + by_x),
                    ],
                    0,
                ),
            ),
        ]

    def kept(rel, arrived):
        return wide(block(4 * rel, 0, slots)) + arrived[0] + arrived[1]

    line, late_line = ZSum(), ZSum()
    arrived = lanes.step(diagonal(3) + late_line.sends(3, late[3]))
    diagonal_3 = arrived[:2]
    late_line.take(arrived[2:])
    arrived = lanes.step(diagonal(2) + late_line.sends(2, late[2]))
    diagonal_2 = arrived[:2]
    late_line.take(arrived[2:])
    arrived = lanes.step(sides(3, diagonal_3) + late_line.sends(1, late[1]))
    late_line.take(arrived[2:])
    owned_late = late_line.total(late[0])
    kept_3 = kept(3, arrived)
    arrived = lanes.step(diagonal(1) + [(to_z(rel), images_part) for rel in (1, 2, 3)])
    diagonal_1 = arrived[:2]
    images = jnp.concatenate([images_part] + arrived[2:], 0)
    arrived = lanes.step(sides(2, diagonal_2) + line.sends(3, kept_3) + [(swap_y, images)])
    line.take(arrived[2:4])
    kept_2 = kept(2, arrived)
    images = jnp.concatenate([images, arrived[4]], 0)
    arrived = lanes.step(diagonal(0) + [(swap_x, images)])
    diagonal_0 = arrived[:2]
    images = jnp.concatenate([images, arrived[2]], 0)
    arrived = lanes.step(sides(1, diagonal_1) + line.sends(2, kept_2))
    line.take(arrived[2:4])
    arrived_0 = lanes.step(sides(0, diagonal_0) + line.sends(1, kept(1, arrived)))
    line.take(arrived_0[2:4])
    return line.total(kept(0, arrived_0)), owned_late, images


def gather_images(value):
    if not is_box():
        return lax.all_gather(value, ("fsdp", "ctx"), axis=0, tiled=True)
    value = jnp.concatenate([value] + [swap_f(value, 2 * rel) for rel in (1, 2, 3)], 0)
    by_x, by_y = swap_x(value), swap_y(value)
    return jnp.concatenate([value, by_y, by_x, swap_x(by_y)], 0)


def gather_else(flat, lanes, line):
    if not is_box():
        return lax.all_gather(flat, ("fsdp", "ctx", "tp"), axis=0, tiled=True)
    z, x = place_z(), lax.axis_index("fsdp") % 2
    y, core = lax.axis_index("ctx"), lax.axis_index("tp")
    own = flat.reshape(1, -1, 128)
    line = [own] + line
    line = [
        jnp.where(
            z == place,
            line[0],
            jnp.where(z == place ^ 1, line[1], jnp.where(z == place ^ 2, line[2], line[3])),
        )
        for place in range(4)
    ]
    line = jnp.concatenate(line, 0)
    by_x, by_y = lanes.step([(swap_x, line), (swap_y, line)])
    half = line.shape[1] // 2
    both = jnp.concatenate(lanes.step([(swap_y, by_x[:, :half]), (swap_x, by_y[:, half:])]), 1)
    y_low = [jnp.where(y == 0, line, by_y), jnp.where(y == 0, by_x, both)]
    y_high = [jnp.where(y == 0, by_y, line), jnp.where(y == 0, both, by_x)]
    chip = jnp.stack(
        [
            jnp.stack([jnp.where(x == 0, y_low[0], y_low[1]), jnp.where(x == 0, y_high[0], y_high[1])], 1),
            jnp.stack([jnp.where(x == 0, y_low[1], y_low[0]), jnp.where(x == 0, y_high[1], y_high[0])], 1),
        ],
        1,
    )
    other = swap_tp(chip)
    return jnp.stack(
        [jnp.where(core == 0, chip, other), jnp.where(core == 0, other, chip)], 3
    ).reshape(-1)


def cut_else(flat):
    rows = flat.reshape(-1, D)
    counts = [P_SIZE, NCLS, TFREQ, D, 2 * D, P_SIZE]
    ends = [sum(counts[: place + 1]) for place in range(6)]
    parts = [rows[end - count : end] for end, count in zip(ends, counts)]
    parts[4] = parts[4].reshape(D, 2 * D)
    parts[5] = parts[5].reshape(D, P_SIZE)
    return tuple(parts)


def total(value):
    if not is_box():
        return lax.psum(value, ("fsdp", "ctx", "tp"))
    value = value + swap_tp(value)
    value = value + swap_y(value)
    for bit in (1, 2, 4):
        value = value + swap_f(value, bit)
    return value


def tp_sum(value):
    if lax.axis_size("tp") == 2:
        return value + swap_tp(value)
    return lax.psum(value, "tp")


def columns_in(value):
    if lax.axis_size("tp") == 2:
        other = swap_tp(value)
        at_zero = lax.axis_index("tp") == 0
        return jnp.concatenate(
            [jnp.where(at_zero, value, other), jnp.where(at_zero, other, value)], -1
        )
    return lax.all_gather(value, "tp", axis=value.ndim - 1, tiled=True)


def rows_in(value_low):
    if lax.axis_size("tp") == 2:
        return [value_low, swap_tp(value_low)]
    return [lax.all_gather(value_low, "tp", axis=0, tiled=True)]


def each_half(work, row_sets):
    if len(row_sets) == 2:
        other = work(row_sets[1])
        sent = swap_tp(other[-1])
        own = work(row_sets[0])
        return [own[:-1], other[:-1]], [own[-1], sent]
    whole = work(row_sets[0])
    return [whole[:-1]], [lax.psum_scatter(whole[-1], "tp", scatter_dimension=0, tiled=True)]


BIG = 56 * 1024 * 1024


def against_value(left_op, right_op):
    return lax.dot_general(
        left_op, right_op, (((1,), (1,)), ((), ())), preferred_element_type=jnp.float32
    )


def untile_into(matrix, tile_set):
    rows, columns = matrix.shape[0] // B, matrix.shape[1] // B
    for row in range(rows):
        for column in range(columns):
            matrix[row * B : (row + 1) * B, column * B : (column + 1) * B] = tile_set[
                row * columns + column
            ]


def segments(tp_parts):
    found = []
    begin = 0
    for height, breadth in shard_shapes(tp_parts):
        amount = height * breadth // (B * B)
        found.append((amount, begin))
        begin += amount
    return found


def weight_spec(kind, tp_parts):
    amount, begin = segments(tp_parts)[kind]
    return pl.BlockSpec(
        (amount, B, B), lambda *step: (begin // amount, 0, 0), pipeline_mode=pl.Buffered(1)
    )


def rows_spec(rows, breadth):
    return pl.BlockSpec((rows, breadth), lambda step: (step, 0))


def shaped(rows, breadth, kind):
    return jax.ShapeDtypeStruct((rows, breadth), kind)


def params():
    return pltpu.CompilerParams(vmem_limit_bytes=BIG)


def attend_kernel(normed_in, qkv_tiles, proj_tiles, projected, attended, partial, w_qkv, w_proj):
    @pl.when(pl.program_id(0) == 0)
    def _():
        untile_into(w_qkv, qkv_tiles)
        untile_into(w_proj, proj_tiles)

    values = low(product(normed_in[...], w_qkv[...]))
    projected[...] = values
    width = values.shape[1] // 3
    results = []
    for head in range(width // HD):
        at = head * HD
        query = values[:, at : at + HD]
        key_rows = values[:, width + at : width + at + HD]
        value_rows = values[:, 2 * width + at : 2 * width + at + HD]
        scores = against_value(query, key_rows) * HD ** (-0.5)
        exponent = jnp.exp(scores - jnp.max(scores, -1, keepdims=True))
        probabilities = low(exponent / jnp.sum(exponent, -1, keepdims=True))
        results.append(low(product(probabilities, value_rows)))
    result = jnp.concatenate(results, 1)
    attended[...] = result
    partial[...] = product(result, w_proj[...])


def attend_call(normed_in, store, tp_parts, local_len):
    rows = normed_in.shape[0]
    width = D // tp_parts
    return pl.pallas_call(
        attend_kernel,
        grid=(rows // local_len,),
        in_specs=[
            rows_spec(local_len, D),
            weight_spec(0, tp_parts),
            weight_spec(1, tp_parts),
        ],
        out_specs=[
            rows_spec(local_len, 3 * width),
            rows_spec(local_len, width),
            rows_spec(local_len, D),
        ],
        out_shape=[
            shaped(rows, 3 * width, jnp.bfloat16),
            shaped(rows, width, jnp.bfloat16),
            shaped(rows, D, jnp.float32),
        ],
        scratch_shapes=[
            pltpu.VMEM((D, 3 * width), jnp.bfloat16),
            pltpu.VMEM((width, D), jnp.bfloat16),
        ],
        compiler_params=params(),
        cost_estimate=pl.CostEstimate(
            flops=rows * D * width * 8, bytes_accessed=rows * D * 8, transcendentals=rows * 2048
        ),
    )(normed_in, store, store)


def attend_back_kernel(
    grad_branch, projected, qkv_tiles, proj_tiles, grad_qkv, partial, w_qkv, w_proj
):
    @pl.when(pl.program_id(0) == 0)
    def _():
        untile_into(w_qkv, qkv_tiles)
        untile_into(w_proj, proj_tiles)

    grad_attended = low(against_value(grad_branch[...], w_proj[...]))
    values = projected[...]
    width = values.shape[1] // 3
    grads = [[], [], []]
    for head in range(width // HD):
        at = head * HD
        query = values[:, at : at + HD]
        key_rows = values[:, width + at : width + at + HD]
        value_rows = values[:, 2 * width + at : 2 * width + at + HD]
        grad_here = grad_attended[:, at : at + HD]
        scores = against_value(query, key_rows) * HD ** (-0.5)
        exponent = jnp.exp(scores - jnp.max(scores, -1, keepdims=True))
        probabilities = exponent / jnp.sum(exponent, -1, keepdims=True)
        grad_prob = against_value(grad_here, value_rows)
        grad_scores = low(
            probabilities
            * (grad_prob - jnp.sum(probabilities * grad_prob, -1, keepdims=True))
        )
        grads[0].append(low(product(grad_scores, key_rows) * HD ** (-0.5)))
        grads[1].append(low(over_rows(grad_scores, query) * HD ** (-0.5)))
        grads[2].append(low(over_rows(low(probabilities), grad_here)))
    result = jnp.concatenate(grads[0] + grads[1] + grads[2], 1)
    grad_qkv[...] = result
    partial[...] = against_value(result, w_qkv[...])


def attend_back_call(grad_branch, projected, store, tp_parts, local_len):
    rows = grad_branch.shape[0]
    width = D // tp_parts
    return pl.pallas_call(
        attend_back_kernel,
        grid=(rows // local_len,),
        in_specs=[
            rows_spec(local_len, D),
            rows_spec(local_len, 3 * width),
            weight_spec(0, tp_parts),
            weight_spec(1, tp_parts),
        ],
        out_specs=[rows_spec(local_len, 3 * width), rows_spec(local_len, D)],
        out_shape=[shaped(rows, 3 * width, jnp.bfloat16), shaped(rows, D, jnp.float32)],
        scratch_shapes=[
            pltpu.VMEM((D, 3 * width), jnp.bfloat16),
            pltpu.VMEM((width, D), jnp.bfloat16),
        ],
        compiler_params=params(),
        cost_estimate=pl.CostEstimate(
            flops=rows * D * width * 10, bytes_accessed=rows * D * 8, transcendentals=rows * 2048
        ),
    )(grad_branch, projected, store, store)


def mlp_kernel(normed_mid, up_tiles, down_tiles, hidden, partial, w_up, w_down):
    @pl.when(pl.program_id(0) == 0)
    def _():
        untile_into(w_up, up_tiles)
        untile_into(w_down, down_tiles)

    values = product(normed_mid[...], w_up[...])
    hidden[...] = values
    partial[...] = product(low(gelu_tanh(values)), w_down[...])


def mlp_call(normed_mid, store, tp_parts, local_len):
    rows = normed_mid.shape[0]
    width = F // tp_parts
    return pl.pallas_call(
        mlp_kernel,
        grid=(rows // local_len,),
        in_specs=[
            rows_spec(local_len, D),
            weight_spec(2, tp_parts),
            weight_spec(3, tp_parts),
        ],
        out_specs=[rows_spec(local_len, width), rows_spec(local_len, D)],
        out_shape=[shaped(rows, width, jnp.float32), shaped(rows, D, jnp.float32)],
        scratch_shapes=[
            pltpu.VMEM((D, width), jnp.bfloat16),
            pltpu.VMEM((width, D), jnp.bfloat16),
        ],
        compiler_params=params(),
        cost_estimate=pl.CostEstimate(
            flops=rows * D * width * 4,
            bytes_accessed=rows * D * 12 + 4 * D * width,
            transcendentals=rows * width,
        ),
    )(normed_mid, store, store)


def mlp_back_kernel(
    grad_mlp, hidden, up_tiles, down_tiles, activation, grad_hidden, partial, w_up, w_down
):
    @pl.when(pl.program_id(0) == 0)
    def _():
        untile_into(w_up, up_tiles)
        untile_into(w_down, down_tiles)

    values = hidden[...]
    factor = math.sqrt(2.0 / math.pi)
    square = values * values
    bent = jnp.tanh(factor * (values + 0.044715 * (square * values)))
    half_up = 0.5 * (1.0 + bent)
    activation[...] = low(values * half_up)
    slope = half_up + 0.5 * values * (1.0 - bent * bent) * (
        factor * (1.0 + 3.0 * 0.044715 * square)
    )
    grad = low(against_value(grad_mlp[...], w_down[...]) * slope)
    grad_hidden[...] = grad
    partial[...] = against_value(grad, w_up[...])


def mlp_back_call(grad_mlp, hidden, store, tp_parts, local_len):
    rows = grad_mlp.shape[0]
    width = F // tp_parts
    return pl.pallas_call(
        mlp_back_kernel,
        grid=(rows // local_len,),
        in_specs=[
            rows_spec(local_len, D),
            rows_spec(local_len, width),
            weight_spec(2, tp_parts),
            weight_spec(3, tp_parts),
        ],
        out_specs=[
            rows_spec(local_len, width),
            rows_spec(local_len, width),
            rows_spec(local_len, D),
        ],
        out_shape=[
            shaped(rows, width, jnp.bfloat16),
            shaped(rows, width, jnp.bfloat16),
            shaped(rows, D, jnp.float32),
        ],
        scratch_shapes=[
            pltpu.VMEM((D, width), jnp.bfloat16),
            pltpu.VMEM((width, D), jnp.bfloat16),
        ],
        compiler_params=params(),
        cost_estimate=pl.CostEstimate(
            flops=rows * D * width * 4,
            bytes_accessed=rows * D * 16 + 4 * D * width,
            transcendentals=rows * width,
        ),
    )(grad_mlp, hidden, store, store)


def modes_call(cond_act, store, tp_parts):
    rows = cond_act.shape[0]
    width = 6 * D // tp_parts

    def kernel(left, tile_set, out):
        for column in range(width // B):
            total_here = 0.0
            for row in range(D // B):
                total_here = total_here + product(
                    left[:, row * B : (row + 1) * B], tile_set[row * (width // B) + column]
                )
            out[:, column * B : (column + 1) * B] = total_here

    return pl.pallas_call(
        kernel,
        grid=(1,),
        in_specs=[rows_spec(rows, D), weight_spec(4, tp_parts)],
        out_specs=rows_spec(rows, width),
        out_shape=shaped(rows, width, jnp.float32),
        compiler_params=params(),
    )(cond_act, store)


def three_parts(value):
    first = low(value)
    rest = value - wide(first)
    second = low(rest)
    return jnp.concatenate([first, second, low(rest - wide(second))], 0)


def against_low(value, weight):
    rows = value.shape[0]
    summed = against(three_parts(value), weight)
    return summed[:rows] + summed[rows : 2 * rows] + summed[2 * rows :]


def modes_back_call(grads, store, tp_parts):
    rows = grads.shape[0]
    width = 6 * D // tp_parts
    parts = three_parts(grads)

    def kernel(left, tile_set, out):
        for row in range(D // B):
            total_here = 0.0
            for column in range(width // B):
                total_here = total_here + against_value(
                    left[:, column * B : (column + 1) * B],
                    tile_set[row * (width // B) + column],
                )
            out[:, row * B : (row + 1) * B] = total_here

    summed = pl.pallas_call(
        kernel,
        grid=(1,),
        in_specs=[rows_spec(3 * rows, width), weight_spec(4, tp_parts)],
        out_specs=rows_spec(3 * rows, D),
        out_shape=shaped(3 * rows, D, jnp.float32),
        compiler_params=params(),
    )(parts, store)
    return summed[:rows] + summed[rows : 2 * rows] + summed[2 * rows :]


def weight_grad_call(lefts, rights, places, first_tile, held):
    height, breadth = lefts[0].shape[1], rights[0].shape[1]
    width = 512 if breadth % 512 == 0 else breadth
    steps = breadth // width
    count = len(lefts)
    row_tiles, column_tiles, all_columns = height // B, width // B, breadth // B
    amount = row_tiles * column_tiles
    given = [array for _, _, array in held if array is not None]

    def kernel(place, *refs):
        left_refs, right_refs = refs[:count], refs[count : 2 * count]
        outs = refs[2 * count + len(given) : 2 * count + len(given) + len(held)]
        turned, ready, sem = refs[-2 - count : -2], refs[-2], refs[-1]
        step = pl.program_id(0)
        slot = lax.rem(step, 2)

        @pl.when(step == 0)
        def _():
            for turned_here, left in zip(turned, left_refs):
                turned_here[...] = left[...].T

        def drain(which):
            pltpu.make_async_copy(
                ready.at[which], outs[0].at[pl.ds(0, amount)], sem.at[which]
            ).wait()

        @pl.when(step >= 2)
        def _():
            drain(slot)

        block = product(turned[0][...], right_refs[0][...])
        for turned_here, right in zip(turned[1:], right_refs[1:]):
            block = block + product(turned_here[...], right[...])
        block = low(block)
        for row in range(row_tiles):
            for column in range(column_tiles):
                ready[slot, row * column_tiles + column] = block[
                    row * B : (row + 1) * B, column * B : (column + 1) * B
                ]

        def send(index, carry):
            row, column = index // column_tiles, index % column_tiles
            where_to = place[first_tile + row * all_columns + step * column_tiles + column]
            for number, (begin, _, _) in enumerate(held):
                end = held[number + 1][0] if number + 1 < len(held) else 1 << 30
                copy = pltpu.make_async_copy(
                    ready.at[slot, index], outs[number].at[where_to - begin], sem.at[slot]
                )
                if len(held) == 1:
                    copy.start()
                else:
                    pl.when((where_to >= begin) & (where_to < end))(copy.start)
            return carry

        lax.fori_loop(0, amount, send, 0)

        @pl.when(step == steps - 1)
        def _():
            drain(slot)
            if steps > 1:
                drain(1 - slot)

    rows = [left.shape[0] for left in lefts]
    anywhere = pl.BlockSpec(memory_space=pl.ANY)
    in_specs = [
        pl.BlockSpec((size, height), lambda step, place: (0, 0), pipeline_mode=pl.Buffered(1))
        for size in rows
    ] + [pl.BlockSpec((size, width), lambda step, place: (0, step)) for size in rows]
    in_specs += [anywhere] * len(given)
    operands = [places, *lefts, *rights, *given]
    aliases = {}
    for number, (_, _, array) in enumerate(held):
        if array is not None:
            aliases[1 + 2 * count + len(aliases)] = number
    results = pl.pallas_call(
        kernel,
        grid_spec=pltpu.PrefetchScalarGridSpec(
            num_scalar_prefetch=1,
            grid=(steps,),
            in_specs=in_specs,
            out_specs=[anywhere] * len(held),
            scratch_shapes=[pltpu.VMEM((height, size), jnp.bfloat16) for size in rows]
            + [pltpu.VMEM((2, amount, B, B), jnp.bfloat16), pltpu.SemaphoreType.DMA((2,))],
        ),
        out_shape=[
            jax.ShapeDtypeStruct((places_here, B, B), jnp.bfloat16) for _, places_here, _ in held
        ],
        input_output_aliases=aliases,
        compiler_params=params(),
        cost_estimate=pl.CostEstimate(
            flops=2 * sum(rows) * height * breadth,
            bytes_accessed=2 * (sum(rows) * (height + breadth) + height * breadth),
            transcendentals=0,
        ),
    )(*operands)
    return [
        (begin, places_here, array) for (begin, places_here, _), array in zip(held, results)
    ]


def place_call(pieces, targets, held):
    count = len(pieces)
    given = [array for _, _, array in held if array is not None]

    def kernel(target, *refs):
        outs = refs[count + len(given) : count + len(given) + len(held)]
        token = refs[count + len(given) + len(held)]
        buffers, loaded, stored = refs[-2 - count : -2], refs[-2], refs[-1]
        token[...] = jnp.zeros_like(token)
        for number in range(count):
            pltpu.make_async_copy(refs[number], buffers[number], loaded.at[number]).start()
        for number, (piece, begin) in enumerate(pieces):
            pltpu.make_async_copy(refs[number], buffers[number], loaded.at[number]).wait()

            def send(index, carry):
                where_to = target[begin + index]
                left = True
                for out_number, (first, amount, _) in enumerate(held):
                    last = out_number == len(held) - 1
                    inside = (where_to >= first) & (where_to < first + amount - 1)
                    at = where_to - first
                    if last:
                        at = jnp.where(inside, at, amount - 1)
                        inside = left
                    else:
                        left = jnp.logical_not(inside)
                    copy = pltpu.make_async_copy(
                        buffers[number].at[index], outs[out_number].at[at], stored.at[number]
                    )
                    if len(held) == 1:
                        copy.start()
                    else:
                        pl.when(inside)(copy.start)
                return carry

            lax.fori_loop(0, piece.shape[0], send, 0)
        for number, (piece, begin) in enumerate(pieces):
            pltpu.make_async_copy(
                buffers[number], outs[0].at[pl.ds(0, piece.shape[0])], stored.at[number]
            ).wait()

    anywhere = pl.BlockSpec(memory_space=pl.ANY)
    operands = [targets] + [piece for piece, _ in pieces] + given
    aliases = {}
    for number, (_, _, array) in enumerate(held):
        if array is not None:
            aliases[1 + count + len(aliases)] = number
    results = pl.pallas_call(
        kernel,
        grid_spec=pltpu.PrefetchScalarGridSpec(
            num_scalar_prefetch=1,
            grid=(1,),
            in_specs=[anywhere] * (len(operands) - 1),
            out_specs=[anywhere] * len(held) + [pl.BlockSpec((8, B), lambda step, target: (0, 0))],
            scratch_shapes=[pltpu.VMEM(piece.shape, jnp.bfloat16) for piece, _ in pieces]
            + [pltpu.SemaphoreType.DMA((count,))] * 2,
        ),
        out_shape=[jax.ShapeDtypeStruct((amount, B, B), jnp.bfloat16) for _, amount, _ in held]
        + [jax.ShapeDtypeStruct((8, B), jnp.float32)],
        input_output_aliases=aliases,
        compiler_params=params(),
        cost_estimate=pl.CostEstimate(
            flops=0,
            bytes_accessed=sum(4 * piece.shape[0] * B * B for piece, _ in pieces),
            transcendentals=0,
        ),
    )(*operands)
    return [(first, amount, array) for (first, amount, _), array in zip(held, results)], results[-1]


def chips_sum(value):
    for swap in (swap_y, swap_x, lambda part: swap_f(part, 2), lambda part: swap_f(part, 4)):
        value = value + swap(value)
    return value


LOT = 16


def lots(count):
    return (count + LOT - 1) // LOT


def bring_strays(store, strays, count, owned_tiles, ordering, slots, me):
    def body(state):
        lot, held = state
        tiles = lax.dynamic_slice_in_dim(strays, lot * LOT, LOT, 0)
        valid = lot * LOT + jnp.arange(LOT) < count
        here = ordering[tiles]
        mine = valid & (here // slots == me)
        sent = jnp.where(mine[:, None, None], owned_tiles[here % slots], 0)
        sent = chips_sum(sent)
        at = jnp.where(valid, tiles, held.shape[0])
        return lot + 1, held.at[at].set(sent, mode="drop")

    return lax.while_loop(lambda state: state[0] < lots(count), body, (0, store))[1]


def sum_strays(owned, parts, strays, count, ordering, slots, me):
    def body(state):
        lot, held = state
        tiles = lax.dynamic_slice_in_dim(strays, lot * LOT, LOT, 0)
        valid = lot * LOT + jnp.arange(LOT) < count
        summed = chips_sum(wide(lax.dynamic_slice_in_dim(parts, lot * LOT, LOT, 0)))
        here = ordering[tiles]
        at = jnp.where(valid & (here // slots == me), here % slots, slots)
        return lot + 1, held.at[at].set(summed, mode="drop")

    return lax.while_loop(lambda state: state[0] < lots(count), body, (0, owned))[1]


def normed_value(stream):
    centred = stream - jnp.mean(stream, -1, keepdims=True)
    rate = lax.rsqrt(jnp.mean(centred * centred, -1, keepdims=True) + EPS_NORM)
    return centred * rate, rate


def rows_kernel_call(kernel, wide_ins, mode_ins, outs):
    own, group = wide_ins[0].shape[:2]
    rows = pl.BlockSpec((1, group, D), lambda step: (step, 0, 0))
    few = lambda count: pl.BlockSpec((1, count, D), lambda step: (step, 0, 0))
    return pl.pallas_call(
        kernel,
        grid=(own,),
        in_specs=[rows] * len(wide_ins) + [few(modes.shape[1]) for modes in mode_ins],
        out_specs=[rows if count is None else few(count) for count, _ in outs],
        out_shape=[
            jax.ShapeDtypeStruct((own, group if count is None else count, D), kind)
            for count, kind in outs
        ],
        compiler_params=params(),
        cost_estimate=pl.CostEstimate(
            flops=own * group * D * 20,
            bytes_accessed=own * group * D * 4 * (len(wide_ins) + len(outs)),
            transcendentals=own * group,
        ),
    )(*wide_ins, *mode_ins)


def modulate_call(stream, modes, shift, scale):
    def kernel(values, mode, out):
        out[0] = low(
            normed_value(values[0])[0] * (1.0 + mode[0, scale : scale + 1, :])
            + mode[0, shift : shift + 1, :]
        )

    return rows_kernel_call(kernel, [stream], [modes], [(None, jnp.bfloat16)])[0]


def residual_call(stream, terms, modes, gate, next_modes, shift, scale):
    def kernel(*refs):
        values, term_refs = refs[0], refs[1 : 1 + len(terms)]
        mode, mode_next, branch, stream_new, out = refs[1 + len(terms) :]
        summed = term_refs[0][0]
        for term in term_refs[1:]:
            summed = summed + term[0]
        branch[0] = summed
        result = values[0] + mode[0, gate : gate + 1, :] * summed
        stream_new[0] = result
        out[0] = low(
            normed_value(result)[0] * (1.0 + mode_next[0, scale : scale + 1, :])
            + mode_next[0, shift : shift + 1, :]
        )

    shape = stream.shape
    return rows_kernel_call(
        kernel,
        [stream] + [term.reshape(shape) for term in terms],
        [modes, next_modes],
        [(None, jnp.float32), (None, jnp.float32), (None, jnp.bfloat16)],
    )


def back_call(stream, terms, upstream, modes, scale, below):
    shape = stream.shape
    wide_ins = [stream] + [term.reshape(shape) for term in terms]
    if upstream is not None:
        wide_ins.append(upstream)
    mode_ins = [modes]
    outs = [(None, jnp.float32), (3 if below else 2, jnp.float32)]
    if below:
        branch, branch_modes, gate = below
        wide_ins.append(branch)
        mode_ins.append(branch_modes)
        outs.append((None, jnp.bfloat16))

    def kernel(*refs):
        ins, modes_in = refs[: len(wide_ins)], refs[len(wide_ins) : len(wide_ins) + len(mode_ins)]
        results = refs[len(wide_ins) + len(mode_ins) :]
        grad = ins[1][0]
        for term in ins[2 : 1 + len(terms)]:
            grad = grad + term[0]
        normal, rate = normed_value(ins[0][0])
        results[1][0, 0:1, :] = jnp.sum(grad, 0, keepdims=True)
        results[1][0, 1:2, :] = jnp.sum(grad * normal, 0, keepdims=True)
        grad = grad * (1.0 + modes_in[0][0, scale : scale + 1, :])
        grad = rate * (
            grad
            - jnp.mean(grad, -1, keepdims=True)
            - normal * jnp.mean(grad * normal, -1, keepdims=True)
        )
        if upstream is not None:
            grad = grad + ins[1 + len(terms)][0]
        results[0][0] = grad
        if below:
            results[1][0, 2:3, :] = jnp.sum(grad * ins[-1][0], 0, keepdims=True)
            results[2][0] = low(modes_in[1][0, gate : gate + 1, :] * grad)

    return rows_kernel_call(kernel, wide_ins, mode_ins, outs)


def update_kernel(clip, grad, master, first, second, bases, master_out, first_out, second_out, low_out):
    eye = lax.broadcasted_iota(jnp.int32, (B, B), 0) == lax.broadcasted_iota(jnp.int32, (B, B), 1)
    for tile in range(grad.shape[0]):
        left_row = bases[tile, 0:1, :]
        right_row = bases[tile, 1:2, :]
        left_col = jnp.sum(jnp.where(eye, left_row, 0.0), 1, keepdims=True)
        left_rate = 2.0 / jnp.sum(left_row * left_row, 1, keepdims=True)
        right_rate = 2.0 / jnp.sum(right_row * right_row, 1, keepdims=True)
        left_scaled = left_col * left_rate
        right_scaled = right_row * right_rate

        def turn(middle):
            middle = middle - left_scaled * jnp.sum(left_col * middle, 0, keepdims=True)
            return middle - jnp.sum(middle * right_row, 1, keepdims=True) * right_scaled

        turned = turn(clip[0, 0] * grad[tile])
        first_new = 0.5 * first[tile] + 0.5 * turned
        second_new = 0.5 * second[tile] + 0.5 * turned * turned
        direction = first_new / (jnp.sqrt(second_new) + 1e-08)
        master_new = master[tile] - RATE * turn(direction)
        master_out[tile] = master_new
        first_out[tile] = first_new
        second_out[tile] = second_new
        low_out[tile] = master_new.astype(jnp.bfloat16)


def update_tiles(clip_factor, grad, master, first, second, bases):
    slots = grad.shape[0]
    amount = 3
    tile_spec = pl.BlockSpec((amount, B, B), lambda step: (step, 0, 0))
    whole = jax.ShapeDtypeStruct(grad.shape, jnp.float32)
    return pl.pallas_call(
        update_kernel,
        grid=(slots // amount,),
        in_specs=[pl.BlockSpec(memory_space=pltpu.SMEM)]
        + [tile_spec] * 4
        + [pl.BlockSpec((amount, 2, B), lambda step: (step, 0, 0))],
        out_specs=[tile_spec] * 4,
        out_shape=[whole, whole, whole, jax.ShapeDtypeStruct(grad.shape, jnp.bfloat16)],
        compiler_params=params(),
        cost_estimate=pl.CostEstimate(
            flops=slots * B * B * 30, bytes_accessed=slots * B * B * 30, transcendentals=slots * B * B
        ),
    )(clip_factor.reshape(1, 1), grad, master, first, second, bases)


def on_device(
    latents,
    noise,
    timesteps,
    labels,
    owners,
    tiles_low,
    tiles_master,
    tiles_first,
    tiles_second,
    bases,
    else_low,
    else_master,
    else_first,
    else_second,
):
    box = is_box()
    tp_parts = lax.axis_size("tp")
    tp_index = lax.axis_index("tp")
    ctx_parts = lax.axis_size("ctx")
    fsdp_parts = lax.axis_size("fsdp")
    images = latents.shape[0]
    local_len = latents.shape[1]
    slots = tiles_low.shape[1]
    sp_rows = images * local_len // tp_parts
    first_row = tp_index * sp_rows
    own = max(1, sp_rows // local_len)
    group = sp_rows // own
    first_image = first_row // local_len
    element_count = images * fsdp_parts * ctx_parts * local_len * P_SIZE
    ordering = jnp.argsort(owners, stable=True)
    inverse = jnp.argsort(ordering)
    all_tiles = inverse.shape[0]
    per_layer = all_tiles // L
    if box:
        early = early_slots(slots)
        me = lax.axis_index("fsdp") * ctx_parts + lax.axis_index("ctx")
        tile = jnp.arange(all_tiles, dtype=jnp.int32)
        owner, slot = inverse // slots, inverse % slots
        is_early = slot < early
        place_early = early_place(owner, slot, early)
        place_late = late_place(owner, slot - early, slots - early)
        gather_places = jnp.where(is_early, place_early, 16 * early + place_late)
        targets = jnp.argsort(gather_places).astype(jnp.int32)
        is_stray = jnp.logical_not(is_early) & (tile < per_layer)
        stray_count = jnp.sum(is_stray.astype(jnp.int32))
        stray_rank = jnp.cumsum(is_stray.astype(jnp.int32)) - 1
        room = 16 * (slots - early)
        strays = jnp.argsort(jnp.where(is_stray, tile, all_tiles + tile)).astype(jnp.int32)
        strays = jnp.concatenate([strays, jnp.zeros((LOT,), jnp.int32)])
        places = jnp.where(
            is_stray,
            room + 16 * (early + 1) + stray_rank,
            jnp.where(is_early, room + early_place(owner, slot, early + 1), place_late),
        ).astype(jnp.int32)
        stores = [(0, per_layer + 1, None), (per_layer, per_layer + 1, None)]
        late_store = None

        def place_early_tiles(tile_group):
            nonlocal stores
            stores, token = place_call(tile_group, targets, stores)
            return token

        def place_late_tiles(tile_group):
            nonlocal late_store
            tile_group = [(piece, 16 * early + at) for piece, at in tile_group]
            if late_store is None:
                late_store = [stores[1]]
            late_store, token = place_call(tile_group, targets, late_store)
            return token

        late_store = None
        else_parts = gather_tiles(
            tiles_low[0], early, place_early_tiles, place_late_tiles, else_low, targets
        )
        store = [
            bring_strays(stores[0][2], strays, stray_count, tiles_low[0], inverse, slots, me),
            late_store[0][2],
        ]
        held = [(0, room, None), (room, 16 * (slots + 1) + LOT, None)]
    else:
        places = jnp.arange(all_tiles, dtype=jnp.int32)
        gathered = lax.all_gather(tiles_low, ("fsdp", "ctx"), axis=1, tiled=True)[0][inverse]
        store = [gathered[:per_layer], gathered[per_layer:]]
        held = [(0, all_tiles, None)]
        else_parts = cut_else(gather_else(else_low, None, None))
    patch_weight, class_table, time_first, time_second, final_weight, head_weight = else_parts
    features_low = low(time_features(timesteps))
    onehot = low(labels[:, None] == jnp.arange(NCLS)[None, :])
    time_hidden = product(features_low, time_first)
    time_act = low(jax.nn.silu(time_hidden))
    condition = product(time_act, time_second) + product(onehot, class_table)
    cond_act = low(jax.nn.silu(condition))
    modes = [
        lax.dynamic_slice_in_dim(
            columns_in(modes_call(cond_act, store[layer_no], tp_parts)), first_image, own, 0
        ).reshape(own, 6, D)
        for layer_no in range(L)
    ]
    final_modes = lax.dynamic_slice_in_dim(
        product(cond_act, final_weight), first_image, own, 0
    ).reshape(own, 2, D)
    row_index = first_row + jnp.arange(sp_rows)
    signal = signal_level(timesteps)
    noisy_input = (
        jnp.sqrt(signal)[:, None, None] * latents + jnp.sqrt(1.0 - signal)[:, None, None] * noise
    )
    noisy_rows = low(
        lax.dynamic_slice_in_dim(
            noisy_input.reshape(images * local_len, P_SIZE), first_row, sp_rows, 0
        )
    )
    target = lax.dynamic_slice_in_dim(
        noise.reshape(images * local_len, P_SIZE), first_row, sp_rows, 0
    )
    stream = (product(noisy_rows, patch_weight) + position_table(row_index % local_len)).reshape(
        own, group, D
    )
    normed_in = modulate_call(stream, modes[0], 0, 1)
    kept = []
    for layer_no in range(L):
        row_sets = rows_in(normed_in.reshape(sp_rows, D))
        halves, terms = each_half(
            lambda rows: attend_call(rows, store[layer_no], tp_parts, local_len), row_sets
        )
        branch, middle, normed_mid = residual_call(
            stream, terms, modes[layer_no], 2, modes[layer_no], 3, 4
        )
        mid_sets = rows_in(normed_mid.reshape(sp_rows, D))
        hidden, terms = each_half(
            lambda rows: mlp_call(rows, store[layer_no], tp_parts, local_len), mid_sets
        )
        last = layer_no == L - 1
        mlp_out, stream_new, normed_in = residual_call(
            middle,
            terms,
            modes[layer_no],
            5,
            final_modes if last else modes[layer_no + 1],
            0,
            1,
        )
        kept.append((stream, row_sets, halves, branch, middle, mid_sets, hidden, mlp_out))
        stream = stream_new
    head_low = normed_in.reshape(sp_rows, D)
    mismatch = product(head_low, head_weight) - target
    loss_part = jnp.sum(mismatch * mismatch) / element_count
    grad_pred = low(2.0 * mismatch / element_count)
    grad_head = over_rows(grad_pred, head_low)
    upstream, final_sums, grad_low = back_call(
        stream,
        [against(grad_pred, head_weight)],
        None,
        final_modes,
        1,
        (kept[-1][7], modes[-1], 5),
    )
    grad_final = final_sums[:, :2].reshape(own, 2 * D)
    gate_sum = final_sums[:, 2:]
    starts = [begin for _, begin in segments(tp_parts)]
    mode_width = 6 * D // tp_parts
    fill = (-3 * images) % 16
    conds = jnp.pad(jnp.concatenate([cond_act] * 3, 0), ((0, fill), (0, 0)))

    def all_images(values):
        return tp_sum(
            lax.dynamic_update_slice_in_dim(
                jnp.zeros((images, values.shape[1]), jnp.float32), values, first_image, 0
            )
        )

    grad_final = all_images(grad_final)
    cond_wide = wide(cond_act)

    def image_part(columns):
        packed = jnp.concatenate(columns, 1)
        packed = jnp.pad(packed, ((0, 0), (0, -packed.shape[1] % 256)))
        part = packed.shape[1] // 2
        return lax.dynamic_slice_in_dim(packed, tp_index * part, part, 1)

    def every_image(columns):
        if not box:
            return gather_images(jnp.concatenate(columns, 1))
        return columns_in(gather_images(image_part(columns)))

    label_column = jnp.broadcast_to(wide(labels)[:, None], (images, 128))
    cuts = [128]
    for length in (TFREQ, D, D):
        cuts.append(cuts[-1] + length)
    early_images = every_image(
        [label_column, wide(features_low), wide(time_act), cond_wide, grad_final]
    )
    all_labels, all_features, all_time, all_cond, all_final = jnp.split(early_images, cuts, 1)
    all_final = all_final[:, : 2 * D]
    head_rows = total(grad_head).T.reshape(P_SIZE, D)
    grad_cond_act = 0.0
    for layer_no in reversed(range(L)):
        stream, row_sets, halves, branch, middle, mid_sets, hidden, mlp_out = kept[layer_no]
        base = layer_no * per_layer
        grad_sets = rows_in(grad_low.reshape(sp_rows, D))
        results, terms = each_half(
            lambda pair: mlp_back_call(pair[0], pair[1], store[layer_no], tp_parts, local_len),
            [(rows, hidden_here[0]) for rows, hidden_here in zip(grad_sets, hidden)],
        )
        held = weight_grad_call(
            [result[0] for result in results], grad_sets, places, base + starts[3], held
        )
        held = weight_grad_call(
            mid_sets, [result[1] for result in results], places, base + starts[2], held
        )
        upstream, mlp_sums, grad_low = back_call(
            middle, terms, upstream, modes[layer_no], 4, (branch, modes[layer_no], 2)
        )
        grad_sets = rows_in(grad_low.reshape(sp_rows, D))
        results, terms = each_half(
            lambda pair: attend_back_call(pair[0], pair[1], store[layer_no], tp_parts, local_len),
            [(rows, half[0]) for rows, half in zip(grad_sets, halves)],
        )
        held = weight_grad_call(
            [half[1] for half in halves], grad_sets, places, base + starts[1], held
        )
        held = weight_grad_call(
            row_sets, [result[0] for result in results], places, base + starts[0], held
        )
        below = None if layer_no == 0 else (kept[layer_no - 1][7], modes[layer_no - 1], 5)
        found = back_call(stream, terms, upstream, modes[layer_no], 1, below)
        grad_modes = jnp.concatenate(
            [found[1][:, :2], mlp_sums[:, 2:], mlp_sums[:, :2], gate_sum], 1
        ).reshape(own, 6 * D)
        mode_image = lax.dynamic_slice_in_dim(
            all_images(grad_modes), tp_index * mode_width, mode_width, 1
        )
        held = weight_grad_call(
            [conds],
            [jnp.pad(three_parts(mode_image), ((0, fill), (0, 0)))],
            places,
            base + starts[4],
            held,
        )
        grad_cond_act = grad_cond_act + modes_back_call(mode_image, store[layer_no], tp_parts)
        upstream = found[0]
        if below:
            grad_low, gate_sum = found[2], found[1][:, 2:]
        if box and layer_no == L - 1:
            grad_low = after(grad_low, held[0][2], held[1][2], early_images, head_rows)
            lanes = Lanes()
            late_sums = scatter_late(held[0][2], slots - early, lanes)
            held = held[1:]
    grad_patch = over_rows(noisy_rows, low(upstream).reshape(sp_rows, D))
    grad_cond_act = tp_sum(grad_cond_act) + against_low(grad_final, final_weight)
    grad_condition = jax.vjp(jax.nn.silu, condition)[1](grad_cond_act)[0]
    grad_time_hidden = jax.vjp(jax.nn.silu, time_hidden)[1](
        against_low(grad_condition, time_second)
    )[0]
    if box:
        patch_sum = tp_sum(grad_patch)
        patch_first = low(patch_sum)
        patch_part = jnp.where(tp_index == 0, patch_first, low(patch_sum - wide(patch_first)))
        parts = lax.dynamic_update_slice_in_dim(
            held[0][2],
            patch_part.reshape(1, B, B),
            early_place(0, early, early + 1),
            0,
        )
        owned, owned_late, images_rows = scatter_early(
            parts, early + 1, lanes, late_sums, image_part([grad_time_hidden, grad_condition])
        )
        late_images = columns_in(images_rows)
        patch_rows = tp_sum(owned[early]).reshape(P_SIZE, D)
        owned = jnp.concatenate([owned[:early], owned_late], 0)
        owned = sum_strays(
            owned, parts[16 * (early + 1) :], strays, stray_count, inverse, slots, me
        )
    else:
        owned = lax.psum_scatter(
            wide(held[0][2])[ordering], ("fsdp", "ctx"), scatter_dimension=0, tiled=True
        )
        patch_rows = lax.psum(grad_patch, ("fsdp", "ctx", "tp"))
        late_images = every_image([grad_time_hidden, grad_condition])
    all_hidden, all_condition = jnp.split(late_images, 2, 1)
    all_onehot = wide(all_labels[:, :1] == jnp.arange(NCLS, dtype=jnp.float32)[None, :])
    share = else_low.shape[0]
    device = (lax.axis_index("fsdp") * ctx_parts + lax.axis_index("ctx")) * tp_parts + tp_index
    begin = device * share
    row_total = else_low.shape[0] * fsdp_parts * ctx_parts * tp_parts // D
    row_count = min(share // D + 2, row_total)
    begin_row = jnp.minimum(begin // D, row_total - row_count)
    row_ids = begin_row + jnp.arange(row_count)
    edge = jnp.zeros((all_cond.shape[0], P_SIZE), jnp.float32)
    factors = jnp.concatenate(
        [edge, all_onehot, all_features, all_time, jnp.repeat(all_cond, 2, axis=1), edge], 1
    )
    factors = lax.dynamic_slice_in_dim(factors, begin_row, row_count, 1)
    first_start = P_SIZE + NCLS
    second_start = first_start + TFREQ
    final_start = second_start + D

    def rows_of(chosen, right):
        return contract("ic,id->cd", jnp.where(chosen[None, :], factors, 0.0), right)

    in_first = (row_ids >= first_start) & (row_ids < second_start)
    in_final = row_ids >= final_start
    odd = (row_ids - final_start) % 2 == 1
    near = rows_of(in_first, all_hidden)
    near = near + rows_of(jnp.logical_not(in_first | in_final), all_condition)
    near = near + rows_of(in_final & jnp.logical_not(odd), all_final[:, :D])
    near = near + rows_of(in_final & odd, all_final[:, D:])
    for begin_here, token_rows in ((0, patch_rows), (row_total - P_SIZE, head_rows)):
        here = row_ids - begin_here
        inside = (here >= 0) & (here < P_SIZE)
        near = jnp.where(
            inside[:, None], token_rows[jnp.clip(here, 0, P_SIZE - 1)], near
        )
    else_grad = lax.dynamic_slice_in_dim(near.reshape(-1), begin - begin_row * D, share, 0)
    squares = jnp.sum(owned * owned) + jnp.sum(else_grad * else_grad)
    totals = total(jnp.stack([loss_part, squares]))
    loss_total = totals[0]
    grad_norm = jnp.sqrt(totals[1])
    clip_factor = jnp.minimum(1.0, 1.0 / grad_norm)
    master_new, first_new, second_new, low_new = update_tiles(
        clip_factor, owned, tiles_master[0], tiles_first[0], tiles_second[0], bases[0]
    )
    else_master_new, else_first_new, else_second_new = adamw_flat(
        clip_factor * else_grad, else_master, else_first, else_second
    )
    return (
        loss_total,
        grad_norm,
        master_new[None],
        first_new[None],
        second_new[None],
        low_new[None],
        else_master_new,
        else_first_new,
        else_second_new,
        low(else_master_new),
    )


def solution(mesh):
    return jax.shard_map(
        on_device,
        mesh=mesh,
        in_specs=(
            P(("fsdp", "ctx"), None, None),
            P(("fsdp", "ctx"), None, None),
            P(("fsdp", "ctx")),
            P(("fsdp", "ctx")),
            P(),
            P("tp", ("fsdp", "ctx"), None, None),
            P("tp", ("fsdp", "ctx"), None, None),
            P("tp", ("fsdp", "ctx"), None, None),
            P("tp", ("fsdp", "ctx"), None, None),
            P("tp", ("fsdp", "ctx"), None, None),
            P(("fsdp", "ctx", "tp")),
            P(("fsdp", "ctx", "tp")),
            P(("fsdp", "ctx", "tp")),
            P(("fsdp", "ctx", "tp")),
        ),
        out_specs=(
            P(),
            P(),
            P("tp", ("fsdp", "ctx"), None, None),
            P("tp", ("fsdp", "ctx"), None, None),
            P("tp", ("fsdp", "ctx"), None, None),
            P("tp", ("fsdp", "ctx"), None, None),
            P(("fsdp", "ctx", "tp")),
            P(("fsdp", "ctx", "tp")),
            P(("fsdp", "ctx", "tp")),
            P(("fsdp", "ctx", "tp")),
        ),
        check_vma=False,
    )
```

```python
import math

import jax
import jax.numpy as jnp
from jax import lax
from jax.experimental import pallas as pl
from jax.experimental.pallas import tpu as pltpu
from jax.sharding import PartitionSpec as P

D = 1024
HD = 64
F = 4096
P_SIZE = 16
TFREQ = 256
NCLS = 1000
GRID = 16
L = 2
B = 128


HIGHEST = lax.Precision.HIGHEST
EPS_NORM = 1e-06
RATE = 0.02
DECAY = 0.1


def matmul(left_op, right_op):
    return jnp.dot(left_op, right_op, precision=HIGHEST)


def contract(formula, left_op, right_op):
    return jnp.einsum(formula, left_op, right_op, precision=HIGHEST)


def product(left_op, right_op):
    return jnp.dot(left_op, right_op, preferred_element_type=jnp.float32)


def over_rows(left_op, right_op):
    return lax.dot_general(
        left_op, right_op, (((0,), (0,)), ((), ())), preferred_element_type=jnp.float32
    )


def against(left_op, right_op):
    return lax.dot_general(
        left_op, right_op, (((1,), (1,)), ((), ())), preferred_element_type=jnp.float32
    )


def normed(stream):
    centred = stream - jnp.mean(stream, -1, keepdims=True)
    return centred * lax.rsqrt(jnp.mean(centred * centred, -1, keepdims=True) + EPS_NORM)


def modulate(stream, offset, factor):
    return normed(stream) * (1.0 + factor) + offset


def gelu_tanh(values):
    return jax.nn.gelu(values, approximate=True)


def time_features(time_steps):
    half_count = TFREQ // 2
    freqs = jnp.exp(-math.log(10000.0) * jnp.arange(half_count, dtype=jnp.float32) / half_count)
    angles = time_steps.astype(jnp.float32)[:, None] * freqs[None, :]
    return jnp.concatenate([jnp.cos(angles), jnp.sin(angles)], -1)


def position_table(token_ids):
    quarter = D // 4
    omegas = 1.0 / 10000.0 ** (jnp.arange(quarter, dtype=jnp.float32) / quarter)
    row_angle = (token_ids // GRID).astype(jnp.float32)[:, None] * omegas[None, :]
    col_angle = (token_ids % GRID).astype(jnp.float32)[:, None] * omegas[None, :]
    return jnp.concatenate(
        [jnp.sin(row_angle), jnp.cos(row_angle), jnp.sin(col_angle), jnp.cos(col_angle)], -1
    )


def signal_level(time_steps):
    phase = (time_steps.astype(jnp.float32) / 1000.0 + 0.008) / 1.008 * (math.pi / 2)
    return jnp.cos(phase) ** 2


def shard_shapes(tp_parts):
    head_width = D // tp_parts
    hidden_width = F // tp_parts
    return [
        (D, 3 * head_width),
        (head_width, D),
        (D, hidden_width),
        (hidden_width, D),
        (D, 6 * head_width),
    ]


def untile(tile_set, height, breadth):
    block = tile_set.shape[-1]
    return (
        tile_set.reshape(height // block, breadth // block, block, block)
        .transpose(0, 2, 1, 3)
        .reshape(height, breadth)
    )


def retile(matrix):
    height, breadth = matrix.shape
    return matrix.reshape(height // B, B, breadth // B, B).transpose(0, 2, 1, 3).reshape(-1, B, B)


def unpack_layers(tile_set, tp_parts):
    layer_list = []
    cursor = 0
    for layer_no in range(L):
        matrices = []
        for height, breadth in shard_shapes(tp_parts):
            amount = height * breadth // (B * B)
            matrices.append(untile(tile_set[cursor : cursor + amount], height, breadth))
            cursor += amount
        layer_list.append(matrices)
    return layer_list


def pack_layers(layer_list):
    return jnp.concatenate([retile(matrix) for matrices in layer_list for matrix in matrices], 0)


def else_shapes():
    return [(P_SIZE, D), (NCLS, D), (TFREQ, D), (D, D), (D, 2 * D), (D, P_SIZE)]


def split_else(flat_params):
    components = []
    cursor = 0
    for height, breadth in else_shapes():
        components.append(flat_params[cursor : cursor + height * breadth].reshape(height, breadth))
        cursor += height * breadth
    return components


def reflection(vectors):
    outer_prod = vectors[..., :, None] * vectors[..., None, :]
    return (
        jnp.eye(vectors.shape[-1], dtype=jnp.float32)
        - 2.0 * outer_prod / jnp.sum(vectors * vectors, -1)[..., None, None]
    )


def rotate(left_basis, middle, right_basis):
    return contract(
        "...ab,...bc->...ac", contract("...ab,...bc->...ac", left_basis, middle), right_basis
    )


def adam_finish(turned, master_state, first_state, second_state, left_basis, right_basis):
    first_new = 0.5 * first_state + 0.5 * turned
    second_new = 0.5 * second_state + 0.5 * turned * turned
    direction = first_new / (jnp.sqrt(second_new) + 1e-08)
    return (master_state - RATE * rotate(left_basis, direction, right_basis), first_new, second_new)


def adamw_flat(grad_clipped, master_state, first_state, second_state):
    first_new = 0.5 * first_state + 0.5 * grad_clipped
    second_new = 0.5 * second_state + 0.5 * grad_clipped * grad_clipped
    master_new = master_state - RATE * (
        first_new / (jnp.sqrt(second_new) + 1e-08) + DECAY * master_state
    )
    return (master_new, first_new, second_new)


def is_box():
    return (lax.axis_size("fsdp"), lax.axis_size("ctx"), lax.axis_size("tp")) == (8, 2, 2)


def swap_tp(value):
    return lax.ppermute(value, "tp", [(0, 1), (1, 0)])


def swap_y(value):
    return lax.ppermute(value, "ctx", [(0, 1), (1, 0)])


def swap_f(value, bit):
    return lax.ppermute(value, "fsdp", [(place, place ^ bit) for place in range(8)])


def swap_x(value):
    return swap_f(value, 1)


def place_z():
    return lax.axis_index("fsdp") // 2


def low(value):
    return value.astype(jnp.bfloat16)


def wide(value):
    return value.astype(jnp.float32)


def after(value, *earlier):
    return lax.optimization_barrier((value, *earlier))[0]


class Lanes:
    def __init__(self):
        self.done = ()

    def step(self, sends, *earlier):
        values = lax.optimization_barrier(tuple(value for _, value in sends) + self.done + earlier)
        self.done = tuple(swap(value) for (swap, _), value in zip(sends, values))
        return list(self.done)


def move_z(step, sources):
    pairs = [(2 * z + x, 2 * (z + step) + x) for z in sources for x in range(2)]
    return lambda value: lax.ppermute(value, "fsdp", pairs)


def to_z(rel):
    return lambda value: swap_f(value, 2 * rel)


class ZLine:
    def __init__(self, own):
        self.above, self.below = [own], [own]

    def sends(self):
        hop = len(self.above)
        return [
            (move_z(1, range(hop - 1, 3)), self.above[-1]),
            (move_z(-1, range(1, 5 - hop)), self.below[-1]),
        ]

    def take(self, arrived):
        self.above.append(arrived[0])
        self.below.append(arrived[1])

    def block(self, rel):
        z = place_z()
        above, below = self.above, self.below
        if rel == 0:
            return above[0]
        if rel == 1:
            return jnp.where(z % 2 == 1, above[1], below[1])
        if rel == 2:
            return jnp.where(z >= 2, above[2], below[2])
        return jnp.where(
            z == 0, below[3], jnp.where(z == 3, above[3], jnp.where(z == 1, below[1], above[1]))
        )


class ZSum:
    def __init__(self):
        self.last = None
        self.up = self.down = None

    def sends(self, rel, block):
        z = place_z()
        if rel == 3:
            self.last = block
            up, down = block, block
        elif rel == 2:
            up, down = block + self.up, block + self.down
        else:
            up = jnp.where(z == 1, self.last, block) + self.up
            down = jnp.where(z == 2, self.last, block) + self.down
        return [
            (move_z(1, range(0, 4 - rel)), low(up)),
            (move_z(-1, range(rel, 4)), low(down)),
        ]

    def take(self, arrived):
        self.up, self.down = arrived

    def total(self, block):
        return block + self.up + self.down


def early_slots(slots):
    return slots - slots * 13 // 36


def gather_tiles(own, early, place_early, place_late, else_low, targets):
    half = early // 2
    lanes = Lanes()
    line, late_line = ZLine(own[:early]), ZLine(own[early:])
    rest = None
    token = ()
    for rel in range(4):
        block = line.block(rel)
        sends = [(swap_x, block), (swap_y, block)]
        waits = token
        if rel == 2:
            waits += (whole,)
        elif rel == 3:
            waits += rest
        going = line if rel < 3 else late_line
        by_x, by_y, *arrived = lanes.step(sends + going.sends(), *waits)
        going.take(arrived)
        sends = [(swap_y, by_x[:half]), (swap_x, by_y[half:])]
        if rel == 0:
            first, second, *arrived = lanes.step(
                sends + [(to_z(other), else_low.reshape(1, -1, 128)) for other in (1, 2, 3)],
                targets,
            )
            whole = gather_else(else_low, lanes, arrived)
            rest = cut_else(whole)
        elif rel < 3:
            first, second, *arrived = lanes.step(sends + late_line.sends())
            late_line.take(arrived)
        else:
            first, second = lanes.step(sends)
        at = 4 * rel * early
        group = [
            (block, at),
            (by_y, at + early),
            (by_x, at + 2 * early),
            (first, at + 3 * early),
            (second, at + 3 * early + half),
        ]
        token = (place_early(group),)
    line = jnp.concatenate([late_line.block(rel) for rel in range(4)], 0)
    count = line.shape[0]
    half = count // 2
    by_x, by_y = lanes.step([(swap_x, line), (swap_y, line)])
    token = place_late([(line, 0)])
    first, second = lanes.step([(swap_y, by_x[:half]), (swap_x, by_y[half:])], token)
    place_late([(by_y, count), (by_x, 2 * count)])
    place_late([(first, 3 * count), (second, 3 * count + half)])
    return rest


def relative(owner):
    rel_f = jnp.bitwise_xor(owner // 2, lax.axis_index("fsdp"))
    return rel_f // 2, rel_f % 2, jnp.bitwise_xor(owner % 2, lax.axis_index("ctx"))


def early_place(owner, slot, slots):
    rel_z, rel_x, rel_y = relative(owner)
    return ((rel_z * 2 + rel_x) * 2 + rel_y) * slots + slot


def late_place(owner, slot, slots):
    rel_z, rel_x, rel_y = relative(owner)
    return ((rel_x * 2 + rel_y) * 4 + rel_z) * slots + slot


def scatter_late_first(parts, slots, lanes, head_sum, images_part):
    both = parts[12 * slots :]
    arrived = lanes.step(
        [(swap_y, both[: 2 * slots]), (swap_x, both[2 * slots :]), (swap_y, head_sum)]
        + [(to_z(rel), images_part) for rel in (1, 2, 3)]
    )
    return arrived[:2], head_sum + arrived[2], jnp.concatenate([images_part] + arrived[3:], 0)


def scatter_late(parts, slots, lanes, wait, later):
    count = 4 * slots
    half = count // 2
    keep, to_y, to_x, _ = (parts[part * count : (part + 1) * count] for part in range(4))
    (by_y, by_x), head_sum, images = wait
    to_x = jnp.concatenate([low(wide(to_x[:half]) + by_y), to_x[half:]], 0)
    to_y = jnp.concatenate([to_y[:half], low(wide(to_y[half:]) + by_x)], 0)
    from_x, from_y, head_x, images_y = lanes.step(
        [(swap_x, to_x), (swap_y, to_y), (swap_x, head_sum), (swap_y, images)], later
    )
    keep = wide(keep) + from_x + from_y
    return (
        [keep[rel * slots : (rel + 1) * slots] for rel in range(4)],
        head_sum + head_x,
        jnp.concatenate([images, images_y], 0),
    )


def scatter_early(parts, slots, lanes, late, head_sum, early_images, images_part):
    half = slots // 2

    def block(part, begin, end):
        return parts[part * slots + begin : part * slots + end]

    def diagonal(rel):
        return [
            (swap_y, block(4 * rel + 3, 0, half)),
            (swap_x, block(4 * rel + 3, half, slots)),
        ]

    def sides(rel, arrived):
        by_y, by_x = arrived
        return [
            (
                swap_x,
                jnp.concatenate(
                    [
                        low(wide(block(4 * rel + 2, 0, half)) + by_y),
                        block(4 * rel + 2, half, slots),
                    ],
                    0,
                ),
            ),
            (
                swap_y,
                jnp.concatenate(
                    [
                        block(4 * rel + 1, 0, half),
                        low(wide(block(4 * rel + 1, half, slots)) + by_x),
                    ],
                    0,
                ),
            ),
        ]

    def kept(rel, arrived):
        return wide(block(4 * rel, 0, slots)) + arrived[0] + arrived[1]

    line, late_line = ZSum(), ZSum()
    arrived = lanes.step(
        diagonal(3) + late_line.sends(3, late[3]) + [(to_z(1), head_sum), (swap_x, early_images)]
    )
    diagonal_3 = arrived[:2]
    late_line.take(arrived[2:4])
    head_sum = head_sum + arrived[4]
    early_images = jnp.concatenate([early_images, arrived[5]], 0)
    arrived = lanes.step(diagonal(2) + late_line.sends(2, late[2]))
    diagonal_2 = arrived[:2]
    late_line.take(arrived[2:])
    arrived = lanes.step(sides(3, diagonal_3) + late_line.sends(1, late[1]))
    late_line.take(arrived[2:])
    owned_late = late_line.total(late[0])
    kept_3 = kept(3, arrived)
    arrived = lanes.step(
        diagonal(1) + [(to_z(rel), images_part) for rel in (1, 2, 3)] + [(to_z(2), head_sum)]
    )
    diagonal_1 = arrived[:2]
    images = jnp.concatenate([images_part] + arrived[2:5], 0)
    head_sum = head_sum + arrived[5]
    arrived = lanes.step(sides(2, diagonal_2) + line.sends(3, kept_3) + [(swap_y, images)])
    line.take(arrived[2:4])
    kept_2 = kept(2, arrived)
    images = jnp.concatenate([images, arrived[4]], 0)
    arrived = lanes.step(diagonal(0) + [(swap_x, images)])
    diagonal_0 = arrived[:2]
    images = jnp.concatenate([images, arrived[2]], 0)
    arrived = lanes.step(sides(1, diagonal_1) + line.sends(2, kept_2))
    line.take(arrived[2:4])
    arrived_0 = lanes.step(sides(0, diagonal_0) + line.sends(1, kept(1, arrived)))
    line.take(arrived_0[2:4])
    return line.total(kept(0, arrived_0)), owned_late, images, head_sum, early_images


def gather_images(value):
    if not is_box():
        return lax.all_gather(value, ("fsdp", "ctx"), axis=0, tiled=True)
    value = jnp.concatenate([value] + [swap_f(value, 2 * rel) for rel in (1, 2, 3)], 0)
    by_x, by_y = swap_x(value), swap_y(value)
    return jnp.concatenate([value, by_y, by_x, swap_x(by_y)], 0)


def gather_else(flat, lanes, line):
    if not is_box():
        return lax.all_gather(flat, ("fsdp", "ctx", "tp"), axis=0, tiled=True)
    z, x = place_z(), lax.axis_index("fsdp") % 2
    y, core = lax.axis_index("ctx"), lax.axis_index("tp")
    own = flat.reshape(1, -1, 128)
    line = [own] + line
    line = [
        jnp.where(
            z == place,
            line[0],
            jnp.where(z == place ^ 1, line[1], jnp.where(z == place ^ 2, line[2], line[3])),
        )
        for place in range(4)
    ]
    line = jnp.concatenate(line, 0)
    by_x, by_y = lanes.step([(swap_x, line), (swap_y, line)])
    half = line.shape[1] // 2
    both = jnp.concatenate(lanes.step([(swap_y, by_x[:, :half]), (swap_x, by_y[:, half:])]), 1)
    y_low = [jnp.where(y == 0, line, by_y), jnp.where(y == 0, by_x, both)]
    y_high = [jnp.where(y == 0, by_y, line), jnp.where(y == 0, both, by_x)]
    chip = jnp.stack(
        [
            jnp.stack([jnp.where(x == 0, y_low[0], y_low[1]), jnp.where(x == 0, y_high[0], y_high[1])], 1),
            jnp.stack([jnp.where(x == 0, y_low[1], y_low[0]), jnp.where(x == 0, y_high[1], y_high[0])], 1),
        ],
        1,
    )
    other = swap_tp(chip)
    return jnp.stack(
        [jnp.where(core == 0, chip, other), jnp.where(core == 0, other, chip)], 3
    )


def cut_else(flat):
    rows = flat.reshape(-1, D)
    counts = [P_SIZE, NCLS, TFREQ, D, 2 * D, P_SIZE]
    ends = [sum(counts[: place + 1]) for place in range(6)]
    parts = [rows[end - count : end] for end, count in zip(ends, counts)]
    parts[4] = parts[4].reshape(D, 2 * D)
    parts[5] = parts[5].reshape(D, P_SIZE)
    return tuple(parts)


def total(value):
    if not is_box():
        return lax.psum(value, ("fsdp", "ctx", "tp"))
    value = value + swap_tp(value)
    value = value + swap_y(value)
    for bit in (1, 2, 4):
        value = value + swap_f(value, bit)
    return value


def tp_sum(value):
    if lax.axis_size("tp") == 2:
        return value + swap_tp(value)
    return lax.psum(value, "tp")


def columns_in(value):
    if lax.axis_size("tp") == 2:
        other = swap_tp(value)
        at_zero = lax.axis_index("tp") == 0
        return jnp.concatenate(
            [jnp.where(at_zero, value, other), jnp.where(at_zero, other, value)], -1
        )
    return lax.all_gather(value, "tp", axis=value.ndim - 1, tiled=True)


def rows_in(value_low):
    if lax.axis_size("tp") == 2:
        return [value_low, swap_tp(value_low)]
    return [lax.all_gather(value_low, "tp", axis=0, tiled=True)]


def each_half(work, row_sets):
    if len(row_sets) == 2:
        other = work(row_sets[1])
        sent = swap_tp(other[-1])
        own = work(row_sets[0])
        return [own[:-1], other[:-1]], [own[-1], sent]
    whole = work(row_sets[0])
    return [whole[:-1]], [lax.psum_scatter(whole[-1], "tp", scatter_dimension=0, tiled=True)]


BIG = 56 * 1024 * 1024


def against_value(left_op, right_op):
    return lax.dot_general(
        left_op, right_op, (((1,), (1,)), ((), ())), preferred_element_type=jnp.float32
    )


def untile_into(matrix, tile_set):
    rows, columns = matrix.shape[0] // B, matrix.shape[1] // B
    for row in range(rows):
        for column in range(columns):
            matrix[row * B : (row + 1) * B, column * B : (column + 1) * B] = tile_set[
                row * columns + column
            ]


def segments(tp_parts):
    found = []
    begin = 0
    for height, breadth in shard_shapes(tp_parts):
        amount = height * breadth // (B * B)
        found.append((amount, begin))
        begin += amount
    return found


def weight_spec(kind, tp_parts):
    amount, begin = segments(tp_parts)[kind]
    return pl.BlockSpec(
        (amount, B, B), lambda *step: (begin // amount, 0, 0), pipeline_mode=pl.Buffered(1)
    )


def rows_spec(rows, breadth):
    return pl.BlockSpec((rows, breadth), lambda step: (step, 0))


def shaped(rows, breadth, kind):
    return jax.ShapeDtypeStruct((rows, breadth), kind)


def params():
    return pltpu.CompilerParams(vmem_limit_bytes=BIG)


def attend_kernel(normed_in, qkv_tiles, proj_tiles, projected, attended, partial, w_qkv, w_proj):
    @pl.when(pl.program_id(0) == 0)
    def _():
        untile_into(w_qkv, qkv_tiles)
        untile_into(w_proj, proj_tiles)

    values = low(product(normed_in[...], w_qkv[...]))
    projected[...] = values
    width = values.shape[1] // 3
    results = []
    for head in range(width // HD):
        at = head * HD
        query = values[:, at : at + HD]
        key_rows = values[:, width + at : width + at + HD]
        value_rows = values[:, 2 * width + at : 2 * width + at + HD]
        scores = against_value(key_rows, query) * HD ** (-0.5)
        exponent = jnp.exp(scores - jnp.max(scores, 0, keepdims=True))
        probabilities = low(exponent / jnp.sum(exponent, 0, keepdims=True))
        results.append(low(over_rows(probabilities, value_rows)))
    result = jnp.concatenate(results, 1)
    attended[...] = result
    partial[...] = product(result, w_proj[...])


def attend_call(normed_in, store, tp_parts, local_len):
    rows = normed_in.shape[0]
    width = D // tp_parts
    return pl.pallas_call(
        attend_kernel,
        grid=(rows // local_len,),
        in_specs=[
            rows_spec(local_len, D),
            weight_spec(0, tp_parts),
            weight_spec(1, tp_parts),
        ],
        out_specs=[
            rows_spec(local_len, 3 * width),
            rows_spec(local_len, width),
            rows_spec(local_len, D),
        ],
        out_shape=[
            shaped(rows, 3 * width, jnp.bfloat16),
            shaped(rows, width, jnp.bfloat16),
            shaped(rows, D, jnp.float32),
        ],
        scratch_shapes=[
            pltpu.VMEM((D, 3 * width), jnp.bfloat16),
            pltpu.VMEM((width, D), jnp.bfloat16),
        ],
        compiler_params=params(),
        cost_estimate=pl.CostEstimate(
            flops=rows * D * width * 8, bytes_accessed=rows * D * 8, transcendentals=rows * 2048
        ),
    )(normed_in, store, store)


def attend_back_kernel(
    grad_branch, projected, qkv_tiles, proj_tiles, grad_qkv, partial, w_qkv, w_proj
):
    @pl.when(pl.program_id(0) == 0)
    def _():
        untile_into(w_qkv, qkv_tiles)
        untile_into(w_proj, proj_tiles)

    grad_attended = low(against_value(grad_branch[...], w_proj[...]))
    values = projected[...]
    width = values.shape[1] // 3
    grads = [[], [], []]
    for head in range(width // HD):
        at = head * HD
        query = values[:, at : at + HD]
        key_rows = values[:, width + at : width + at + HD]
        value_rows = values[:, 2 * width + at : 2 * width + at + HD]
        grad_here = grad_attended[:, at : at + HD]
        scores = against_value(key_rows, query) * HD ** (-0.5)
        exponent = jnp.exp(scores - jnp.max(scores, 0, keepdims=True))
        probabilities = exponent / jnp.sum(exponent, 0, keepdims=True)
        grad_prob = against_value(value_rows, grad_here)
        grad_scores = low(
            probabilities
            * (grad_prob - jnp.sum(probabilities * grad_prob, 0, keepdims=True))
        )
        grads[0].append(low(over_rows(grad_scores, key_rows) * HD ** (-0.5)))
        grads[1].append(low(product(grad_scores, query) * HD ** (-0.5)))
        grads[2].append(low(product(low(probabilities), grad_here)))
    result = jnp.concatenate(grads[0] + grads[1] + grads[2], 1)
    grad_qkv[...] = result
    partial[...] = against_value(result, w_qkv[...])


def attend_back_call(grad_branch, projected, store, tp_parts, local_len):
    rows = grad_branch.shape[0]
    width = D // tp_parts
    return pl.pallas_call(
        attend_back_kernel,
        grid=(rows // local_len,),
        in_specs=[
            rows_spec(local_len, D),
            rows_spec(local_len, 3 * width),
            weight_spec(0, tp_parts),
            weight_spec(1, tp_parts),
        ],
        out_specs=[rows_spec(local_len, 3 * width), rows_spec(local_len, D)],
        out_shape=[shaped(rows, 3 * width, jnp.bfloat16), shaped(rows, D, jnp.float32)],
        scratch_shapes=[
            pltpu.VMEM((D, 3 * width), jnp.bfloat16),
            pltpu.VMEM((width, D), jnp.bfloat16),
        ],
        compiler_params=params(),
        cost_estimate=pl.CostEstimate(
            flops=rows * D * width * 10, bytes_accessed=rows * D * 8, transcendentals=rows * 2048
        ),
    )(grad_branch, projected, store, store)


def mlp_chunk(tp_parts):
    return min(4 * B, F // tp_parts)


def chunk_specs(tp_parts):
    amount = D * mlp_chunk(tp_parts) // (B * B)
    up, down = (segments(tp_parts)[kind][1] // amount for kind in (2, 3))
    return [
        pl.BlockSpec((amount, B, B), lambda step: (up + step, 0, 0)),
        pl.BlockSpec((amount, B, B), lambda step: (down + step, 0, 0)),
    ]


def store_of_tile(tile, tp_parts):
    amount, begin = segments(tp_parts)[2]
    within = tile % sum(count for count, _ in segments(tp_parts)) - begin
    columns, wide_step = F // tp_parts // B, mlp_chunk(tp_parts) // B
    row, column = within // columns, within % columns
    moved = (column // wide_step * (D // B) + row) * wide_step + column % wide_step
    return jnp.where((within >= 0) & (within < amount), tile + moved - within, tile)


def add_to(total_ref, value):
    @pl.when(pl.program_id(0) == 0)
    def _():
        total_ref[...] = value

    @pl.when(pl.program_id(0) > 0)
    def _():
        total_ref[...] += value


def mlp_kernel(normed_mid, up_tiles, down_tiles, hidden, partial, w_up, w_down):
    untile_into(w_up, up_tiles)
    untile_into(w_down, down_tiles)
    values = product(normed_mid[...], w_up[...])
    hidden[...] = values
    add_to(partial, product(low(gelu_tanh(values)), w_down[...]))


def chunk_scratch(tp_parts):
    width = mlp_chunk(tp_parts)
    return [pltpu.VMEM((D, width), jnp.bfloat16), pltpu.VMEM((width, D), jnp.bfloat16)]


def all_rows(rows):
    return pl.BlockSpec((rows, D), lambda step: (0, 0))


def mlp_call(normed_mid, store, tp_parts, local_len):
    rows = normed_mid.shape[0]
    width, step_width = F // tp_parts, mlp_chunk(tp_parts)
    step_spec = pl.BlockSpec((rows, step_width), lambda step: (0, step))
    return pl.pallas_call(
        mlp_kernel,
        grid=(width // step_width,),
        in_specs=[all_rows(rows)] + chunk_specs(tp_parts),
        out_specs=[step_spec, all_rows(rows)],
        out_shape=[shaped(rows, width, jnp.float32), shaped(rows, D, jnp.float32)],
        scratch_shapes=chunk_scratch(tp_parts),
        compiler_params=params(),
        cost_estimate=pl.CostEstimate(
            flops=rows * D * width * 4,
            bytes_accessed=rows * D * 12 + 4 * D * width,
            transcendentals=rows * width,
        ),
    )(normed_mid, store, store)


def mlp_back_kernel(
    grad_mlp, hidden, up_tiles, down_tiles, activation, grad_hidden, partial, w_up, w_down
):
    untile_into(w_up, up_tiles)
    untile_into(w_down, down_tiles)
    values = hidden[...]
    factor = math.sqrt(2.0 / math.pi)
    square = values * values
    bent = jnp.tanh(factor * (values + 0.044715 * (square * values)))
    half_up = 0.5 * (1.0 + bent)
    activation[...] = low(values * half_up)
    slope = half_up + 0.5 * values * (1.0 - bent * bent) * (
        factor * (1.0 + 3.0 * 0.044715 * square)
    )
    grad = low(against_value(grad_mlp[...], w_down[...]) * slope)
    grad_hidden[...] = grad
    add_to(partial, against_value(grad, w_up[...]))


def mlp_back_call(grad_mlp, hidden, store, tp_parts, local_len):
    rows = grad_mlp.shape[0]
    width, step_width = F // tp_parts, mlp_chunk(tp_parts)
    step_spec = pl.BlockSpec((rows, step_width), lambda step: (0, step))
    return pl.pallas_call(
        mlp_back_kernel,
        grid=(width // step_width,),
        in_specs=[all_rows(rows), step_spec] + chunk_specs(tp_parts),
        out_specs=[step_spec, step_spec, all_rows(rows)],
        out_shape=[
            shaped(rows, width, jnp.bfloat16),
            shaped(rows, width, jnp.bfloat16),
            shaped(rows, D, jnp.float32),
        ],
        scratch_shapes=chunk_scratch(tp_parts),
        compiler_params=params(),
        cost_estimate=pl.CostEstimate(
            flops=rows * D * width * 4,
            bytes_accessed=rows * D * 16 + 4 * D * width,
            transcendentals=rows * width,
        ),
    )(grad_mlp, hidden, store, store)


def modes_call(cond_act, store, tp_parts):
    rows = cond_act.shape[0]
    width = 6 * D // tp_parts

    def kernel(left, tile_set, out):
        for column in range(width // B):
            total_here = 0.0
            for row in range(D // B):
                total_here = total_here + product(
                    left[:, row * B : (row + 1) * B], tile_set[row * (width // B) + column]
                )
            out[:, column * B : (column + 1) * B] = total_here

    return pl.pallas_call(
        kernel,
        grid=(1,),
        in_specs=[rows_spec(rows, D), weight_spec(4, tp_parts)],
        out_specs=rows_spec(rows, width),
        out_shape=shaped(rows, width, jnp.float32),
        compiler_params=params(),
    )(cond_act, store)


def three_parts(value):
    first = low(value)
    rest = value - wide(first)
    second = low(rest)
    return jnp.concatenate([first, second, low(rest - wide(second))], 0)


def against_low(value, weight):
    rows = value.shape[0]
    summed = against(three_parts(value), weight)
    return summed[:rows] + summed[rows : 2 * rows] + summed[2 * rows :]


def modes_back_call(grads, store, tp_parts):
    rows = grads.shape[0]
    width = 6 * D // tp_parts
    parts = three_parts(grads)

    def kernel(left, tile_set, out):
        for row in range(D // B):
            total_here = 0.0
            for column in range(width // B):
                total_here = total_here + against_value(
                    left[:, column * B : (column + 1) * B],
                    tile_set[row * (width // B) + column],
                )
            out[:, row * B : (row + 1) * B] = total_here

    summed = pl.pallas_call(
        kernel,
        grid=(1,),
        in_specs=[rows_spec(3 * rows, width), weight_spec(4, tp_parts)],
        out_specs=rows_spec(3 * rows, D),
        out_shape=shaped(3 * rows, D, jnp.float32),
        compiler_params=params(),
    )(parts, store)
    return summed[:rows] + summed[rows : 2 * rows] + summed[2 * rows :]


def weight_grad_call(lefts, rights, places, first_tile, held):
    height, breadth = lefts[0].shape[1], rights[0].shape[1]
    steps = min(4, height // B)
    count = len(lefts)
    row_tiles, column_tiles = height // B // steps, breadth // B
    amount = row_tiles * column_tiles
    given = [array for _, _, array in held if array is not None]

    def kernel(place, *refs):
        left_refs, right_refs = refs[:count], refs[count : 2 * count]
        outs = refs[2 * count + len(given) : 2 * count + len(given) + len(held)]
        ready, sem = refs[-2], refs[-1]
        step = pl.program_id(0)
        slot = lax.rem(step, 2)

        def drain(which):
            pltpu.make_async_copy(
                ready.at[which], outs[0].at[pl.ds(0, amount)], sem.at[which]
            ).wait()

        @pl.when(step >= 2)
        def _():
            drain(slot)

        block = over_rows(left_refs[0][...], right_refs[0][...])
        for left, right in zip(left_refs[1:], right_refs[1:]):
            block = block + over_rows(left[...], right[...])
        block = low(block)
        for row in range(row_tiles):
            for column in range(column_tiles):
                ready[slot, row * column_tiles + column] = block[
                    row * B : (row + 1) * B, column * B : (column + 1) * B
                ]

        def send(index, carry):
            where_to = place[first_tile + step * amount + index]
            for number, (begin, _, _) in enumerate(held):
                end = held[number + 1][0] if number + 1 < len(held) else 1 << 30
                copy = pltpu.make_async_copy(
                    ready.at[slot, index], outs[number].at[where_to - begin], sem.at[slot]
                )
                if len(held) == 1:
                    copy.start()
                else:
                    pl.when((where_to >= begin) & (where_to < end))(copy.start)
            return carry

        lax.fori_loop(0, amount, send, 0)

        @pl.when(step == steps - 1)
        def _():
            drain(slot)
            if steps > 1:
                drain(1 - slot)

    rows = [left.shape[0] for left in lefts]
    anywhere = pl.BlockSpec(memory_space=pl.ANY)
    in_specs = [
        pl.BlockSpec((size, height // steps), lambda step, place: (0, step)) for size in rows
    ] + [
        pl.BlockSpec((size, breadth), lambda step, place: (0, 0), pipeline_mode=pl.Buffered(1))
        for size in rows
    ]
    in_specs += [anywhere] * len(given)
    operands = [places, *lefts, *rights, *given]
    aliases = {}
    for number, (_, _, array) in enumerate(held):
        if array is not None:
            aliases[1 + 2 * count + len(aliases)] = number
    results = pl.pallas_call(
        kernel,
        grid_spec=pltpu.PrefetchScalarGridSpec(
            num_scalar_prefetch=1,
            grid=(steps,),
            in_specs=in_specs,
            out_specs=[anywhere] * len(held),
            scratch_shapes=[
                pltpu.VMEM((2, amount, B, B), jnp.bfloat16),
                pltpu.SemaphoreType.DMA((2,)),
            ],
        ),
        out_shape=[
            jax.ShapeDtypeStruct((places_here, B, B), jnp.bfloat16) for _, places_here, _ in held
        ],
        input_output_aliases=aliases,
        compiler_params=params(),
        cost_estimate=pl.CostEstimate(
            flops=2 * sum(rows) * height * breadth,
            bytes_accessed=2 * (sum(rows) * (height + breadth) + height * breadth),
            transcendentals=0,
        ),
    )(*operands)
    return [
        (begin, places_here, array) for (begin, places_here, _), array in zip(held, results)
    ]


def place_call(pieces, targets, held):
    count = len(pieces)
    given = [array for _, _, array in held if array is not None]

    def kernel(target, *refs):
        outs = refs[count + len(given) : count + len(given) + len(held)]
        token = refs[count + len(given) + len(held)]
        buffers, loaded, stored = refs[-2 - count : -2], refs[-2], refs[-1]
        token[...] = jnp.zeros_like(token)
        for number in range(count):
            pltpu.make_async_copy(refs[number], buffers[number], loaded.at[number]).start()
        for number, (piece, begin) in enumerate(pieces):
            pltpu.make_async_copy(refs[number], buffers[number], loaded.at[number]).wait()

            def send(index, carry):
                where_to = target[begin + index]
                left = True
                for out_number, (first, amount, _) in enumerate(held):
                    last = out_number == len(held) - 1
                    inside = (where_to >= first) & (where_to < first + amount - 1)
                    at = where_to - first
                    if last:
                        at = jnp.where(inside, at, amount - 1)
                        inside = left
                    else:
                        left = jnp.logical_not(inside)
                    copy = pltpu.make_async_copy(
                        buffers[number].at[index], outs[out_number].at[at], stored.at[number]
                    )
                    if len(held) == 1:
                        copy.start()
                    else:
                        pl.when(inside)(copy.start)
                return carry

            lax.fori_loop(0, piece.shape[0], send, 0)
        for number, (piece, begin) in enumerate(pieces):
            pltpu.make_async_copy(
                buffers[number], outs[0].at[pl.ds(0, piece.shape[0])], stored.at[number]
            ).wait()

    anywhere = pl.BlockSpec(memory_space=pl.ANY)
    operands = [targets] + [piece for piece, _ in pieces] + given
    aliases = {}
    for number, (_, _, array) in enumerate(held):
        if array is not None:
            aliases[1 + count + len(aliases)] = number
    results = pl.pallas_call(
        kernel,
        grid_spec=pltpu.PrefetchScalarGridSpec(
            num_scalar_prefetch=1,
            grid=(1,),
            in_specs=[anywhere] * (len(operands) - 1),
            out_specs=[anywhere] * len(held) + [pl.BlockSpec((8, B), lambda step, target: (0, 0))],
            scratch_shapes=[pltpu.VMEM(piece.shape, jnp.bfloat16) for piece, _ in pieces]
            + [pltpu.SemaphoreType.DMA((count,))] * 2,
        ),
        out_shape=[jax.ShapeDtypeStruct((amount, B, B), jnp.bfloat16) for _, amount, _ in held]
        + [jax.ShapeDtypeStruct((8, B), jnp.float32)],
        input_output_aliases=aliases,
        compiler_params=params(),
        cost_estimate=pl.CostEstimate(
            flops=0,
            bytes_accessed=sum(4 * piece.shape[0] * B * B for piece, _ in pieces),
            transcendentals=0,
        ),
    )(*operands)
    return [(first, amount, array) for (first, amount, _), array in zip(held, results)], results[-1]


def chips_sum(value):
    for swap in (swap_y, swap_x, lambda part: swap_f(part, 2), lambda part: swap_f(part, 4)):
        value = value + swap(value)
    return value


LOT = 16


def lots(count):
    return (count + LOT - 1) // LOT


def bring_strays(store, strays, count, owned_tiles, ordering, slots, me, tp_parts):
    def body(state):
        lot, held = state
        tiles = lax.dynamic_slice_in_dim(strays, lot * LOT, LOT, 0)
        valid = lot * LOT + jnp.arange(LOT) < count
        here = ordering[tiles]
        mine = valid & (here // slots == me)
        sent = jnp.where(mine[:, None, None], owned_tiles[here % slots], 0)
        sent = chips_sum(sent)
        at = jnp.where(valid, store_of_tile(tiles, tp_parts), held.shape[0])
        return lot + 1, held.at[at].set(sent, mode="drop")

    return lax.while_loop(lambda state: state[0] < lots(count), body, (0, store))[1]


def sum_strays(owned, parts, strays, count, ordering, slots, me):
    def body(state):
        lot, held = state
        tiles = lax.dynamic_slice_in_dim(strays, lot * LOT, LOT, 0)
        valid = lot * LOT + jnp.arange(LOT) < count
        summed = chips_sum(wide(lax.dynamic_slice_in_dim(parts, lot * LOT, LOT, 0)))
        here = ordering[tiles]
        at = jnp.where(valid & (here // slots == me), here % slots, slots)
        return lot + 1, held.at[at].set(summed, mode="drop")

    return lax.while_loop(lambda state: state[0] < lots(count), body, (0, owned))[1]


def normed_value(stream):
    centred = stream - jnp.mean(stream, -1, keepdims=True)
    rate = lax.rsqrt(jnp.mean(centred * centred, -1, keepdims=True) + EPS_NORM)
    return centred * rate, rate


def rows_kernel_call(kernel, wide_ins, mode_ins, outs):
    own, group = wide_ins[0].shape[:2]
    rows = pl.BlockSpec((1, group, D), lambda step: (step, 0, 0))
    few = lambda count: pl.BlockSpec((1, count, D), lambda step: (step, 0, 0))
    return pl.pallas_call(
        kernel,
        grid=(own,),
        in_specs=[rows] * len(wide_ins) + [few(modes.shape[1]) for modes in mode_ins],
        out_specs=[rows if count is None else few(count) for count, _ in outs],
        out_shape=[
            jax.ShapeDtypeStruct((own, group if count is None else count, D), kind)
            for count, kind in outs
        ],
        compiler_params=params(),
        cost_estimate=pl.CostEstimate(
            flops=own * group * D * 20,
            bytes_accessed=own * group * D * 4 * (len(wide_ins) + len(outs)),
            transcendentals=own * group,
        ),
    )(*wide_ins, *mode_ins)


def modulate_call(stream, modes, shift, scale):
    def kernel(values, mode, out):
        out[0] = low(
            normed_value(values[0])[0] * (1.0 + mode[0, scale : scale + 1, :])
            + mode[0, shift : shift + 1, :]
        )

    return rows_kernel_call(kernel, [stream], [modes], [(None, jnp.bfloat16)])[0]


def residual_call(stream, terms, modes, gate, next_modes, shift, scale):
    def kernel(*refs):
        values, term_refs = refs[0], refs[1 : 1 + len(terms)]
        mode, mode_next, branch, stream_new, out = refs[1 + len(terms) :]
        summed = term_refs[0][0]
        for term in term_refs[1:]:
            summed = summed + term[0]
        branch[0] = summed
        result = values[0] + mode[0, gate : gate + 1, :] * summed
        stream_new[0] = result
        out[0] = low(
            normed_value(result)[0] * (1.0 + mode_next[0, scale : scale + 1, :])
            + mode_next[0, shift : shift + 1, :]
        )

    shape = stream.shape
    return rows_kernel_call(
        kernel,
        [stream] + [term.reshape(shape) for term in terms],
        [modes, next_modes],
        [(None, jnp.float32), (None, jnp.float32), (None, jnp.bfloat16)],
    )


def back_call(stream, terms, upstream, modes, scale, below):
    shape = stream.shape
    wide_ins = [stream] + [term.reshape(shape) for term in terms]
    if upstream is not None:
        wide_ins.append(upstream)
    mode_ins = [modes]
    outs = [(None, jnp.float32), (3 if below else 2, jnp.float32)]
    if below:
        branch, branch_modes, gate = below
        wide_ins.append(branch)
        mode_ins.append(branch_modes)
        outs.append((None, jnp.bfloat16))

    def kernel(*refs):
        ins, modes_in = refs[: len(wide_ins)], refs[len(wide_ins) : len(wide_ins) + len(mode_ins)]
        results = refs[len(wide_ins) + len(mode_ins) :]
        grad = ins[1][0]
        for term in ins[2 : 1 + len(terms)]:
            grad = grad + term[0]
        normal, rate = normed_value(ins[0][0])
        results[1][0, 0:1, :] = jnp.sum(grad, 0, keepdims=True)
        results[1][0, 1:2, :] = jnp.sum(grad * normal, 0, keepdims=True)
        grad = grad * (1.0 + modes_in[0][0, scale : scale + 1, :])
        grad = rate * (
            grad
            - jnp.mean(grad, -1, keepdims=True)
            - normal * jnp.mean(grad * normal, -1, keepdims=True)
        )
        if upstream is not None:
            grad = grad + ins[1 + len(terms)][0]
        results[0][0] = grad
        if below:
            results[1][0, 2:3, :] = jnp.sum(grad * ins[-1][0], 0, keepdims=True)
            results[2][0] = low(modes_in[1][0, gate : gate + 1, :] * grad)

    return rows_kernel_call(kernel, wide_ins, mode_ins, outs)


def update_kernel(clip, grad, master, first, second, bases, master_out, first_out, second_out, low_out):
    eye = lax.broadcasted_iota(jnp.int32, (B, B), 0) == lax.broadcasted_iota(jnp.int32, (B, B), 1)
    left_row = bases[:, 0:1, :]
    right_row = bases[:, 1:2, :]
    left_col = jnp.sum(jnp.where(eye[None], left_row, 0.0), 2, keepdims=True)
    left_scaled = left_col * (2.0 / jnp.sum(left_row * left_row, 2, keepdims=True))
    right_scaled = right_row * (2.0 / jnp.sum(right_row * right_row, 2, keepdims=True))

    def turn(middle):
        middle = middle - left_scaled * jnp.sum(left_col * middle, 1, keepdims=True)
        return middle - jnp.sum(middle * right_row, 2, keepdims=True) * right_scaled

    turned = turn(clip[0, 0] * grad[...])
    first_new = 0.5 * first[...] + 0.5 * turned
    second_new = 0.5 * second[...] + 0.5 * turned * turned
    first_out[...] = first_new
    second_out[...] = second_new
    master_new = master[...] - RATE * turn(first_new / (jnp.sqrt(second_new) + 1e-08))
    master_out[...] = master_new
    low_out[...] = master_new.astype(jnp.bfloat16)


def update_tiles(clip_factor, grad, master, first, second, bases):
    slots = grad.shape[0]
    amount = max(count for count in (1, 2, 3, 4, 6, 8) if slots % count == 0)
    tile_spec = pl.BlockSpec((amount, B, B), lambda step: (step, 0, 0))
    whole = jax.ShapeDtypeStruct(grad.shape, jnp.float32)
    return pl.pallas_call(
        update_kernel,
        grid=(slots // amount,),
        in_specs=[pl.BlockSpec(memory_space=pltpu.SMEM)]
        + [tile_spec] * 4
        + [pl.BlockSpec((amount, 2, B), lambda step: (step, 0, 0))],
        out_specs=[tile_spec] * 4,
        out_shape=[whole, whole, whole, jax.ShapeDtypeStruct(grad.shape, jnp.bfloat16)],
        compiler_params=params(),
        cost_estimate=pl.CostEstimate(
            flops=slots * B * B * 30, bytes_accessed=slots * B * B * 30, transcendentals=slots * B * B
        ),
    )(clip_factor.reshape(1, 1), grad, master, first, second, bases)


def on_device(
    latents,
    noise,
    timesteps,
    labels,
    owners,
    tiles_low,
    tiles_master,
    tiles_first,
    tiles_second,
    bases,
    else_low,
    else_master,
    else_first,
    else_second,
):
    box = is_box()
    tp_parts = lax.axis_size("tp")
    tp_index = lax.axis_index("tp")
    ctx_parts = lax.axis_size("ctx")
    fsdp_parts = lax.axis_size("fsdp")
    images = latents.shape[0]
    local_len = latents.shape[1]
    slots = tiles_low.shape[1]
    sp_rows = images * local_len // tp_parts
    first_row = tp_index * sp_rows
    own = max(1, sp_rows // local_len)
    group = sp_rows // own
    first_image = first_row // local_len
    element_count = images * fsdp_parts * ctx_parts * local_len * P_SIZE
    ordering = jnp.argsort(owners, stable=True)
    inverse = jnp.argsort(ordering)
    all_tiles = inverse.shape[0]
    per_layer = all_tiles // L
    if box:
        early = early_slots(slots)
        me = lax.axis_index("fsdp") * ctx_parts + lax.axis_index("ctx")
        tile = jnp.arange(all_tiles, dtype=jnp.int32)
        owner, slot = inverse // slots, inverse % slots
        is_early = slot < early
        place_early = early_place(owner, slot, early)
        place_late = late_place(owner, slot - early, slots - early)
        gather_places = jnp.where(is_early, place_early, 16 * early + place_late)
        targets = store_of_tile(jnp.argsort(gather_places), tp_parts).astype(jnp.int32)
        is_stray = jnp.logical_not(is_early) & (tile < per_layer)
        stray_count = jnp.sum(is_stray.astype(jnp.int32))
        stray_rank = jnp.cumsum(is_stray.astype(jnp.int32)) - 1
        room = 16 * (slots - early)
        strays = jnp.argsort(jnp.where(is_stray, tile, all_tiles + tile)).astype(jnp.int32)
        strays = jnp.concatenate([strays, jnp.zeros((LOT,), jnp.int32)])
        places = jnp.where(
            is_stray,
            room + 16 * (early + 1) + stray_rank,
            jnp.where(is_early, room + early_place(owner, slot, early + 1), place_late),
        ).astype(jnp.int32)
        stores = [(0, per_layer + 1, None), (per_layer, per_layer + 1, None)]
        late_store = None

        def place_early_tiles(tile_group):
            nonlocal stores
            stores, token = place_call(tile_group, targets, stores)
            return token

        def place_late_tiles(tile_group):
            nonlocal late_store
            tile_group = [(piece, 16 * early + at) for piece, at in tile_group]
            if late_store is None:
                late_store = [stores[1]]
            late_store, token = place_call(tile_group, targets, late_store)
            return token

        late_store = None
        else_parts = gather_tiles(
            tiles_low[0], early, place_early_tiles, place_late_tiles, else_low, targets
        )
        store = [
            bring_strays(
                stores[0][2], strays, stray_count, tiles_low[0], inverse, slots, me, tp_parts
            ),
            late_store[0][2],
        ]
        held = [(0, room, None), (room, 16 * (slots + 1) + LOT, None)]
    else:
        places = jnp.arange(all_tiles, dtype=jnp.int32)
        tile_stored = jnp.argsort(store_of_tile(places, tp_parts))
        gathered = lax.all_gather(tiles_low, ("fsdp", "ctx"), axis=1, tiled=True)[0]
        gathered = gathered[inverse[tile_stored]]
        store = [gathered[:per_layer], gathered[per_layer:]]
        held = [(0, all_tiles, None)]
        else_parts = cut_else(gather_else(else_low, None, None))
    patch_weight, class_table, time_first, time_second, final_weight, head_weight = else_parts
    features_low = low(time_features(timesteps))
    onehot = low(labels[:, None] == jnp.arange(NCLS)[None, :])
    time_hidden = product(features_low, time_first)
    time_act = low(jax.nn.silu(time_hidden))
    condition = product(time_act, time_second) + product(onehot, class_table)
    cond_act = low(jax.nn.silu(condition))
    modes = [
        lax.dynamic_slice_in_dim(
            columns_in(modes_call(cond_act, store[layer_no], tp_parts)), first_image, own, 0
        ).reshape(own, 6, D)
        for layer_no in range(L)
    ]
    final_modes = lax.dynamic_slice_in_dim(
        product(cond_act, final_weight), first_image, own, 0
    ).reshape(own, 2, D)
    row_index = first_row + jnp.arange(sp_rows)
    signal = signal_level(timesteps)
    noisy_input = (
        jnp.sqrt(signal)[:, None, None] * latents + jnp.sqrt(1.0 - signal)[:, None, None] * noise
    )
    noisy_rows = low(
        lax.dynamic_slice_in_dim(
            noisy_input.reshape(images * local_len, P_SIZE), first_row, sp_rows, 0
        )
    )
    target = lax.dynamic_slice_in_dim(
        noise.reshape(images * local_len, P_SIZE), first_row, sp_rows, 0
    )
    stream = (product(noisy_rows, patch_weight) + position_table(row_index % local_len)).reshape(
        own, group, D
    )
    normed_in = modulate_call(stream, modes[0], 0, 1)
    kept = []
    for layer_no in range(L):
        row_sets = rows_in(normed_in.reshape(sp_rows, D))
        halves, terms = each_half(
            lambda rows: attend_call(rows, store[layer_no], tp_parts, local_len), row_sets
        )
        branch, middle, normed_mid = residual_call(
            stream, terms, modes[layer_no], 2, modes[layer_no], 3, 4
        )
        mid_sets = rows_in(normed_mid.reshape(sp_rows, D))
        hidden, terms = each_half(
            lambda rows: mlp_call(rows, store[layer_no], tp_parts, local_len), mid_sets
        )
        last = layer_no == L - 1
        mlp_out, stream_new, normed_in = residual_call(
            middle,
            terms,
            modes[layer_no],
            5,
            final_modes if last else modes[layer_no + 1],
            0,
            1,
        )
        kept.append((stream, row_sets, halves, branch, middle, mid_sets, hidden, mlp_out))
        stream = stream_new
    head_low = normed_in.reshape(sp_rows, D)
    mismatch = product(head_low, head_weight) - target
    loss_part = jnp.sum(mismatch * mismatch) / element_count
    grad_pred = low(2.0 * mismatch / element_count)
    grad_head = over_rows(grad_pred, head_low)
    upstream, final_sums, grad_low = back_call(
        stream,
        [against(grad_pred, head_weight)],
        None,
        final_modes,
        1,
        (kept[-1][7], modes[-1], 5),
    )
    grad_final = final_sums[:, :2].reshape(own, 2 * D)
    gate_sum = final_sums[:, 2:]
    starts = [begin for _, begin in segments(tp_parts)]
    mode_width = 6 * D // tp_parts
    fill = (-3 * images) % 16
    conds = jnp.pad(jnp.concatenate([cond_act] * 3, 0), ((0, fill), (0, 0)))

    def all_images(values):
        return tp_sum(
            lax.dynamic_update_slice_in_dim(
                jnp.zeros((images, values.shape[1]), jnp.float32), values, first_image, 0
            )
        )

    grad_final = all_images(grad_final)
    cond_wide = wide(cond_act)

    def image_part(columns):
        packed = jnp.concatenate(columns, 1)
        packed = jnp.pad(packed, ((0, 0), (0, -packed.shape[1] % 256)))
        part = packed.shape[1] // 2
        return lax.dynamic_slice_in_dim(packed, tp_index * part, part, 1)

    label_column = jnp.broadcast_to(wide(labels)[:, None], (images, 128))
    early_columns = [label_column, wide(features_low), wide(time_act), cond_wide, grad_final]
    grad_cond_act = 0.0
    for layer_no in reversed(range(L)):
        stream, row_sets, halves, branch, middle, mid_sets, hidden, mlp_out = kept[layer_no]
        base = layer_no * per_layer
        grad_sets = rows_in(grad_low.reshape(sp_rows, D))
        results, terms = each_half(
            lambda pair: mlp_back_call(pair[0], pair[1], store[layer_no], tp_parts, local_len),
            [(rows, hidden_here[0]) for rows, hidden_here in zip(grad_sets, hidden)],
        )
        held = weight_grad_call(
            [result[0] for result in results], grad_sets, places, base + starts[3], held
        )
        held = weight_grad_call(
            mid_sets, [result[1] for result in results], places, base + starts[2], held
        )
        upstream, mlp_sums, grad_low = back_call(
            middle, terms, upstream, modes[layer_no], 4, (branch, modes[layer_no], 2)
        )
        if box and layer_no == 0:
            late_sums = scatter_late(late_parts, slots - early, lanes, late_first, upstream)
        grad_sets = rows_in(grad_low.reshape(sp_rows, D))
        results, terms = each_half(
            lambda pair: attend_back_call(pair[0], pair[1], store[layer_no], tp_parts, local_len),
            [(rows, half[0]) for rows, half in zip(grad_sets, halves)],
        )
        held = weight_grad_call(
            [half[1] for half in halves], grad_sets, places, base + starts[1], held
        )
        held = weight_grad_call(
            row_sets, [result[0] for result in results], places, base + starts[0], held
        )
        below = None if layer_no == 0 else (kept[layer_no - 1][7], modes[layer_no - 1], 5)
        found = back_call(stream, terms, upstream, modes[layer_no], 1, below)
        grad_modes = jnp.concatenate(
            [found[1][:, :2], mlp_sums[:, 2:], mlp_sums[:, :2], gate_sum], 1
        ).reshape(own, 6 * D)
        mode_image = lax.dynamic_slice_in_dim(
            all_images(grad_modes), tp_index * mode_width, mode_width, 1
        )
        held = weight_grad_call(
            [conds],
            [jnp.pad(three_parts(mode_image), ((0, fill), (0, 0)))],
            places,
            base + starts[4],
            held,
        )
        grad_cond_act = grad_cond_act + modes_back_call(mode_image, store[layer_no], tp_parts)
        upstream = found[0]
        if below:
            grad_low, gate_sum = found[2], found[1][:, 2:]
        if box and layer_no == L - 1:
            grad_low = after(grad_low, held[0][2], held[1][2])
            lanes = Lanes()
            late_parts = held[0][2]
            late_first = scatter_late_first(
                late_parts,
                slots - early,
                lanes,
                tp_sum(grad_head),
                image_part(early_columns),
            )
            held = held[1:]
    grad_patch = over_rows(noisy_rows, low(upstream).reshape(sp_rows, D))
    grad_cond_act = tp_sum(grad_cond_act) + against_low(grad_final, final_weight)
    grad_condition = jax.vjp(jax.nn.silu, condition)[1](grad_cond_act)[0]
    grad_time_hidden = jax.vjp(jax.nn.silu, time_hidden)[1](
        against_low(grad_condition, time_second)
    )[0]
    if box:
        patch_sum = tp_sum(grad_patch).reshape(1, B, B)
        patch_first = low(patch_sum)
        parts = lax.dynamic_update_slice_in_dim(
            held[0][2],
            jnp.where(tp_index == 0, patch_first, low(patch_sum - wide(patch_first))),
            early_place(0, early, early + 1),
            0,
        )
        owned, owned_late, late_images, head_sum, early_images = scatter_early(
            parts,
            early + 1,
            lanes,
            *late_sums,
            image_part([grad_time_hidden, grad_condition]),
        )
        late_images = columns_in(late_images)
        early_images = columns_in(early_images)
        head_rows = head_sum.T.reshape(P_SIZE, D)
        patch_rows = tp_sum(owned[early]).reshape(P_SIZE, D)
        owned = jnp.concatenate([owned[:early], owned_late], 0)
        owned = sum_strays(
            owned, parts[16 * (early + 1) :], strays, stray_count, inverse, slots, me
        )
    else:
        owned = lax.psum_scatter(
            wide(held[0][2])[ordering], ("fsdp", "ctx"), scatter_dimension=0, tiled=True
        )
        patch_rows = lax.psum(grad_patch, ("fsdp", "ctx", "tp"))
        head_rows = lax.psum(grad_head, ("fsdp", "ctx", "tp")).T.reshape(P_SIZE, D)
        late_images = gather_images(jnp.concatenate([grad_time_hidden, grad_condition], 1))
        early_images = gather_images(jnp.concatenate(early_columns, 1))
    all_hidden, all_condition = jnp.split(late_images, 2, 1)
    cuts = [128]
    for length in (TFREQ, D, D):
        cuts.append(cuts[-1] + length)
    all_labels, all_features, all_time, all_cond, all_final = jnp.split(early_images, cuts, 1)
    all_final = all_final[:, : 2 * D]
    all_onehot = wide(all_labels[:, :1] == jnp.arange(NCLS, dtype=jnp.float32)[None, :])
    share = else_low.shape[0]
    device = (lax.axis_index("fsdp") * ctx_parts + lax.axis_index("ctx")) * tp_parts + tp_index
    begin = device * share
    row_total = else_low.shape[0] * fsdp_parts * ctx_parts * tp_parts // D
    row_count = min(share // D + 2, row_total)
    begin_row = jnp.minimum(begin // D, row_total - row_count)
    row_ids = begin_row + jnp.arange(row_count)
    edge = jnp.zeros((all_cond.shape[0], P_SIZE), jnp.float32)
    factors = jnp.concatenate(
        [edge, all_onehot, all_features, all_time, jnp.repeat(all_cond, 2, axis=1), edge], 1
    )
    factors = lax.dynamic_slice_in_dim(factors, begin_row, row_count, 1)
    first_start = P_SIZE + NCLS
    second_start = first_start + TFREQ
    final_start = second_start + D

    def rows_of(chosen, right):
        return contract("ic,id->cd", jnp.where(chosen[None, :], factors, 0.0), right)

    in_first = (row_ids >= first_start) & (row_ids < second_start)
    in_final = row_ids >= final_start
    odd = (row_ids - final_start) % 2 == 1
    near = rows_of(in_first, all_hidden)
    near = near + rows_of(jnp.logical_not(in_first | in_final), all_condition)
    near = near + rows_of(in_final & jnp.logical_not(odd), all_final[:, :D])
    near = near + rows_of(in_final & odd, all_final[:, D:])
    for begin_here, token_rows in ((0, patch_rows), (row_total - P_SIZE, head_rows)):
        here = row_ids - begin_here
        inside = (here >= 0) & (here < P_SIZE)
        near = jnp.where(
            inside[:, None], token_rows[jnp.clip(here, 0, P_SIZE - 1)], near
        )
    else_grad = lax.dynamic_slice_in_dim(near.reshape(-1), begin - begin_row * D, share, 0)
    squares = jnp.sum(owned * owned) + jnp.sum(else_grad * else_grad)
    totals = total(jnp.stack([loss_part, squares]))
    loss_total = totals[0]
    grad_norm = jnp.sqrt(totals[1])
    clip_factor = jnp.minimum(1.0, 1.0 / grad_norm)
    master_new, first_new, second_new, low_new = update_tiles(
        clip_factor, owned, tiles_master[0], tiles_first[0], tiles_second[0], bases[0]
    )
    else_master_new, else_first_new, else_second_new = adamw_flat(
        clip_factor * else_grad, else_master, else_first, else_second
    )
    return (
        loss_total,
        grad_norm,
        master_new[None],
        first_new[None],
        second_new[None],
        low_new[None],
        else_master_new,
        else_first_new,
        else_second_new,
        low(else_master_new),
    )


def solution(mesh):
    return jax.shard_map(
        on_device,
        mesh=mesh,
        in_specs=(
            P(("fsdp", "ctx"), None, None),
            P(("fsdp", "ctx"), None, None),
            P(("fsdp", "ctx")),
            P(("fsdp", "ctx")),
            P(),
            P("tp", ("fsdp", "ctx"), None, None),
            P("tp", ("fsdp", "ctx"), None, None),
            P("tp", ("fsdp", "ctx"), None, None),
            P("tp", ("fsdp", "ctx"), None, None),
            P("tp", ("fsdp", "ctx"), None, None),
            P(("fsdp", "ctx", "tp")),
            P(("fsdp", "ctx", "tp")),
            P(("fsdp", "ctx", "tp")),
            P(("fsdp", "ctx", "tp")),
        ),
        out_specs=(
            P(),
            P(),
            P("tp", ("fsdp", "ctx"), None, None),
            P("tp", ("fsdp", "ctx"), None, None),
            P("tp", ("fsdp", "ctx"), None, None),
            P("tp", ("fsdp", "ctx"), None, None),
            P(("fsdp", "ctx", "tp")),
            P(("fsdp", "ctx", "tp")),
            P(("fsdp", "ctx", "tp")),
            P(("fsdp", "ctx", "tp")),
        ),
        check_vma=False,
    )
```

```python
import math

import jax
import jax.numpy as jnp
from jax import lax
from jax.experimental import pallas as pl
from jax.experimental.pallas import tpu as pltpu
from jax.sharding import PartitionSpec as P

D = 1024
HD = 64
F = 4096
P_SIZE = 16
TFREQ = 256
NCLS = 1000
GRID = 16
L = 2
B = 128


HIGHEST = lax.Precision.HIGHEST
EPS_NORM = 1e-06
RATE = 0.02
DECAY = 0.1


def matmul(left_op, right_op):
    return jnp.dot(left_op, right_op, precision=HIGHEST)


def contract(formula, left_op, right_op):
    return jnp.einsum(formula, left_op, right_op, precision=HIGHEST)


def product(left_op, right_op):
    return jnp.dot(left_op, right_op, preferred_element_type=jnp.float32)


def over_rows(left_op, right_op):
    return lax.dot_general(
        left_op, right_op, (((0,), (0,)), ((), ())), preferred_element_type=jnp.float32
    )


def against(left_op, right_op):
    return lax.dot_general(
        left_op, right_op, (((1,), (1,)), ((), ())), preferred_element_type=jnp.float32
    )


def normed(stream):
    centred = stream - jnp.mean(stream, -1, keepdims=True)
    return centred * lax.rsqrt(jnp.mean(centred * centred, -1, keepdims=True) + EPS_NORM)


def modulate(stream, offset, factor):
    return normed(stream) * (1.0 + factor) + offset


def gelu_tanh(values):
    return jax.nn.gelu(values, approximate=True)


def time_features(time_steps):
    half_count = TFREQ // 2
    freqs = jnp.exp(-math.log(10000.0) * jnp.arange(half_count, dtype=jnp.float32) / half_count)
    angles = time_steps.astype(jnp.float32)[:, None] * freqs[None, :]
    return jnp.concatenate([jnp.cos(angles), jnp.sin(angles)], -1)


def position_table(token_ids):
    quarter = D // 4
    omegas = 1.0 / 10000.0 ** (jnp.arange(quarter, dtype=jnp.float32) / quarter)
    row_angle = (token_ids // GRID).astype(jnp.float32)[:, None] * omegas[None, :]
    col_angle = (token_ids % GRID).astype(jnp.float32)[:, None] * omegas[None, :]
    return jnp.concatenate(
        [jnp.sin(row_angle), jnp.cos(row_angle), jnp.sin(col_angle), jnp.cos(col_angle)], -1
    )


def signal_level(time_steps):
    phase = (time_steps.astype(jnp.float32) / 1000.0 + 0.008) / 1.008 * (math.pi / 2)
    return jnp.cos(phase) ** 2


def shard_shapes(tp_parts):
    head_width = D // tp_parts
    hidden_width = F // tp_parts
    return [
        (D, 3 * head_width),
        (head_width, D),
        (D, hidden_width),
        (hidden_width, D),
        (D, 6 * head_width),
    ]


def untile(tile_set, height, breadth):
    block = tile_set.shape[-1]
    return (
        tile_set.reshape(height // block, breadth // block, block, block)
        .transpose(0, 2, 1, 3)
        .reshape(height, breadth)
    )


def retile(matrix):
    height, breadth = matrix.shape
    return matrix.reshape(height // B, B, breadth // B, B).transpose(0, 2, 1, 3).reshape(-1, B, B)


def unpack_layers(tile_set, tp_parts):
    layer_list = []
    cursor = 0
    for layer_no in range(L):
        matrices = []
        for height, breadth in shard_shapes(tp_parts):
            amount = height * breadth // (B * B)
            matrices.append(untile(tile_set[cursor : cursor + amount], height, breadth))
            cursor += amount
        layer_list.append(matrices)
    return layer_list


def pack_layers(layer_list):
    return jnp.concatenate([retile(matrix) for matrices in layer_list for matrix in matrices], 0)


def else_shapes():
    return [(P_SIZE, D), (NCLS, D), (TFREQ, D), (D, D), (D, 2 * D), (D, P_SIZE)]


def split_else(flat_params):
    components = []
    cursor = 0
    for height, breadth in else_shapes():
        components.append(flat_params[cursor : cursor + height * breadth].reshape(height, breadth))
        cursor += height * breadth
    return components


def reflection(vectors):
    outer_prod = vectors[..., :, None] * vectors[..., None, :]
    return (
        jnp.eye(vectors.shape[-1], dtype=jnp.float32)
        - 2.0 * outer_prod / jnp.sum(vectors * vectors, -1)[..., None, None]
    )


def rotate(left_basis, middle, right_basis):
    return contract(
        "...ab,...bc->...ac", contract("...ab,...bc->...ac", left_basis, middle), right_basis
    )


def adam_finish(turned, master_state, first_state, second_state, left_basis, right_basis):
    first_new = 0.5 * first_state + 0.5 * turned
    second_new = 0.5 * second_state + 0.5 * turned * turned
    direction = first_new / (jnp.sqrt(second_new) + 1e-08)
    return (master_state - RATE * rotate(left_basis, direction, right_basis), first_new, second_new)


def adamw_flat(grad_clipped, master_state, first_state, second_state):
    first_new = 0.5 * first_state + 0.5 * grad_clipped
    second_new = 0.5 * second_state + 0.5 * grad_clipped * grad_clipped
    master_new = master_state - RATE * (
        first_new / (jnp.sqrt(second_new) + 1e-08) + DECAY * master_state
    )
    return (master_new, first_new, second_new)


def is_box():
    return (lax.axis_size("fsdp"), lax.axis_size("ctx"), lax.axis_size("tp")) == (8, 2, 2)


def swap_tp(value):
    return lax.ppermute(value, "tp", [(0, 1), (1, 0)])


def swap_y(value):
    return lax.ppermute(value, "ctx", [(0, 1), (1, 0)])


def swap_f(value, bit):
    return lax.ppermute(value, "fsdp", [(place, place ^ bit) for place in range(8)])


def swap_x(value):
    return swap_f(value, 1)


def place_z():
    return lax.axis_index("fsdp") // 2


def low(value):
    return value.astype(jnp.bfloat16)


def wide(value):
    return value.astype(jnp.float32)


def after(value, *earlier):
    return lax.optimization_barrier((value, *earlier))[0]


class Lanes:
    def __init__(self):
        self.done = ()

    def step(self, sends, *earlier):
        values = lax.optimization_barrier(tuple(value for _, value in sends) + self.done + earlier)
        self.done = tuple(swap(value) for (swap, _), value in zip(sends, values))
        return list(self.done)


def move_z(step, sources):
    pairs = [(2 * z + x, 2 * (z + step) + x) for z in sources for x in range(2)]
    return lambda value: lax.ppermute(value, "fsdp", pairs)


def to_z(rel):
    return lambda value: swap_f(value, 2 * rel)


class ZLine:
    def __init__(self, own):
        self.above, self.below = [own], [own]

    def sends(self):
        hop = len(self.above)
        return [
            (move_z(1, range(hop - 1, 3)), self.above[-1]),
            (move_z(-1, range(1, 5 - hop)), self.below[-1]),
        ]

    def take(self, arrived):
        self.above.append(arrived[0])
        self.below.append(arrived[1])

    def block(self, rel, token=None):
        z = place_z()
        if token is not None:
            z = z + token[0, 0]
        above, below = self.above, self.below
        if rel == 0:
            return above[0]
        if rel == 1:
            return jnp.where(z % 2 == 1, above[1], below[1])
        if rel == 2:
            return jnp.where(z >= 2, above[2], below[2])
        return jnp.where(
            z == 0, below[3], jnp.where(z == 3, above[3], jnp.where(z == 1, below[1], above[1]))
        )


class ZSum:
    def __init__(self):
        self.last = None
        self.up = self.down = None

    def sends(self, rel, block):
        z = place_z()
        if rel == 3:
            self.last = block
            up, down = block, block
        elif rel == 2:
            up, down = block + self.up, block + self.down
        else:
            up = jnp.where(z == 1, self.last, block) + self.up
            down = jnp.where(z == 2, self.last, block) + self.down
        return [
            (move_z(1, range(0, 4 - rel)), low(up)),
            (move_z(-1, range(rel, 4)), low(down)),
        ]

    def take(self, arrived):
        self.up, self.down = arrived

    def total(self, block):
        return block + self.up + self.down


def early_slots(slots):
    return slots - slots * 25 // 72


def gather_tiles(own, early, place_early, place_late, else_low, targets):
    half = early // 2
    lanes = Lanes()
    line, late_line = ZLine(own[:early]), ZLine(own[early:])
    rest = whole = None
    tokens = []
    for rel in range(4):
        block = line.block(rel, tokens[rel - 2] if rel >= 2 else None)
        sends = [(swap_x, block), (swap_y, block)]
        waits = ()
        if rel == 3:
            waits = rest[0]
        going = line if rel < 3 else late_line
        sends += going.sends()
        if rel == 1:
            by_x, by_y, above, below, *both = lanes.step(sends + else_diagonal)
            whole = finish_else(else_line, both)
            rest = cut_else(whole)
        else:
            by_x, by_y, above, below = lanes.step(sends, *waits)
        going.take((above, below))
        sends = [(swap_y, by_x[:half]), (swap_x, by_y[half:])]
        if rel == 0:
            first, second, *arrived = lanes.step(
                sends + [(to_z(other), else_low.reshape(1, -1, 128)) for other in (1, 2, 3)],
                targets,
            )
            else_line, else_diagonal = start_else(else_low, lanes, arrived)
        elif rel < 3:
            first, second, *arrived = lanes.step(sends + late_line.sends())
            late_line.take(arrived)
        else:
            first, second = lanes.step(sends)
        at = 4 * rel * early
        group = [
            (block, at),
            (by_y, at + early),
            (by_x, at + 2 * early),
            (first, at + 3 * early),
            (second, at + 3 * early + half),
        ]
        tokens.append(place_early(group))
    line = jnp.concatenate([late_line.block(rel) for rel in range(4)], 0)
    count = line.shape[0]
    half = count // 2
    by_x, by_y = lanes.step([(swap_x, line), (swap_y, line)])
    place_late([(line, 0)])

    def finish():
        first, second = lanes.step([(swap_y, by_x[:half]), (swap_x, by_y[half:])])
        place_late([(by_y, count), (by_x, 2 * count)])
        place_late([(first, 3 * count), (second, 3 * count + half)])

    return rest, finish, (by_x, by_y)


def relative(owner):
    rel_f = jnp.bitwise_xor(owner // 2, lax.axis_index("fsdp"))
    return rel_f // 2, rel_f % 2, jnp.bitwise_xor(owner % 2, lax.axis_index("ctx"))


def early_place(owner, slot, slots):
    rel_z, rel_x, rel_y = relative(owner)
    return ((rel_z * 2 + rel_x) * 2 + rel_y) * slots + slot


def late_place(owner, slot, slots):
    rel_z, rel_x, rel_y = relative(owner)
    return ((rel_x * 2 + rel_y) * 4 + rel_z) * slots + slot


def scatter_late_first(parts, slots, lanes):
    both = parts[12 * slots :]
    return lanes.step([(swap_y, both[: 2 * slots]), (swap_x, both[2 * slots :])])


def scatter_late(parts, slots, lanes, wait, head_sum, images_part, *earlier):
    count = 4 * slots
    half = count // 2
    keep, to_y, to_x, _ = (parts[part * count : (part + 1) * count] for part in range(4))
    by_y, by_x = wait
    to_x = jnp.concatenate([low(wide(to_x[:half]) + by_y), to_x[half:]], 0)
    to_y = jnp.concatenate([to_y[:half], low(wide(to_y[half:]) + by_x)], 0)
    from_x, from_y, head_y, *images = lanes.step(
        [(swap_x, to_x), (swap_y, to_y), (swap_y, head_sum)]
        + [(to_z(rel), images_part) for rel in (1, 2, 3)],
        *earlier,
    )
    keep = wide(keep) + from_x + from_y
    return (
        [keep[rel * slots : (rel + 1) * slots] for rel in range(4)],
        head_sum + head_y,
        jnp.concatenate([images_part] + images, 0),
    )


def scatter_early(parts, slots, lanes, late, head_sum, early_images, images_part):
    half = slots // 2

    def block(part, begin, end):
        return parts[part * slots + begin : part * slots + end]

    def diagonal(rel):
        return [
            (swap_y, block(4 * rel + 3, 0, half)),
            (swap_x, block(4 * rel + 3, half, slots)),
        ]

    def sides(rel, arrived):
        by_y, by_x = arrived
        return [
            (
                swap_x,
                jnp.concatenate(
                    [
                        low(wide(block(4 * rel + 2, 0, half)) + by_y),
                        block(4 * rel + 2, half, slots),
                    ],
                    0,
                ),
            ),
            (
                swap_y,
                jnp.concatenate(
                    [
                        block(4 * rel + 1, 0, half),
                        low(wide(block(4 * rel + 1, half, slots)) + by_x),
                    ],
                    0,
                ),
            ),
        ]

    def kept(rel, arrived):
        return wide(block(4 * rel, 0, slots)) + arrived[0] + arrived[1]

    line, late_line = ZSum(), ZSum()
    arrived = lanes.step(
        diagonal(3) + late_line.sends(3, late[3]) + [(swap_x, head_sum), (swap_y, early_images)]
    )
    diagonal_3 = arrived[:2]
    late_line.take(arrived[2:4])
    head_sum = head_sum + arrived[4]
    early_images = jnp.concatenate([early_images, arrived[5]], 0)
    arrived = lanes.step(
        diagonal(2) + late_line.sends(2, late[2]) + [(to_z(1), head_sum), (swap_x, early_images)]
    )
    diagonal_2 = arrived[:2]
    late_line.take(arrived[2:4])
    head_sum = head_sum + arrived[4]
    early_images = jnp.concatenate([early_images, arrived[5]], 0)
    arrived = lanes.step(sides(3, diagonal_3) + late_line.sends(1, late[1]))
    late_line.take(arrived[2:])
    owned_late = late_line.total(late[0])
    kept_3 = kept(3, arrived)
    arrived = lanes.step(
        diagonal(1) + [(to_z(rel), images_part) for rel in (1, 2, 3)] + [(to_z(2), head_sum)]
    )
    diagonal_1 = arrived[:2]
    images = jnp.concatenate([images_part] + arrived[2:5], 0)
    head_sum = head_sum + arrived[5]
    arrived = lanes.step(sides(2, diagonal_2) + line.sends(3, kept_3) + [(swap_y, images)])
    line.take(arrived[2:4])
    kept_2 = kept(2, arrived)
    images = jnp.concatenate([images, arrived[4]], 0)
    arrived = lanes.step(diagonal(0) + [(swap_x, images)])
    diagonal_0 = arrived[:2]
    images = jnp.concatenate([images, arrived[2]], 0)
    arrived = lanes.step(sides(1, diagonal_1) + line.sends(2, kept_2))
    line.take(arrived[2:4])
    arrived_0 = lanes.step(sides(0, diagonal_0) + line.sends(1, kept(1, arrived)))
    line.take(arrived_0[2:4])
    return line.total(kept(0, arrived_0)), owned_late, images, head_sum, early_images


def gather_images(value):
    if not is_box():
        return lax.all_gather(value, ("fsdp", "ctx"), axis=0, tiled=True)
    value = jnp.concatenate([value] + [swap_f(value, 2 * rel) for rel in (1, 2, 3)], 0)
    by_x, by_y = swap_x(value), swap_y(value)
    return jnp.concatenate([value, by_y, by_x, swap_x(by_y)], 0)


def start_else(flat, lanes, arrived):
    z = place_z()
    line = [flat.reshape(1, -1, 128)] + arrived
    line = [
        jnp.where(
            z == place,
            line[0],
            jnp.where(z == place ^ 1, line[1], jnp.where(z == place ^ 2, line[2], line[3])),
        )
        for place in range(4)
    ]
    line = jnp.concatenate(line, 0)
    by_x, by_y = lanes.step([(swap_x, line), (swap_y, line)])
    half = line.shape[1] // 2
    return (line, by_x, by_y), [(swap_y, by_x[:, :half]), (swap_x, by_y[:, half:])]


def finish_else(lines, both):
    x, y, core = lax.axis_index("fsdp") % 2, lax.axis_index("ctx"), lax.axis_index("tp")
    line, by_x, by_y = lines
    both = jnp.concatenate(both, 1)
    y_low = [jnp.where(y == 0, line, by_y), jnp.where(y == 0, by_x, both)]
    y_high = [jnp.where(y == 0, by_y, line), jnp.where(y == 0, both, by_x)]
    chip = jnp.stack(
        [
            jnp.stack([jnp.where(x == 0, y_low[0], y_low[1]), jnp.where(x == 0, y_high[0], y_high[1])], 1),
            jnp.stack([jnp.where(x == 0, y_low[1], y_low[0]), jnp.where(x == 0, y_high[1], y_high[0])], 1),
        ],
        1,
    )
    other = swap_tp(chip)
    return jnp.stack(
        [jnp.where(core == 0, chip, other), jnp.where(core == 0, other, chip)], 3
    )


def cut_else(whole):
    rows = whole.reshape(-1, D)
    counts = [P_SIZE, NCLS, TFREQ, D, 2 * D, P_SIZE]
    ends = [sum(counts[: place + 1]) for place in range(6)]
    parts = [rows[end - count : end] for end, count in zip(ends, counts)]
    return tuple(parts[:4]), parts[4], parts[5].reshape(D, P_SIZE)


def final_product(left_op, final_rows):
    rows = left_op.shape[0]
    nothing = jnp.zeros_like(left_op)
    spread = jnp.concatenate(
        [
            jnp.stack([left_op, nothing], -1).reshape(rows, 2 * D),
            jnp.stack([nothing, left_op], -1).reshape(rows, 2 * D),
        ],
        0,
    )
    found = product(spread, final_rows)
    return jnp.stack([found[:rows], found[rows:]], 1)


def final_product_back(grads, final_rows):
    rows = grads.shape[0]
    found = against_low(jnp.concatenate([grads[:, :D], grads[:, D:]], 0), final_rows)
    return found[:rows].reshape(rows, D, 2)[:, :, 0] + found[rows:].reshape(rows, D, 2)[:, :, 1]


def total(value):
    if not is_box():
        return lax.psum(value, ("fsdp", "ctx", "tp"))
    value = value + swap_tp(value)
    value = value + swap_y(value)
    for bit in (1, 2, 4):
        value = value + swap_f(value, bit)
    return value


def tp_sum(value):
    if lax.axis_size("tp") == 2:
        return value + swap_tp(value)
    return lax.psum(value, "tp")


def columns_in(value):
    if lax.axis_size("tp") == 2:
        other = swap_tp(value)
        at_zero = lax.axis_index("tp") == 0
        return jnp.concatenate(
            [jnp.where(at_zero, value, other), jnp.where(at_zero, other, value)], -1
        )
    return lax.all_gather(value, "tp", axis=value.ndim - 1, tiled=True)


def rows_in(value_low):
    if lax.axis_size("tp") == 2:
        return [value_low, swap_tp(value_low)]
    return [lax.all_gather(value_low, "tp", axis=0, tiled=True)]


def each_half(work, row_sets):
    if len(row_sets) == 2:
        other = work(row_sets[1])
        sent = swap_tp(other[-1])
        own = work(row_sets[0])
        return [own[:-1], other[:-1]], [own[-1], sent]
    whole = work(row_sets[0])
    return [whole[:-1]], [lax.psum_scatter(whole[-1], "tp", scatter_dimension=0, tiled=True)]


BIG = 56 * 1024 * 1024


def against_value(left_op, right_op):
    return lax.dot_general(
        left_op, right_op, (((1,), (1,)), ((), ())), preferred_element_type=jnp.float32
    )


def untile_into(matrix, tile_set):
    rows, columns = matrix.shape[0] // B, matrix.shape[1] // B
    for row in range(rows):
        for column in range(columns):
            matrix[row * B : (row + 1) * B, column * B : (column + 1) * B] = tile_set[
                row * columns + column
            ]


def segments(tp_parts):
    found = []
    begin = 0
    for height, breadth in shard_shapes(tp_parts):
        amount = height * breadth // (B * B)
        found.append((amount, begin))
        begin += amount
    return found


def weight_spec(kind, tp_parts):
    amount, begin = segments(tp_parts)[kind]
    return pl.BlockSpec(
        (amount, B, B), lambda *step: (begin // amount, 0, 0), pipeline_mode=pl.Buffered(1)
    )


def rows_spec(rows, breadth):
    return pl.BlockSpec((rows, breadth), lambda step: (step, 0))


def shaped(rows, breadth, kind):
    return jax.ShapeDtypeStruct((rows, breadth), kind)


def params():
    return pltpu.CompilerParams(vmem_limit_bytes=BIG)


def attend_kernel(normed_in, qkv_tiles, proj_tiles, projected, attended, partial, w_qkv, w_proj):
    @pl.when(pl.program_id(0) == 0)
    def _():
        untile_into(w_qkv, qkv_tiles)
        untile_into(w_proj, proj_tiles)

    values = low(product(normed_in[...], w_qkv[...]))
    projected[...] = values
    width = values.shape[1] // 3
    results = []
    for head in range(width // HD):
        at = head * HD
        query = values[:, at : at + HD]
        key_rows = values[:, width + at : width + at + HD]
        value_rows = values[:, 2 * width + at : 2 * width + at + HD]
        scores = against_value(key_rows, query) * HD ** (-0.5)
        exponent = jnp.exp(scores - jnp.max(scores, 0, keepdims=True))
        probabilities = low(exponent / jnp.sum(exponent, 0, keepdims=True))
        results.append(low(over_rows(probabilities, value_rows)))
    result = jnp.concatenate(results, 1)
    attended[...] = result
    partial[...] = product(result, w_proj[...])


def attend_call(normed_in, store, tp_parts, local_len):
    rows = normed_in.shape[0]
    width = D // tp_parts
    return pl.pallas_call(
        attend_kernel,
        grid=(rows // local_len,),
        in_specs=[
            rows_spec(local_len, D),
            weight_spec(0, tp_parts),
            weight_spec(1, tp_parts),
        ],
        out_specs=[
            rows_spec(local_len, 3 * width),
            rows_spec(local_len, width),
            rows_spec(local_len, D),
        ],
        out_shape=[
            shaped(rows, 3 * width, jnp.bfloat16),
            shaped(rows, width, jnp.bfloat16),
            shaped(rows, D, jnp.float32),
        ],
        scratch_shapes=[
            pltpu.VMEM((D, 3 * width), jnp.bfloat16),
            pltpu.VMEM((width, D), jnp.bfloat16),
        ],
        compiler_params=params(),
        cost_estimate=pl.CostEstimate(
            flops=rows * D * width * 8, bytes_accessed=rows * D * 8, transcendentals=rows * 2048
        ),
    )(normed_in, store, store)


def attend_back_kernel(
    grad_branch, projected, qkv_tiles, proj_tiles, grad_qkv, partial, w_qkv, w_proj
):
    @pl.when(pl.program_id(0) == 0)
    def _():
        untile_into(w_qkv, qkv_tiles)
        untile_into(w_proj, proj_tiles)

    grad_attended = low(against_value(grad_branch[...], w_proj[...]))
    values = projected[...]
    width = values.shape[1] // 3
    grads = [[], [], []]
    for head in range(width // HD):
        at = head * HD
        query = values[:, at : at + HD]
        key_rows = values[:, width + at : width + at + HD]
        value_rows = values[:, 2 * width + at : 2 * width + at + HD]
        grad_here = grad_attended[:, at : at + HD]
        scores = against_value(key_rows, query) * HD ** (-0.5)
        exponent = jnp.exp(scores - jnp.max(scores, 0, keepdims=True))
        probabilities = exponent / jnp.sum(exponent, 0, keepdims=True)
        grad_prob = against_value(value_rows, grad_here)
        grad_scores = low(
            probabilities
            * (grad_prob - jnp.sum(probabilities * grad_prob, 0, keepdims=True))
        )
        grads[0].append(low(over_rows(grad_scores, key_rows) * HD ** (-0.5)))
        grads[1].append(low(product(grad_scores, query) * HD ** (-0.5)))
        grads[2].append(low(product(low(probabilities), grad_here)))
    result = jnp.concatenate(grads[0] + grads[1] + grads[2], 1)
    grad_qkv[...] = result
    partial[...] = against_value(result, w_qkv[...])


def attend_back_call(grad_branch, projected, store, tp_parts, local_len):
    rows = grad_branch.shape[0]
    width = D // tp_parts
    return pl.pallas_call(
        attend_back_kernel,
        grid=(rows // local_len,),
        in_specs=[
            rows_spec(local_len, D),
            rows_spec(local_len, 3 * width),
            weight_spec(0, tp_parts),
            weight_spec(1, tp_parts),
        ],
        out_specs=[rows_spec(local_len, 3 * width), rows_spec(local_len, D)],
        out_shape=[shaped(rows, 3 * width, jnp.bfloat16), shaped(rows, D, jnp.float32)],
        scratch_shapes=[
            pltpu.VMEM((D, 3 * width), jnp.bfloat16),
            pltpu.VMEM((width, D), jnp.bfloat16),
        ],
        compiler_params=params(),
        cost_estimate=pl.CostEstimate(
            flops=rows * D * width * 10, bytes_accessed=rows * D * 8, transcendentals=rows * 2048
        ),
    )(grad_branch, projected, store, store)


def mlp_chunk(tp_parts):
    return min(4 * B, F // tp_parts)


def chunk_specs(tp_parts):
    amount = D * mlp_chunk(tp_parts) // (B * B)
    up, down = (segments(tp_parts)[kind][1] // amount for kind in (2, 3))
    return [
        pl.BlockSpec((amount, B, B), lambda step: (up + step, 0, 0)),
        pl.BlockSpec((amount, B, B), lambda step: (down + step, 0, 0)),
    ]


def store_of_tile(tile, tp_parts):
    amount, begin = segments(tp_parts)[2]
    within = tile % sum(count for count, _ in segments(tp_parts)) - begin
    columns, wide_step = F // tp_parts // B, mlp_chunk(tp_parts) // B
    row, column = within // columns, within % columns
    moved = (column // wide_step * (D // B) + row) * wide_step + column % wide_step
    return jnp.where((within >= 0) & (within < amount), tile + moved - within, tile)


def add_to(total_ref, value):
    @pl.when(pl.program_id(0) == 0)
    def _():
        total_ref[...] = value

    @pl.when(pl.program_id(0) > 0)
    def _():
        total_ref[...] += value


def mlp_kernel(normed_mid, up_tiles, down_tiles, hidden, partial, w_up, w_down):
    untile_into(w_up, up_tiles)
    untile_into(w_down, down_tiles)
    values = product(normed_mid[...], w_up[...])
    hidden[...] = values
    add_to(partial, product(low(gelu_tanh(values)), w_down[...]))


def chunk_scratch(tp_parts):
    width = mlp_chunk(tp_parts)
    return [pltpu.VMEM((D, width), jnp.bfloat16), pltpu.VMEM((width, D), jnp.bfloat16)]


def all_rows(rows):
    return pl.BlockSpec((rows, D), lambda step: (0, 0))


def mlp_call(normed_mid, store, tp_parts, local_len):
    rows = normed_mid.shape[0]
    width, step_width = F // tp_parts, mlp_chunk(tp_parts)
    step_spec = pl.BlockSpec((rows, step_width), lambda step: (0, step))
    return pl.pallas_call(
        mlp_kernel,
        grid=(width // step_width,),
        in_specs=[all_rows(rows)] + chunk_specs(tp_parts),
        out_specs=[step_spec, all_rows(rows)],
        out_shape=[shaped(rows, width, jnp.float32), shaped(rows, D, jnp.float32)],
        scratch_shapes=chunk_scratch(tp_parts),
        compiler_params=params(),
        cost_estimate=pl.CostEstimate(
            flops=rows * D * width * 4,
            bytes_accessed=rows * D * 12 + 4 * D * width,
            transcendentals=rows * width,
        ),
    )(normed_mid, store, store)


def mlp_back_kernel(
    grad_mlp, hidden, up_tiles, down_tiles, activation, grad_hidden, partial, w_up, w_down
):
    untile_into(w_up, up_tiles)
    untile_into(w_down, down_tiles)
    values = hidden[...]
    factor = math.sqrt(2.0 / math.pi)
    square = values * values
    bent = jnp.tanh(factor * (values + 0.044715 * (square * values)))
    half_up = 0.5 * (1.0 + bent)
    activation[...] = low(values * half_up)
    slope = half_up + 0.5 * values * (1.0 - bent * bent) * (
        factor * (1.0 + 3.0 * 0.044715 * square)
    )
    grad = low(against_value(grad_mlp[...], w_down[...]) * slope)
    grad_hidden[...] = grad
    add_to(partial, against_value(grad, w_up[...]))


def mlp_back_call(grad_mlp, hidden, store, tp_parts, local_len):
    rows = grad_mlp.shape[0]
    width, step_width = F // tp_parts, mlp_chunk(tp_parts)
    step_spec = pl.BlockSpec((rows, step_width), lambda step: (0, step))
    return pl.pallas_call(
        mlp_back_kernel,
        grid=(width // step_width,),
        in_specs=[all_rows(rows), step_spec] + chunk_specs(tp_parts),
        out_specs=[step_spec, step_spec, all_rows(rows)],
        out_shape=[
            shaped(rows, width, jnp.bfloat16),
            shaped(rows, width, jnp.bfloat16),
            shaped(rows, D, jnp.float32),
        ],
        scratch_shapes=chunk_scratch(tp_parts),
        compiler_params=params(),
        cost_estimate=pl.CostEstimate(
            flops=rows * D * width * 4,
            bytes_accessed=rows * D * 16 + 4 * D * width,
            transcendentals=rows * width,
        ),
    )(grad_mlp, hidden, store, store)


def modes_call(cond_act, store, tp_parts):
    rows = cond_act.shape[0]
    width = 6 * D // tp_parts

    def kernel(left, tile_set, out):
        for column in range(width // B):
            total_here = 0.0
            for row in range(D // B):
                total_here = total_here + product(
                    left[:, row * B : (row + 1) * B], tile_set[row * (width // B) + column]
                )
            out[:, column * B : (column + 1) * B] = total_here

    return pl.pallas_call(
        kernel,
        grid=(1,),
        in_specs=[rows_spec(rows, D), weight_spec(4, tp_parts)],
        out_specs=rows_spec(rows, width),
        out_shape=shaped(rows, width, jnp.float32),
        compiler_params=params(),
    )(cond_act, store)


def three_parts(value):
    first = low(value)
    rest = value - wide(first)
    second = low(rest)
    return jnp.concatenate([first, second, low(rest - wide(second))], 0)


def against_low(value, weight):
    rows = value.shape[0]
    summed = against(three_parts(value), weight)
    return summed[:rows] + summed[rows : 2 * rows] + summed[2 * rows :]


def modes_back_call(grads, store, tp_parts):
    rows = grads.shape[0]
    width = 6 * D // tp_parts
    parts = three_parts(grads)

    def kernel(left, tile_set, out):
        for row in range(D // B):
            total_here = 0.0
            for column in range(width // B):
                total_here = total_here + against_value(
                    left[:, column * B : (column + 1) * B],
                    tile_set[row * (width // B) + column],
                )
            out[:, row * B : (row + 1) * B] = total_here

    summed = pl.pallas_call(
        kernel,
        grid=(1,),
        in_specs=[rows_spec(3 * rows, width), weight_spec(4, tp_parts)],
        out_specs=rows_spec(3 * rows, D),
        out_shape=shaped(3 * rows, D, jnp.float32),
        compiler_params=params(),
    )(parts, store)
    return summed[:rows] + summed[rows : 2 * rows] + summed[2 * rows :]


def weight_grad_call(lefts, rights, places, first_tile, held):
    height, breadth = lefts[0].shape[1], rights[0].shape[1]
    steps = min(4, height // B)
    count = len(lefts)
    row_tiles, column_tiles = height // B // steps, breadth // B
    amount = row_tiles * column_tiles
    given = [array for _, _, array in held if array is not None]

    def kernel(place, *refs):
        left_refs, right_refs = refs[:count], refs[count : 2 * count]
        outs = refs[2 * count + len(given) : 2 * count + len(given) + len(held)]
        ready, sem = refs[-2], refs[-1]
        step = pl.program_id(0)
        slot = lax.rem(step, 2)

        def drain(which):
            pltpu.make_async_copy(
                ready.at[which], outs[0].at[pl.ds(0, amount)], sem.at[which]
            ).wait()

        @pl.when(step >= 2)
        def _():
            drain(slot)

        block = over_rows(left_refs[0][...], right_refs[0][...])
        for left, right in zip(left_refs[1:], right_refs[1:]):
            block = block + over_rows(left[...], right[...])
        block = low(block)
        for row in range(row_tiles):
            for column in range(column_tiles):
                ready[slot, row * column_tiles + column] = block[
                    row * B : (row + 1) * B, column * B : (column + 1) * B
                ]

        def send(index, carry):
            where_to = place[first_tile + step * amount + index]
            for number, (begin, _, _) in enumerate(held):
                end = held[number + 1][0] if number + 1 < len(held) else 1 << 30
                copy = pltpu.make_async_copy(
                    ready.at[slot, index], outs[number].at[where_to - begin], sem.at[slot]
                )
                if len(held) == 1:
                    copy.start()
                else:
                    pl.when((where_to >= begin) & (where_to < end))(copy.start)
            return carry

        lax.fori_loop(0, amount, send, 0)

        @pl.when(step == steps - 1)
        def _():
            drain(slot)
            if steps > 1:
                drain(1 - slot)

    rows = [left.shape[0] for left in lefts]
    anywhere = pl.BlockSpec(memory_space=pl.ANY)
    in_specs = [
        pl.BlockSpec((size, height // steps), lambda step, place: (0, step)) for size in rows
    ] + [
        pl.BlockSpec((size, breadth), lambda step, place: (0, 0), pipeline_mode=pl.Buffered(1))
        for size in rows
    ]
    in_specs += [anywhere] * len(given)
    operands = [places, *lefts, *rights, *given]
    aliases = {}
    for number, (_, _, array) in enumerate(held):
        if array is not None:
            aliases[1 + 2 * count + len(aliases)] = number
    results = pl.pallas_call(
        kernel,
        grid_spec=pltpu.PrefetchScalarGridSpec(
            num_scalar_prefetch=1,
            grid=(steps,),
            in_specs=in_specs,
            out_specs=[anywhere] * len(held),
            scratch_shapes=[
                pltpu.VMEM((2, amount, B, B), jnp.bfloat16),
                pltpu.SemaphoreType.DMA((2,)),
            ],
        ),
        out_shape=[
            jax.ShapeDtypeStruct((places_here, B, B), jnp.bfloat16) for _, places_here, _ in held
        ],
        input_output_aliases=aliases,
        compiler_params=params(),
        cost_estimate=pl.CostEstimate(
            flops=2 * sum(rows) * height * breadth,
            bytes_accessed=2 * (sum(rows) * (height + breadth) + height * breadth),
            transcendentals=0,
        ),
    )(*operands)
    return [
        (begin, places_here, array) for (begin, places_here, _), array in zip(held, results)
    ]


def place_call(pieces, targets, held):
    count = len(pieces)
    given = [array for _, _, array in held if array is not None]

    def kernel(target, *refs):
        outs = refs[count + len(given) : count + len(given) + len(held)]
        token = refs[count + len(given) + len(held)]
        buffers, loaded, stored = refs[-2 - count : -2], refs[-2], refs[-1]
        token[...] = jnp.zeros_like(token)
        for number in range(count):
            pltpu.make_async_copy(refs[number], buffers[number], loaded.at[number]).start()
        for number, (piece, begin) in enumerate(pieces):
            pltpu.make_async_copy(refs[number], buffers[number], loaded.at[number]).wait()

            def send(index, carry):
                where_to = target[begin + index]
                left = True
                for out_number, (first, amount, _) in enumerate(held):
                    last = out_number == len(held) - 1
                    inside = (where_to >= first) & (where_to < first + amount - 1)
                    at = where_to - first
                    if last:
                        at = jnp.where(inside, at, amount - 1)
                        inside = left
                    else:
                        left = jnp.logical_not(inside)
                    copy = pltpu.make_async_copy(
                        buffers[number].at[index], outs[out_number].at[at], stored.at[number]
                    )
                    if len(held) == 1:
                        copy.start()
                    else:
                        pl.when(inside)(copy.start)
                return carry

            lax.fori_loop(0, piece.shape[0], send, 0)
        for number, (piece, begin) in enumerate(pieces):
            pltpu.make_async_copy(
                buffers[number], outs[0].at[pl.ds(0, piece.shape[0])], stored.at[number]
            ).wait()

    anywhere = pl.BlockSpec(memory_space=pl.ANY)
    operands = [targets] + [piece for piece, _ in pieces] + given
    aliases = {}
    for number, (_, _, array) in enumerate(held):
        if array is not None:
            aliases[1 + count + len(aliases)] = number
    results = pl.pallas_call(
        kernel,
        grid_spec=pltpu.PrefetchScalarGridSpec(
            num_scalar_prefetch=1,
            grid=(1,),
            in_specs=[anywhere] * (len(operands) - 1),
            out_specs=[anywhere] * len(held) + [pl.BlockSpec((8, B), lambda step, target: (0, 0))],
            scratch_shapes=[pltpu.VMEM(piece.shape, jnp.bfloat16) for piece, _ in pieces]
            + [pltpu.SemaphoreType.DMA((count,))] * 2,
        ),
        out_shape=[jax.ShapeDtypeStruct((amount, B, B), jnp.bfloat16) for _, amount, _ in held]
        + [jax.ShapeDtypeStruct((8, B), jnp.int32)],
        input_output_aliases=aliases,
        compiler_params=params(),
        cost_estimate=pl.CostEstimate(
            flops=0,
            bytes_accessed=sum(4 * piece.shape[0] * B * B for piece, _ in pieces),
            transcendentals=0,
        ),
    )(*operands)
    return [(first, amount, array) for (first, amount, _), array in zip(held, results)], results[-1]


def chips_sum(value):
    for swap in (swap_y, swap_x, lambda part: swap_f(part, 2), lambda part: swap_f(part, 4)):
        value = value + swap(value)
    return value


LOT = 8


def lots(count):
    return (count + LOT - 1) // LOT


def bring_strays(store, strays, count, owned_tiles, ordering, slots, me, tp_parts):
    def body(state):
        lot, held = state
        tiles = lax.dynamic_slice_in_dim(strays, lot * LOT, LOT, 0)
        valid = lot * LOT + jnp.arange(LOT) < count
        here = ordering[tiles]
        mine = valid & (here // slots == me)
        sent = jnp.where(mine[:, None, None], owned_tiles[here % slots], 0)
        sent = chips_sum(sent)
        at = jnp.where(valid, store_of_tile(tiles, tp_parts), held.shape[0])
        return lot + 1, held.at[at].set(sent, mode="drop")

    return lax.while_loop(lambda state: state[0] < lots(count), body, (0, store))[1]


def sum_strays(owned, parts, strays, count, ordering, slots, me):
    def body(state):
        lot, held = state
        tiles = lax.dynamic_slice_in_dim(strays, lot * LOT, LOT, 0)
        valid = lot * LOT + jnp.arange(LOT) < count
        summed = chips_sum(wide(lax.dynamic_slice_in_dim(parts, lot * LOT, LOT, 0)))
        here = ordering[tiles]
        at = jnp.where(valid & (here // slots == me), here % slots, slots)
        return lot + 1, held.at[at].set(summed, mode="drop")

    return lax.while_loop(lambda state: state[0] < lots(count), body, (0, owned))[1]


def normed_value(stream):
    centred = stream - jnp.mean(stream, -1, keepdims=True)
    rate = lax.rsqrt(jnp.mean(centred * centred, -1, keepdims=True) + EPS_NORM)
    return centred * rate, rate


def rows_kernel_call(kernel, wide_ins, mode_ins, outs, earlier=()):
    count = len(wide_ins) + len(mode_ins)

    def body(*refs):
        kernel(*refs[:count], *refs[count + len(earlier) :])

    own, group = wide_ins[0].shape[:2]
    rows = pl.BlockSpec((1, group, D), lambda step: (step, 0, 0))
    few = lambda count: pl.BlockSpec((1, count, D), lambda step: (step, 0, 0))
    return pl.pallas_call(
        body,
        grid=(own,),
        in_specs=[rows] * len(wide_ins)
        + [few(modes.shape[1]) for modes in mode_ins]
        + [pl.BlockSpec(memory_space=pl.ANY)] * len(earlier),
        out_specs=[rows if count is None else few(count) for count, _ in outs],
        out_shape=[
            jax.ShapeDtypeStruct((own, group if count is None else count, D), kind)
            for count, kind in outs
        ],
        compiler_params=params(),
        cost_estimate=pl.CostEstimate(
            flops=own * group * D * 20,
            bytes_accessed=own * group * D * 4 * (len(wide_ins) + len(outs)),
            transcendentals=own * group,
        ),
    )(*wide_ins, *mode_ins, *earlier)


def modulate_call(stream, modes, shift, scale):
    def kernel(values, mode, out):
        out[0] = low(
            normed_value(values[0])[0] * (1.0 + mode[0, scale : scale + 1, :])
            + mode[0, shift : shift + 1, :]
        )

    return rows_kernel_call(kernel, [stream], [modes], [(None, jnp.bfloat16)])[0]


def residual_call(stream, terms, modes, gate, next_modes, shift, scale, earlier=()):
    def kernel(*refs):
        values, term_refs = refs[0], refs[1 : 1 + len(terms)]
        mode, mode_next, branch, stream_new, out = refs[1 + len(terms) :]
        summed = term_refs[0][0]
        for term in term_refs[1:]:
            summed = summed + term[0]
        branch[0] = summed
        result = values[0] + mode[0, gate : gate + 1, :] * summed
        stream_new[0] = result
        out[0] = low(
            normed_value(result)[0] * (1.0 + mode_next[0, scale : scale + 1, :])
            + mode_next[0, shift : shift + 1, :]
        )

    shape = stream.shape
    return rows_kernel_call(
        kernel,
        [stream] + [term.reshape(shape) for term in terms],
        [modes, next_modes],
        [(None, jnp.float32), (None, jnp.float32), (None, jnp.bfloat16)],
        earlier,
    )


def back_call(stream, terms, upstream, modes, scale, below, earlier=()):
    shape = stream.shape
    wide_ins = [stream] + [term.reshape(shape) for term in terms]
    if upstream is not None:
        wide_ins.append(upstream)
    mode_ins = [modes]
    outs = [(None, jnp.float32), (3 if below else 2, jnp.float32)]
    if below:
        branch, branch_modes, gate = below
        wide_ins.append(branch)
        mode_ins.append(branch_modes)
        outs.append((None, jnp.bfloat16))

    def kernel(*refs):
        ins, modes_in = refs[: len(wide_ins)], refs[len(wide_ins) : len(wide_ins) + len(mode_ins)]
        results = refs[len(wide_ins) + len(mode_ins) :]
        grad = ins[1][0]
        for term in ins[2 : 1 + len(terms)]:
            grad = grad + term[0]
        normal, rate = normed_value(ins[0][0])
        results[1][0, 0:1, :] = jnp.sum(grad, 0, keepdims=True)
        results[1][0, 1:2, :] = jnp.sum(grad * normal, 0, keepdims=True)
        grad = grad * (1.0 + modes_in[0][0, scale : scale + 1, :])
        grad = rate * (
            grad
            - jnp.mean(grad, -1, keepdims=True)
            - normal * jnp.mean(grad * normal, -1, keepdims=True)
        )
        if upstream is not None:
            grad = grad + ins[1 + len(terms)][0]
        results[0][0] = grad
        if below:
            results[1][0, 2:3, :] = jnp.sum(grad * ins[-1][0], 0, keepdims=True)
            results[2][0] = low(modes_in[1][0, gate : gate + 1, :] * grad)

    return rows_kernel_call(kernel, wide_ins, mode_ins, outs, earlier)


def update_kernel(clip, grad, master, first, second, bases, master_out, first_out, second_out, low_out):
    eye = lax.broadcasted_iota(jnp.int32, (B, B), 0) == lax.broadcasted_iota(jnp.int32, (B, B), 1)
    left_row = bases[:, 0:1, :]
    right_row = bases[:, 1:2, :]
    left_col = jnp.sum(jnp.where(eye[None], left_row, 0.0), 2, keepdims=True)
    left_scaled = left_col * (2.0 / jnp.sum(left_row * left_row, 2, keepdims=True))
    right_scaled = right_row * (2.0 / jnp.sum(right_row * right_row, 2, keepdims=True))

    def turn(middle):
        middle = middle - left_scaled * jnp.sum(left_col * middle, 1, keepdims=True)
        return middle - jnp.sum(middle * right_row, 2, keepdims=True) * right_scaled

    turned = turn(clip[0, 0] * grad[...])
    first_new = 0.5 * first[...] + 0.5 * turned
    second_new = 0.5 * second[...] + 0.5 * turned * turned
    first_out[...] = first_new
    second_out[...] = second_new
    master_new = master[...] - RATE * turn(first_new / (jnp.sqrt(second_new) + 1e-08))
    master_out[...] = master_new
    low_out[...] = master_new.astype(jnp.bfloat16)


def update_tiles(clip_factor, grad, master, first, second, bases):
    slots = grad.shape[0]
    amount = max(count for count in (1, 2, 3, 4, 6, 8) if slots % count == 0)
    tile_spec = pl.BlockSpec((amount, B, B), lambda step: (step, 0, 0))
    whole = jax.ShapeDtypeStruct(grad.shape, jnp.float32)
    return pl.pallas_call(
        update_kernel,
        grid=(slots // amount,),
        in_specs=[pl.BlockSpec(memory_space=pltpu.SMEM)]
        + [tile_spec] * 4
        + [pl.BlockSpec((amount, 2, B), lambda step: (step, 0, 0))],
        out_specs=[tile_spec] * 4,
        out_shape=[whole, whole, whole, jax.ShapeDtypeStruct(grad.shape, jnp.bfloat16)],
        compiler_params=params(),
        cost_estimate=pl.CostEstimate(
            flops=slots * B * B * 30, bytes_accessed=slots * B * B * 30, transcendentals=slots * B * B
        ),
    )(clip_factor.reshape(1, 1), grad, master, first, second, bases)


def on_device(
    latents,
    noise,
    timesteps,
    labels,
    owners,
    tiles_low,
    tiles_master,
    tiles_first,
    tiles_second,
    bases,
    else_low,
    else_master,
    else_first,
    else_second,
):
    box = is_box()
    tp_parts = lax.axis_size("tp")
    tp_index = lax.axis_index("tp")
    ctx_parts = lax.axis_size("ctx")
    fsdp_parts = lax.axis_size("fsdp")
    images = latents.shape[0]
    local_len = latents.shape[1]
    slots = tiles_low.shape[1]
    sp_rows = images * local_len // tp_parts
    first_row = tp_index * sp_rows
    own = max(1, sp_rows // local_len)
    group = sp_rows // own
    first_image = first_row // local_len
    element_count = images * fsdp_parts * ctx_parts * local_len * P_SIZE
    ordering = jnp.argsort(owners, stable=True)
    inverse = jnp.argsort(ordering)
    all_tiles = inverse.shape[0]
    per_layer = all_tiles // L
    if box:
        early = early_slots(slots)
        me = lax.axis_index("fsdp") * ctx_parts + lax.axis_index("ctx")
        tile = jnp.arange(all_tiles, dtype=jnp.int32)
        owner, slot = inverse // slots, inverse % slots
        is_early = slot < early
        place_early = early_place(owner, slot, early)
        place_late = late_place(owner, slot - early, slots - early)
        gather_places = jnp.where(is_early, place_early, 16 * early + place_late)
        targets = store_of_tile(jnp.argsort(gather_places), tp_parts).astype(jnp.int32)
        is_stray = jnp.logical_not(is_early) & (tile < per_layer)
        stray_count = jnp.sum(is_stray.astype(jnp.int32))
        stray_rank = jnp.cumsum(is_stray.astype(jnp.int32)) - 1
        room = 16 * (slots - early)
        strays = jnp.argsort(jnp.where(is_stray, tile, all_tiles + tile)).astype(jnp.int32)
        strays = jnp.concatenate([strays, jnp.zeros((LOT,), jnp.int32)])
        places = jnp.where(
            is_stray,
            room + 16 * (early + 1) + stray_rank,
            jnp.where(is_early, room + early_place(owner, slot, early + 1), place_late),
        ).astype(jnp.int32)
        stores = [(0, per_layer + 1, None), (per_layer, per_layer + 1, None)]
        late_store = None

        def place_early_tiles(tile_group):
            nonlocal stores
            stores, token = place_call(tile_group, targets, stores)
            return token

        def place_late_tiles(tile_group):
            nonlocal late_store
            tile_group = [(piece, 16 * early + at) for piece, at in tile_group]
            if late_store is None:
                late_store = [stores[1]]
            late_store, token = place_call(tile_group, targets, late_store)
            return token

        late_store = None
        else_parts, finish_gather, arriving = gather_tiles(
            tiles_low[0], early, place_early_tiles, place_late_tiles, else_low, targets
        )
        store = [
            bring_strays(
                stores[0][2], strays, stray_count, tiles_low[0], inverse, slots, me, tp_parts
            ),
            None,
        ]
        held = [(0, room, None), (room, 16 * (slots + 1) + LOT, None)]
    else:
        places = jnp.arange(all_tiles, dtype=jnp.int32)
        tile_stored = jnp.argsort(store_of_tile(places, tp_parts))
        gathered = lax.all_gather(tiles_low, ("fsdp", "ctx"), axis=1, tiled=True)[0]
        gathered = gathered[inverse[tile_stored]]
        store = [gathered[:per_layer], gathered[per_layer:]]
        held = [(0, all_tiles, None)]
        else_parts = cut_else(lax.all_gather(else_low, ("fsdp", "ctx", "tp"), axis=0, tiled=True))
    (patch_weight, class_table, time_first, time_second), final_rows, head_weight = else_parts
    features_low = low(time_features(timesteps))
    onehot = low(labels[:, None] == jnp.arange(NCLS)[None, :])
    time_hidden = product(features_low, time_first)
    time_act = low(jax.nn.silu(time_hidden))
    condition = product(time_act, time_second) + product(onehot, class_table)
    cond_act = low(jax.nn.silu(condition))
    def modes_of(layer_no):
        return lax.dynamic_slice_in_dim(
            columns_in(modes_call(cond_act, store[layer_no], tp_parts)), first_image, own, 0
        ).reshape(own, 6, D)

    modes = [modes_of(0)]
    final_modes = lax.dynamic_slice_in_dim(
        final_product(cond_act, final_rows), first_image, own, 0
    )
    row_index = first_row + jnp.arange(sp_rows)
    signal = signal_level(timesteps)
    noisy_input = (
        jnp.sqrt(signal)[:, None, None] * latents + jnp.sqrt(1.0 - signal)[:, None, None] * noise
    )
    noisy_rows = low(
        lax.dynamic_slice_in_dim(
            noisy_input.reshape(images * local_len, P_SIZE), first_row, sp_rows, 0
        )
    )
    target = lax.dynamic_slice_in_dim(
        noise.reshape(images * local_len, P_SIZE), first_row, sp_rows, 0
    )
    stream = (product(noisy_rows, patch_weight) + position_table(row_index % local_len)).reshape(
        own, group, D
    )
    normed_in = modulate_call(stream, modes[0], 0, 1)
    kept = []
    for layer_no in range(L):
        row_sets = rows_in(normed_in.reshape(sp_rows, D))
        halves, terms = each_half(
            lambda rows: attend_call(rows, store[layer_no], tp_parts, local_len), row_sets
        )
        branch, middle, normed_mid = residual_call(
            stream,
            terms,
            modes[layer_no],
            2,
            modes[layer_no],
            3,
            4,
            arriving if box and layer_no == 0 else (),
        )
        mid_sets = rows_in(normed_mid.reshape(sp_rows, D))
        hidden, terms = each_half(
            lambda rows: mlp_call(rows, store[layer_no], tp_parts, local_len), mid_sets
        )
        last = layer_no == L - 1
        if not last:
            if box:
                finish_gather()
                store[1] = late_store[0][2]
            modes.append(modes_of(layer_no + 1))
        mlp_out, stream_new, normed_in = residual_call(
            middle,
            terms,
            modes[layer_no],
            5,
            final_modes if last else modes[layer_no + 1],
            0,
            1,
        )
        kept.append((stream, row_sets, halves, branch, middle, mid_sets, hidden, mlp_out))
        stream = stream_new
    head_low = normed_in.reshape(sp_rows, D)
    mismatch = product(head_low, head_weight) - target
    loss_part = jnp.sum(mismatch * mismatch) / element_count
    grad_pred = low(2.0 * mismatch / element_count)
    grad_head = over_rows(grad_pred, head_low)
    upstream, final_sums, grad_low = back_call(
        stream,
        [against(grad_pred, head_weight)],
        None,
        final_modes,
        1,
        (kept[-1][7], modes[-1], 5),
    )
    grad_final = final_sums[:, :2].reshape(own, 2 * D)
    gate_sum = final_sums[:, 2:]
    starts = [begin for _, begin in segments(tp_parts)]
    mode_width = 6 * D // tp_parts
    fill = (-3 * images) % 16
    conds = jnp.pad(jnp.concatenate([cond_act] * 3, 0), ((0, fill), (0, 0)))

    def all_images(values):
        return tp_sum(
            lax.dynamic_update_slice_in_dim(
                jnp.zeros((images, values.shape[1]), jnp.float32), values, first_image, 0
            )
        )

    grad_final = all_images(grad_final)
    cond_wide = wide(cond_act)

    def image_part(columns):
        packed = jnp.concatenate(columns, 1)
        packed = jnp.pad(packed, ((0, 0), (0, -packed.shape[1] % 256)))
        part = packed.shape[1] // 2
        return lax.dynamic_slice_in_dim(packed, tp_index * part, part, 1)

    label_column = jnp.broadcast_to(wide(labels)[:, None], (images, 128))
    early_columns = [label_column, wide(features_low), wide(time_act), cond_wide, grad_final]
    grad_cond_act = 0.0
    for layer_no in reversed(range(L)):
        stream, row_sets, halves, branch, middle, mid_sets, hidden, mlp_out = kept[layer_no]
        base = layer_no * per_layer
        grad_sets = rows_in(grad_low.reshape(sp_rows, D))
        results, terms = each_half(
            lambda pair: mlp_back_call(pair[0], pair[1], store[layer_no], tp_parts, local_len),
            [(rows, hidden_here[0]) for rows, hidden_here in zip(grad_sets, hidden)],
        )
        held = weight_grad_call(
            [result[0] for result in results], grad_sets, places, base + starts[3], held
        )
        held = weight_grad_call(
            mid_sets, [result[1] for result in results], places, base + starts[2], held
        )
        upstream, mlp_sums, grad_low = back_call(
            middle, terms, upstream, modes[layer_no], 4, (branch, modes[layer_no], 2)
        )
        if box and layer_no == 0:
            late_sums = scatter_late(
                late_parts,
                slots - early,
                lanes,
                late_first,
                tp_sum(grad_head),
                image_part(early_columns),
                upstream,
                grad_cond_early,
            )
        grad_sets = rows_in(grad_low.reshape(sp_rows, D))
        results, terms = each_half(
            lambda pair: attend_back_call(pair[0], pair[1], store[layer_no], tp_parts, local_len),
            [(rows, half[0]) for rows, half in zip(grad_sets, halves)],
        )
        held = weight_grad_call(
            [half[1] for half in halves], grad_sets, places, base + starts[1], held
        )
        held = weight_grad_call(
            row_sets, [result[0] for result in results], places, base + starts[0], held
        )
        below = None if layer_no == 0 else (kept[layer_no - 1][7], modes[layer_no - 1], 5)
        found = back_call(
            stream,
            terms,
            upstream,
            modes[layer_no],
            1,
            below,
            (late_sums[0][0],) if box and layer_no == 0 else (),
        )
        grad_modes = jnp.concatenate(
            [found[1][:, :2], mlp_sums[:, 2:], mlp_sums[:, :2], gate_sum], 1
        ).reshape(own, 6 * D)
        mode_image = lax.dynamic_slice_in_dim(
            all_images(grad_modes), tp_index * mode_width, mode_width, 1
        )
        held = weight_grad_call(
            [conds],
            [jnp.pad(three_parts(mode_image), ((0, fill), (0, 0)))],
            places,
            base + starts[4],
            held,
        )
        grad_cond_act = grad_cond_act + modes_back_call(mode_image, store[layer_no], tp_parts)
        upstream = found[0]
        if below:
            grad_low, gate_sum = found[2], found[1][:, 2:]
        if box and layer_no == L - 1:
            grad_low = after(grad_low, held[0][2], held[1][2])
            lanes = Lanes()
            late_parts = held[0][2]
            late_first = scatter_late_first(late_parts, slots - early, lanes)
            grad_cond_early = grad_cond_act
            held = held[1:]
    grad_patch = over_rows(noisy_rows, low(upstream).reshape(sp_rows, D))
    grad_cond_act = tp_sum(grad_cond_act) + final_product_back(grad_final, final_rows)
    grad_condition = jax.vjp(jax.nn.silu, condition)[1](grad_cond_act)[0]
    grad_time_hidden = jax.vjp(jax.nn.silu, time_hidden)[1](
        against_low(grad_condition, time_second)
    )[0]
    if box:
        patch_sum = tp_sum(grad_patch).reshape(1, B, B)
        patch_first = low(patch_sum)
        parts = lax.dynamic_update_slice_in_dim(
            held[0][2],
            jnp.where(tp_index == 0, patch_first, low(patch_sum - wide(patch_first))),
            early_place(0, early, early + 1),
            0,
        )
        owned, owned_late, late_images, head_sum, early_images = scatter_early(
            parts,
            early + 1,
            lanes,
            *late_sums,
            image_part([grad_time_hidden, grad_condition]),
        )
        late_images = columns_in(late_images)
        early_images = columns_in(early_images)
        head_rows = head_sum.T.reshape(P_SIZE, D)
        patch_rows = tp_sum(owned[early]).reshape(P_SIZE, D)
        owned = jnp.concatenate([owned[:early], owned_late], 0)
        owned = sum_strays(
            owned, parts[16 * (early + 1) :], strays, stray_count, inverse, slots, me
        )
    else:
        owned = lax.psum_scatter(
            wide(held[0][2])[ordering], ("fsdp", "ctx"), scatter_dimension=0, tiled=True
        )
        patch_rows = lax.psum(grad_patch, ("fsdp", "ctx", "tp"))
        head_rows = lax.psum(grad_head, ("fsdp", "ctx", "tp")).T.reshape(P_SIZE, D)
        late_images = gather_images(jnp.concatenate([grad_time_hidden, grad_condition], 1))
        early_images = gather_images(jnp.concatenate(early_columns, 1))
    all_hidden, all_condition = jnp.split(late_images, 2, 1)
    cuts = [128]
    for length in (TFREQ, D, D):
        cuts.append(cuts[-1] + length)
    all_labels, all_features, all_time, all_cond, all_final = jnp.split(early_images, cuts, 1)
    all_final = all_final[:, : 2 * D]
    all_onehot = wide(all_labels[:, :1] == jnp.arange(NCLS, dtype=jnp.float32)[None, :])
    share = else_low.shape[0]
    device = (lax.axis_index("fsdp") * ctx_parts + lax.axis_index("ctx")) * tp_parts + tp_index
    begin = device * share
    row_total = else_low.shape[0] * fsdp_parts * ctx_parts * tp_parts // D
    row_count = min(share // D + 2, row_total)
    begin_row = jnp.minimum(begin // D, row_total - row_count)
    row_ids = begin_row + jnp.arange(row_count)
    edge = jnp.zeros((all_cond.shape[0], P_SIZE), jnp.float32)
    factors = jnp.concatenate(
        [edge, all_onehot, all_features, all_time, jnp.repeat(all_cond, 2, axis=1), edge], 1
    )
    factors = lax.dynamic_slice_in_dim(factors, begin_row, row_count, 1)
    first_start = P_SIZE + NCLS
    second_start = first_start + TFREQ
    final_start = second_start + D

    def rows_of(chosen, right):
        return contract("ic,id->cd", jnp.where(chosen[None, :], factors, 0.0), right)

    in_first = (row_ids >= first_start) & (row_ids < second_start)
    in_final = row_ids >= final_start
    odd = (row_ids - final_start) % 2 == 1
    near = rows_of(in_first, all_hidden)
    near = near + rows_of(jnp.logical_not(in_first | in_final), all_condition)
    near = near + rows_of(in_final & jnp.logical_not(odd), all_final[:, :D])
    near = near + rows_of(in_final & odd, all_final[:, D:])
    for begin_here, token_rows in ((0, patch_rows), (row_total - P_SIZE, head_rows)):
        here = row_ids - begin_here
        inside = (here >= 0) & (here < P_SIZE)
        near = jnp.where(
            inside[:, None], token_rows[jnp.clip(here, 0, P_SIZE - 1)], near
        )
    else_grad = lax.dynamic_slice_in_dim(near.reshape(-1), begin - begin_row * D, share, 0)
    squares = jnp.sum(owned * owned) + jnp.sum(else_grad * else_grad)
    totals = total(jnp.stack([loss_part, squares]))
    loss_total = totals[0]
    grad_norm = jnp.sqrt(totals[1])
    clip_factor = jnp.minimum(1.0, 1.0 / grad_norm)
    master_new, first_new, second_new, low_new = update_tiles(
        clip_factor, owned, tiles_master[0], tiles_first[0], tiles_second[0], bases[0]
    )
    else_master_new, else_first_new, else_second_new = adamw_flat(
        clip_factor * else_grad, else_master, else_first, else_second
    )
    return (
        loss_total,
        grad_norm,
        master_new[None],
        first_new[None],
        second_new[None],
        low_new[None],
        else_master_new,
        else_first_new,
        else_second_new,
        low(else_master_new),
    )


def solution(mesh):
    return jax.shard_map(
        on_device,
        mesh=mesh,
        in_specs=(
            P(("fsdp", "ctx"), None, None),
            P(("fsdp", "ctx"), None, None),
            P(("fsdp", "ctx")),
            P(("fsdp", "ctx")),
            P(),
            P("tp", ("fsdp", "ctx"), None, None),
            P("tp", ("fsdp", "ctx"), None, None),
            P("tp", ("fsdp", "ctx"), None, None),
            P("tp", ("fsdp", "ctx"), None, None),
            P("tp", ("fsdp", "ctx"), None, None),
            P(("fsdp", "ctx", "tp")),
            P(("fsdp", "ctx", "tp")),
            P(("fsdp", "ctx", "tp")),
            P(("fsdp", "ctx", "tp")),
        ),
        out_specs=(
            P(),
            P(),
            P("tp", ("fsdp", "ctx"), None, None),
            P("tp", ("fsdp", "ctx"), None, None),
            P("tp", ("fsdp", "ctx"), None, None),
            P("tp", ("fsdp", "ctx"), None, None),
            P(("fsdp", "ctx", "tp")),
            P(("fsdp", "ctx", "tp")),
            P(("fsdp", "ctx", "tp")),
            P(("fsdp", "ctx", "tp")),
        ),
        check_vma=False,
    )
```

```python
import math

import jax
import jax.numpy as jnp
from jax import lax
from jax.experimental import pallas as pl
from jax.experimental.pallas import tpu as pltpu
from jax.sharding import PartitionSpec as P

D = 1024
HD = 64
F = 4096
P_SIZE = 16
TFREQ = 256
NCLS = 1000
GRID = 16
L = 2
B = 128


HIGHEST = lax.Precision.HIGHEST
EPS_NORM = 1e-06
RATE = 0.02
DECAY = 0.1


def matmul(left_op, right_op):
    return jnp.dot(left_op, right_op, precision=HIGHEST)


def contract(formula, left_op, right_op):
    return jnp.einsum(formula, left_op, right_op, precision=HIGHEST)


def product(left_op, right_op):
    return jnp.dot(left_op, right_op, preferred_element_type=jnp.float32)


def over_rows(left_op, right_op):
    return lax.dot_general(
        left_op, right_op, (((0,), (0,)), ((), ())), preferred_element_type=jnp.float32
    )


def against(left_op, right_op):
    return lax.dot_general(
        left_op, right_op, (((1,), (1,)), ((), ())), preferred_element_type=jnp.float32
    )


def normed(stream):
    centred = stream - jnp.mean(stream, -1, keepdims=True)
    return centred * lax.rsqrt(jnp.mean(centred * centred, -1, keepdims=True) + EPS_NORM)


def modulate(stream, offset, factor):
    return normed(stream) * (1.0 + factor) + offset


def gelu_tanh(values):
    return jax.nn.gelu(values, approximate=True)


def time_features(time_steps):
    half_count = TFREQ // 2
    freqs = jnp.exp(-math.log(10000.0) * jnp.arange(half_count, dtype=jnp.float32) / half_count)
    angles = time_steps.astype(jnp.float32)[:, None] * freqs[None, :]
    return jnp.concatenate([jnp.cos(angles), jnp.sin(angles)], -1)


def position_table(token_ids):
    quarter = D // 4
    omegas = 1.0 / 10000.0 ** (jnp.arange(quarter, dtype=jnp.float32) / quarter)
    row_angle = (token_ids // GRID).astype(jnp.float32)[:, None] * omegas[None, :]
    col_angle = (token_ids % GRID).astype(jnp.float32)[:, None] * omegas[None, :]
    return jnp.concatenate(
        [jnp.sin(row_angle), jnp.cos(row_angle), jnp.sin(col_angle), jnp.cos(col_angle)], -1
    )


def signal_level(time_steps):
    phase = (time_steps.astype(jnp.float32) / 1000.0 + 0.008) / 1.008 * (math.pi / 2)
    return jnp.cos(phase) ** 2


def shard_shapes(tp_parts):
    head_width = D // tp_parts
    hidden_width = F // tp_parts
    return [
        (D, 3 * head_width),
        (head_width, D),
        (D, hidden_width),
        (hidden_width, D),
        (D, 6 * head_width),
    ]


def untile(tile_set, height, breadth):
    block = tile_set.shape[-1]
    return (
        tile_set.reshape(height // block, breadth // block, block, block)
        .transpose(0, 2, 1, 3)
        .reshape(height, breadth)
    )


def retile(matrix):
    height, breadth = matrix.shape
    return matrix.reshape(height // B, B, breadth // B, B).transpose(0, 2, 1, 3).reshape(-1, B, B)


def unpack_layers(tile_set, tp_parts):
    layer_list = []
    cursor = 0
    for layer_no in range(L):
        matrices = []
        for height, breadth in shard_shapes(tp_parts):
            amount = height * breadth // (B * B)
            matrices.append(untile(tile_set[cursor : cursor + amount], height, breadth))
            cursor += amount
        layer_list.append(matrices)
    return layer_list


def pack_layers(layer_list):
    return jnp.concatenate([retile(matrix) for matrices in layer_list for matrix in matrices], 0)


def else_shapes():
    return [(P_SIZE, D), (NCLS, D), (TFREQ, D), (D, D), (D, 2 * D), (D, P_SIZE)]


def split_else(flat_params):
    components = []
    cursor = 0
    for height, breadth in else_shapes():
        components.append(flat_params[cursor : cursor + height * breadth].reshape(height, breadth))
        cursor += height * breadth
    return components


def reflection(vectors):
    outer_prod = vectors[..., :, None] * vectors[..., None, :]
    return (
        jnp.eye(vectors.shape[-1], dtype=jnp.float32)
        - 2.0 * outer_prod / jnp.sum(vectors * vectors, -1)[..., None, None]
    )


def rotate(left_basis, middle, right_basis):
    return contract(
        "...ab,...bc->...ac", contract("...ab,...bc->...ac", left_basis, middle), right_basis
    )


def adam_finish(turned, master_state, first_state, second_state, left_basis, right_basis):
    first_new = 0.5 * first_state + 0.5 * turned
    second_new = 0.5 * second_state + 0.5 * turned * turned
    direction = first_new / (jnp.sqrt(second_new) + 1e-08)
    return (master_state - RATE * rotate(left_basis, direction, right_basis), first_new, second_new)


def adamw_flat(grad_clipped, master_state, first_state, second_state):
    first_new = 0.5 * first_state + 0.5 * grad_clipped
    second_new = 0.5 * second_state + 0.5 * grad_clipped * grad_clipped
    master_new = master_state - RATE * (
        first_new / (jnp.sqrt(second_new) + 1e-08) + DECAY * master_state
    )
    return (master_new, first_new, second_new)


def is_box():
    return (lax.axis_size("fsdp"), lax.axis_size("ctx"), lax.axis_size("tp")) == (8, 2, 2)


def swap_tp(value):
    return lax.ppermute(value, "tp", [(0, 1), (1, 0)])


def swap_y(value):
    return lax.ppermute(value, "ctx", [(0, 1), (1, 0)])


def swap_f(value, bit):
    return lax.ppermute(value, "fsdp", [(place, place ^ bit) for place in range(8)])


def swap_x(value):
    return swap_f(value, 1)


def place_z():
    return lax.axis_index("fsdp") // 2


def low(value):
    return value.astype(jnp.bfloat16)


def wide(value):
    return value.astype(jnp.float32)


def after(value, *earlier):
    return lax.optimization_barrier((value, *earlier))[0]


class Lanes:
    def __init__(self):
        self.done = ()

    def step(self, sends, *earlier):
        values = lax.optimization_barrier(tuple(value for _, value in sends) + self.done + earlier)
        self.done = tuple(swap(value) for (swap, _), value in zip(sends, values))
        return list(self.done)


def move_z(step, sources):
    pairs = [(2 * z + x, 2 * (z + step) + x) for z in sources for x in range(2)]
    return lambda value: lax.ppermute(value, "fsdp", pairs)


def to_z(rel):
    return lambda value: swap_f(value, 2 * rel)


class ZLine:
    def __init__(self, own):
        self.above, self.below = [own], [own]

    def sends(self):
        hop = len(self.above)
        return [
            (move_z(1, range(hop - 1, 3)), self.above[-1]),
            (move_z(-1, range(1, 5 - hop)), self.below[-1]),
        ]

    def take(self, arrived):
        self.above.append(arrived[0])
        self.below.append(arrived[1])

    def block(self, rel, token=None):
        z = place_z()
        if token is not None:
            z = z + token[0, 0]
        above, below = self.above, self.below
        if rel == 0:
            return above[0]
        if rel == 1:
            return jnp.where(z % 2 == 1, above[1], below[1])
        if rel == 2:
            return jnp.where(z >= 2, above[2], below[2])
        return jnp.where(
            z == 0, below[3], jnp.where(z == 3, above[3], jnp.where(z == 1, below[1], above[1]))
        )


class ZSum:
    def __init__(self):
        self.last = None
        self.up = self.down = None

    def sends(self, rel, block):
        z = place_z()
        if rel == 3:
            self.last = block
            up, down = block, block
        elif rel == 2:
            up, down = block + self.up, block + self.down
        else:
            up = jnp.where(z == 1, self.last, block) + self.up
            down = jnp.where(z == 2, self.last, block) + self.down
        return [
            (move_z(1, range(0, 4 - rel)), low(up)),
            (move_z(-1, range(rel, 4)), low(down)),
        ]

    def take(self, arrived):
        self.up, self.down = arrived

    def total(self, block):
        return block + self.up + self.down


def early_slots(slots):
    return slots - slots * 25 // 72


def gather_tiles(own, early, place_early, place_late, else_low, targets):
    half = early // 2
    lanes = Lanes()
    line, late_line = ZLine(own[:early]), ZLine(own[early:])
    rest = whole = None
    tokens = []
    for rel in range(4):
        block = line.block(rel, tokens[rel - 2] if rel >= 2 else None)
        sends = [(swap_x, block), (swap_y, block)]
        waits = ()
        if rel == 3:
            waits = rest[0]
        going = line if rel < 3 else late_line
        sends += going.sends()
        if rel == 1:
            by_x, by_y, above, below, *both = lanes.step(sends + else_diagonal)
            whole = finish_else(else_line, both)
            rest = cut_else(whole)
        else:
            by_x, by_y, above, below = lanes.step(sends, *waits)
        going.take((above, below))
        sends = [(swap_y, by_x[:half]), (swap_x, by_y[half:])]
        if rel == 0:
            first, second, *arrived = lanes.step(
                sends + [(to_z(other), else_low.reshape(1, -1, 128)) for other in (1, 2, 3)],
                targets,
            )
            else_line, else_diagonal = start_else(else_low, lanes, arrived)
        elif rel < 3:
            first, second, *arrived = lanes.step(sends + late_line.sends())
            late_line.take(arrived)
        else:
            first, second = lanes.step(sends)
        at = 4 * rel * early
        group = [
            (block, at),
            (by_y, at + early),
            (by_x, at + 2 * early),
            (first, at + 3 * early),
            (second, at + 3 * early + half),
        ]
        earlier = ()
        if rel == 3:
            late = jnp.concatenate([late_line.block(other) for other in range(4)], 0)
            earlier = (late,)
        tokens.append(place_early(group, *earlier))
    line = late
    count = line.shape[0]
    half = count // 2
    by_x, by_y = lanes.step([(swap_x, line), (swap_y, line)])
    place_late([(line, 0)])

    def finish(*earlier):
        first, second = lanes.step([(swap_y, by_x[:half]), (swap_x, by_y[half:])])
        place_late([(by_y, count), (by_x, 2 * count)])
        place_late([(first, 3 * count), (second, 3 * count + half)], *earlier)

    return rest, finish, (by_x, by_y)


def relative(owner):
    rel_f = jnp.bitwise_xor(owner // 2, lax.axis_index("fsdp"))
    return rel_f // 2, rel_f % 2, jnp.bitwise_xor(owner % 2, lax.axis_index("ctx"))


def early_place(owner, slot, slots):
    rel_z, rel_x, rel_y = relative(owner)
    return ((rel_z * 2 + rel_x) * 2 + rel_y) * slots + slot


def late_place(owner, slot, slots):
    rel_z, rel_x, rel_y = relative(owner)
    return ((rel_x * 2 + rel_y) * 4 + rel_z) * slots + slot


def scatter_late_first(parts, slots, lanes):
    both = parts[12 * slots :]
    return lanes.step([(swap_y, both[: 2 * slots]), (swap_x, both[2 * slots :])])


def scatter_late(parts, slots, lanes, wait, head_sum, images_part, *earlier):
    count = 4 * slots
    half = count // 2
    keep, to_y, to_x, _ = (parts[part * count : (part + 1) * count] for part in range(4))
    by_y, by_x = wait
    to_x = jnp.concatenate([low(wide(to_x[:half]) + by_y), to_x[half:]], 0)
    to_y = jnp.concatenate([to_y[:half], low(wide(to_y[half:]) + by_x)], 0)
    from_x, from_y, head_y, *images = lanes.step(
        [(swap_x, to_x), (swap_y, to_y), (swap_y, head_sum)]
        + [(to_z(rel), images_part) for rel in (1, 2, 3)],
        *earlier,
    )
    keep = wide(keep) + from_x + from_y
    return (
        [keep[rel * slots : (rel + 1) * slots] for rel in range(4)],
        head_sum + head_y,
        jnp.concatenate([images_part] + images, 0),
    )


def scatter_early(parts, slots, lanes, late, head_sum, early_images, images_part):
    half = slots // 2

    def block(part, begin, end):
        return parts[part * slots + begin : part * slots + end]

    def diagonal(rel):
        return [
            (swap_y, block(4 * rel + 3, 0, half)),
            (swap_x, block(4 * rel + 3, half, slots)),
        ]

    def sides(rel, arrived):
        by_y, by_x = arrived
        return [
            (
                swap_x,
                jnp.concatenate(
                    [
                        low(wide(block(4 * rel + 2, 0, half)) + by_y),
                        block(4 * rel + 2, half, slots),
                    ],
                    0,
                ),
            ),
            (
                swap_y,
                jnp.concatenate(
                    [
                        block(4 * rel + 1, 0, half),
                        low(wide(block(4 * rel + 1, half, slots)) + by_x),
                    ],
                    0,
                ),
            ),
        ]

    def kept(rel, arrived):
        return wide(block(4 * rel, 0, slots)) + arrived[0] + arrived[1]

    line, late_line = ZSum(), ZSum()
    arrived = lanes.step(
        diagonal(3) + late_line.sends(3, late[3]) + [(swap_x, head_sum), (swap_y, early_images)]
    )
    diagonal_3 = arrived[:2]
    late_line.take(arrived[2:4])
    head_sum = head_sum + arrived[4]
    early_images = jnp.concatenate([early_images, arrived[5]], 0)
    arrived = lanes.step(
        diagonal(2) + late_line.sends(2, late[2]) + [(to_z(1), head_sum), (swap_x, early_images)]
    )
    diagonal_2 = arrived[:2]
    late_line.take(arrived[2:4])
    head_sum = head_sum + arrived[4]
    early_images = jnp.concatenate([early_images, arrived[5]], 0)
    arrived = lanes.step(sides(3, diagonal_3) + late_line.sends(1, late[1]))
    late_line.take(arrived[2:])
    owned_late = late_line.total(late[0])
    kept_3 = kept(3, arrived)
    arrived = lanes.step(
        diagonal(1) + [(to_z(rel), images_part) for rel in (1, 2, 3)] + [(to_z(2), head_sum)]
    )
    diagonal_1 = arrived[:2]
    images = jnp.concatenate([images_part] + arrived[2:5], 0)
    head_sum = head_sum + arrived[5]
    arrived = lanes.step(sides(2, diagonal_2) + line.sends(3, kept_3) + [(swap_y, images)])
    line.take(arrived[2:4])
    kept_2 = kept(2, arrived)
    images = jnp.concatenate([images, arrived[4]], 0)
    arrived = lanes.step(diagonal(0) + [(swap_x, images)])
    diagonal_0 = arrived[:2]
    images = jnp.concatenate([images, arrived[2]], 0)
    arrived = lanes.step(sides(1, diagonal_1) + line.sends(2, kept_2))
    line.take(arrived[2:4])
    arrived_0 = lanes.step(sides(0, diagonal_0) + line.sends(1, kept(1, arrived)))
    line.take(arrived_0[2:4])
    return line.total(kept(0, arrived_0)), owned_late, images, head_sum, early_images


def gather_images(value):
    if not is_box():
        return lax.all_gather(value, ("fsdp", "ctx"), axis=0, tiled=True)
    value = jnp.concatenate([value] + [swap_f(value, 2 * rel) for rel in (1, 2, 3)], 0)
    by_x, by_y = swap_x(value), swap_y(value)
    return jnp.concatenate([value, by_y, by_x, swap_x(by_y)], 0)


def start_else(flat, lanes, arrived):
    z = place_z()
    line = [flat.reshape(1, -1, 128)] + arrived
    line = [
        jnp.where(
            z == place,
            line[0],
            jnp.where(z == place ^ 1, line[1], jnp.where(z == place ^ 2, line[2], line[3])),
        )
        for place in range(4)
    ]
    line = jnp.concatenate(line, 0)
    by_x, by_y = lanes.step([(swap_x, line), (swap_y, line)])
    half = line.shape[1] // 2
    return (line, by_x, by_y), [(swap_y, by_x[:, :half]), (swap_x, by_y[:, half:])]


def finish_else(lines, both):
    x, y, core = lax.axis_index("fsdp") % 2, lax.axis_index("ctx"), lax.axis_index("tp")
    line, by_x, by_y = lines
    both = jnp.concatenate(both, 1)
    y_low = [jnp.where(y == 0, line, by_y), jnp.where(y == 0, by_x, both)]
    y_high = [jnp.where(y == 0, by_y, line), jnp.where(y == 0, both, by_x)]
    chip = jnp.stack(
        [
            jnp.stack([jnp.where(x == 0, y_low[0], y_low[1]), jnp.where(x == 0, y_high[0], y_high[1])], 1),
            jnp.stack([jnp.where(x == 0, y_low[1], y_low[0]), jnp.where(x == 0, y_high[1], y_high[0])], 1),
        ],
        1,
    )
    other = swap_tp(chip)
    return jnp.stack(
        [jnp.where(core == 0, chip, other), jnp.where(core == 0, other, chip)], 3
    )


def cut_else(whole):
    rows = whole.reshape(-1, D)
    counts = [P_SIZE, NCLS, TFREQ, D, 2 * D, P_SIZE]
    ends = [sum(counts[: place + 1]) for place in range(6)]
    parts = [rows[end - count : end] for end, count in zip(ends, counts)]
    return tuple(parts[:4]), parts[4], parts[5].reshape(D, P_SIZE)


def final_product(left_op, final_rows):
    rows = left_op.shape[0]
    nothing = jnp.zeros_like(left_op)
    spread = jnp.concatenate(
        [
            jnp.stack([left_op, nothing], -1).reshape(rows, 2 * D),
            jnp.stack([nothing, left_op], -1).reshape(rows, 2 * D),
        ],
        0,
    )
    found = product(spread, final_rows)
    return jnp.stack([found[:rows], found[rows:]], 1)


def final_product_back(grads, final_rows):
    rows = grads.shape[0]
    found = against_low(jnp.concatenate([grads[:, :D], grads[:, D:]], 0), final_rows)
    return found[:rows].reshape(rows, D, 2)[:, :, 0] + found[rows:].reshape(rows, D, 2)[:, :, 1]


def total(value):
    if not is_box():
        return lax.psum(value, ("fsdp", "ctx", "tp"))
    value = value + swap_tp(value)
    value = value + swap_y(value)
    for bit in (1, 2, 4):
        value = value + swap_f(value, bit)
    return value


def tp_sum(value):
    if lax.axis_size("tp") == 2:
        return value + swap_tp(value)
    return lax.psum(value, "tp")


def columns_in(value):
    if lax.axis_size("tp") == 2:
        other = swap_tp(value)
        at_zero = lax.axis_index("tp") == 0
        return jnp.concatenate(
            [jnp.where(at_zero, value, other), jnp.where(at_zero, other, value)], -1
        )
    return lax.all_gather(value, "tp", axis=value.ndim - 1, tiled=True)


def rows_in(value_low):
    if lax.axis_size("tp") == 2:
        return [value_low, swap_tp(value_low)]
    return [lax.all_gather(value_low, "tp", axis=0, tiled=True)]


def each_half(work, row_sets):
    if len(row_sets) == 2:
        other = work(row_sets[1])
        sent = swap_tp(other[-1])
        own = work(row_sets[0])
        return [own[:-1], other[:-1]], [own[-1], sent]
    whole = work(row_sets[0])
    return [whole[:-1]], [lax.psum_scatter(whole[-1], "tp", scatter_dimension=0, tiled=True)]


BIG = 56 * 1024 * 1024


def against_value(left_op, right_op):
    return lax.dot_general(
        left_op, right_op, (((1,), (1,)), ((), ())), preferred_element_type=jnp.float32
    )


def untile_into(matrix, tile_set):
    rows, columns = matrix.shape[0] // B, matrix.shape[1] // B
    for row in range(rows):
        for column in range(columns):
            matrix[row * B : (row + 1) * B, column * B : (column + 1) * B] = tile_set[
                row * columns + column
            ]


def segments(tp_parts):
    found = []
    begin = 0
    for height, breadth in shard_shapes(tp_parts):
        amount = height * breadth // (B * B)
        found.append((amount, begin))
        begin += amount
    return found


def weight_spec(kind, tp_parts):
    amount, begin = segments(tp_parts)[kind]
    return pl.BlockSpec(
        (amount, B, B), lambda *step: (begin // amount, 0, 0), pipeline_mode=pl.Buffered(1)
    )


def rows_spec(rows, breadth):
    return pl.BlockSpec((rows, breadth), lambda step: (step, 0))


def shaped(rows, breadth, kind):
    return jax.ShapeDtypeStruct((rows, breadth), kind)


def params():
    return pltpu.CompilerParams(vmem_limit_bytes=BIG)


def attend_kernel(normed_in, qkv_tiles, proj_tiles, *refs):
    projected, attended, partial, w_qkv, w_proj = refs[-5:]

    @pl.when(pl.program_id(0) == 0)
    def _():
        untile_into(w_qkv, qkv_tiles)
        untile_into(w_proj, proj_tiles)

    values = low(product(normed_in[...], w_qkv[...]))
    projected[...] = values
    width = values.shape[1] // 3
    results = []
    for head in range(width // HD):
        at = head * HD
        query = values[:, at : at + HD]
        key_rows = values[:, width + at : width + at + HD]
        value_rows = values[:, 2 * width + at : 2 * width + at + HD]
        scores = against_value(key_rows, query) * HD ** (-0.5)
        exponent = jnp.exp(scores - jnp.max(scores, 0, keepdims=True))
        probabilities = low(exponent / jnp.sum(exponent, 0, keepdims=True))
        results.append(low(over_rows(probabilities, value_rows)))
    result = jnp.concatenate(results, 1)
    attended[...] = result
    partial[...] = product(result, w_proj[...])


def attend_call(normed_in, store, tp_parts, local_len, earlier=()):
    rows = normed_in.shape[0]
    width = D // tp_parts
    return pl.pallas_call(
        attend_kernel,
        grid=(rows // local_len,),
        in_specs=[
            rows_spec(local_len, D),
            weight_spec(0, tp_parts),
            weight_spec(1, tp_parts),
        ]
        + [pl.BlockSpec(memory_space=pl.ANY)] * len(earlier),
        out_specs=[
            rows_spec(local_len, 3 * width),
            rows_spec(local_len, width),
            rows_spec(local_len, D),
        ],
        out_shape=[
            shaped(rows, 3 * width, jnp.bfloat16),
            shaped(rows, width, jnp.bfloat16),
            shaped(rows, D, jnp.float32),
        ],
        scratch_shapes=[
            pltpu.VMEM((D, 3 * width), jnp.bfloat16),
            pltpu.VMEM((width, D), jnp.bfloat16),
        ],
        compiler_params=params(),
        cost_estimate=pl.CostEstimate(
            flops=rows * D * width * 8, bytes_accessed=rows * D * 8, transcendentals=rows * 2048
        ),
    )(normed_in, store, store, *earlier)


def attend_back_kernel(
    grad_branch, projected, qkv_tiles, proj_tiles, grad_qkv, partial, w_qkv, w_proj
):
    @pl.when(pl.program_id(0) == 0)
    def _():
        untile_into(w_qkv, qkv_tiles)
        untile_into(w_proj, proj_tiles)

    grad_attended = low(against_value(grad_branch[...], w_proj[...]))
    values = projected[...]
    width = values.shape[1] // 3
    grads = [[], [], []]
    for head in range(width // HD):
        at = head * HD
        query = values[:, at : at + HD]
        key_rows = values[:, width + at : width + at + HD]
        value_rows = values[:, 2 * width + at : 2 * width + at + HD]
        grad_here = grad_attended[:, at : at + HD]
        scores = against_value(key_rows, query) * HD ** (-0.5)
        exponent = jnp.exp(scores - jnp.max(scores, 0, keepdims=True))
        probabilities = exponent / jnp.sum(exponent, 0, keepdims=True)
        grad_prob = against_value(value_rows, grad_here)
        grad_scores = low(
            probabilities
            * (grad_prob - jnp.sum(probabilities * grad_prob, 0, keepdims=True))
        )
        grads[0].append(low(over_rows(grad_scores, key_rows) * HD ** (-0.5)))
        grads[1].append(low(product(grad_scores, query) * HD ** (-0.5)))
        grads[2].append(low(product(low(probabilities), grad_here)))
    result = jnp.concatenate(grads[0] + grads[1] + grads[2], 1)
    grad_qkv[...] = result
    partial[...] = against_value(result, w_qkv[...])


def attend_back_call(grad_branch, projected, store, tp_parts, local_len):
    rows = grad_branch.shape[0]
    width = D // tp_parts
    return pl.pallas_call(
        attend_back_kernel,
        grid=(rows // local_len,),
        in_specs=[
            rows_spec(local_len, D),
            rows_spec(local_len, 3 * width),
            weight_spec(0, tp_parts),
            weight_spec(1, tp_parts),
        ],
        out_specs=[rows_spec(local_len, 3 * width), rows_spec(local_len, D)],
        out_shape=[shaped(rows, 3 * width, jnp.bfloat16), shaped(rows, D, jnp.float32)],
        scratch_shapes=[
            pltpu.VMEM((D, 3 * width), jnp.bfloat16),
            pltpu.VMEM((width, D), jnp.bfloat16),
        ],
        compiler_params=params(),
        cost_estimate=pl.CostEstimate(
            flops=rows * D * width * 10, bytes_accessed=rows * D * 8, transcendentals=rows * 2048
        ),
    )(grad_branch, projected, store, store)


def mlp_chunk(tp_parts):
    return min(4 * B, F // tp_parts)


def chunk_specs(tp_parts):
    amount = D * mlp_chunk(tp_parts) // (B * B)
    up, down = (segments(tp_parts)[kind][1] // amount for kind in (2, 3))
    return [
        pl.BlockSpec((amount, B, B), lambda step: (up + step, 0, 0)),
        pl.BlockSpec((amount, B, B), lambda step: (down + step, 0, 0)),
    ]


def store_of_tile(tile, tp_parts):
    amount, begin = segments(tp_parts)[2]
    within = tile % sum(count for count, _ in segments(tp_parts)) - begin
    columns, wide_step = F // tp_parts // B, mlp_chunk(tp_parts) // B
    row, column = within // columns, within % columns
    moved = (column // wide_step * (D // B) + row) * wide_step + column % wide_step
    return jnp.where((within >= 0) & (within < amount), tile + moved - within, tile)


def add_to(total_ref, value):
    @pl.when(pl.program_id(0) == 0)
    def _():
        total_ref[...] = value

    @pl.when(pl.program_id(0) > 0)
    def _():
        total_ref[...] += value


def mlp_kernel(normed_mid, up_tiles, down_tiles, hidden, partial, w_up, w_down):
    untile_into(w_up, up_tiles)
    untile_into(w_down, down_tiles)
    values = product(normed_mid[...], w_up[...])
    hidden[...] = values
    add_to(partial, product(low(gelu_tanh(values)), w_down[...]))


def chunk_scratch(tp_parts):
    width = mlp_chunk(tp_parts)
    return [pltpu.VMEM((D, width), jnp.bfloat16), pltpu.VMEM((width, D), jnp.bfloat16)]


def all_rows(rows):
    return pl.BlockSpec((rows, D), lambda step: (0, 0))


def mlp_call(normed_mid, store, tp_parts, local_len):
    rows = normed_mid.shape[0]
    width, step_width = F // tp_parts, mlp_chunk(tp_parts)
    step_spec = pl.BlockSpec((rows, step_width), lambda step: (0, step))
    return pl.pallas_call(
        mlp_kernel,
        grid=(width // step_width,),
        in_specs=[all_rows(rows)] + chunk_specs(tp_parts),
        out_specs=[step_spec, all_rows(rows)],
        out_shape=[shaped(rows, width, jnp.float32), shaped(rows, D, jnp.float32)],
        scratch_shapes=chunk_scratch(tp_parts),
        compiler_params=params(),
        cost_estimate=pl.CostEstimate(
            flops=rows * D * width * 4,
            bytes_accessed=rows * D * 12 + 4 * D * width,
            transcendentals=rows * width,
        ),
    )(normed_mid, store, store)


def mlp_back_kernel(
    grad_mlp, hidden, up_tiles, down_tiles, activation, grad_hidden, partial, w_up, w_down
):
    untile_into(w_up, up_tiles)
    untile_into(w_down, down_tiles)
    values = hidden[...]
    factor = math.sqrt(2.0 / math.pi)
    square = values * values
    bent = jnp.tanh(factor * (values + 0.044715 * (square * values)))
    half_up = 0.5 * (1.0 + bent)
    activation[...] = low(values * half_up)
    slope = half_up + 0.5 * values * (1.0 - bent * bent) * (
        factor * (1.0 + 3.0 * 0.044715 * square)
    )
    grad = low(against_value(grad_mlp[...], w_down[...]) * slope)
    grad_hidden[...] = grad
    add_to(partial, against_value(grad, w_up[...]))


def mlp_back_call(grad_mlp, hidden, store, tp_parts, local_len):
    rows = grad_mlp.shape[0]
    width, step_width = F // tp_parts, mlp_chunk(tp_parts)
    step_spec = pl.BlockSpec((rows, step_width), lambda step: (0, step))
    return pl.pallas_call(
        mlp_back_kernel,
        grid=(width // step_width,),
        in_specs=[all_rows(rows), step_spec] + chunk_specs(tp_parts),
        out_specs=[step_spec, step_spec, all_rows(rows)],
        out_shape=[
            shaped(rows, width, jnp.bfloat16),
            shaped(rows, width, jnp.bfloat16),
            shaped(rows, D, jnp.float32),
        ],
        scratch_shapes=chunk_scratch(tp_parts),
        compiler_params=params(),
        cost_estimate=pl.CostEstimate(
            flops=rows * D * width * 4,
            bytes_accessed=rows * D * 16 + 4 * D * width,
            transcendentals=rows * width,
        ),
    )(grad_mlp, hidden, store, store)


def modes_call(cond_act, store, tp_parts):
    rows = cond_act.shape[0]
    width = 6 * D // tp_parts

    def kernel(left, tile_set, out):
        for column in range(width // B):
            total_here = 0.0
            for row in range(D // B):
                total_here = total_here + product(
                    left[:, row * B : (row + 1) * B], tile_set[row * (width // B) + column]
                )
            out[:, column * B : (column + 1) * B] = total_here

    return pl.pallas_call(
        kernel,
        grid=(1,),
        in_specs=[rows_spec(rows, D), weight_spec(4, tp_parts)],
        out_specs=rows_spec(rows, width),
        out_shape=shaped(rows, width, jnp.float32),
        compiler_params=params(),
    )(cond_act, store)


def three_parts(value):
    first = low(value)
    rest = value - wide(first)
    second = low(rest)
    return jnp.concatenate([first, second, low(rest - wide(second))], 0)


def against_low(value, weight):
    rows = value.shape[0]
    summed = against(three_parts(value), weight)
    return summed[:rows] + summed[rows : 2 * rows] + summed[2 * rows :]


def modes_back_call(grads, store, tp_parts):
    rows = grads.shape[0]
    width = 6 * D // tp_parts
    parts = three_parts(grads)

    def kernel(left, tile_set, out):
        for row in range(D // B):
            total_here = 0.0
            for column in range(width // B):
                total_here = total_here + against_value(
                    left[:, column * B : (column + 1) * B],
                    tile_set[row * (width // B) + column],
                )
            out[:, row * B : (row + 1) * B] = total_here

    summed = pl.pallas_call(
        kernel,
        grid=(1,),
        in_specs=[rows_spec(3 * rows, width), weight_spec(4, tp_parts)],
        out_specs=rows_spec(3 * rows, D),
        out_shape=shaped(3 * rows, D, jnp.float32),
        compiler_params=params(),
    )(parts, store)
    return summed[:rows] + summed[rows : 2 * rows] + summed[2 * rows :]


def weight_grad_call(lefts, rights, places, first_tile, held):
    height, breadth = lefts[0].shape[1], rights[0].shape[1]
    steps = min(4, height // B)
    count = len(lefts)
    row_tiles, column_tiles = height // B // steps, breadth // B
    amount = row_tiles * column_tiles
    given = [array for _, _, array in held if array is not None]

    def kernel(place, *refs):
        left_refs, right_refs = refs[:count], refs[count : 2 * count]
        outs = refs[2 * count + len(given) : 2 * count + len(given) + len(held)]
        ready, sem = refs[-2], refs[-1]
        step = pl.program_id(0)
        slot = lax.rem(step, 2)

        def drain(which):
            pltpu.make_async_copy(
                ready.at[which], outs[0].at[pl.ds(0, amount)], sem.at[which]
            ).wait()

        @pl.when(step >= 2)
        def _():
            drain(slot)

        block = over_rows(left_refs[0][...], right_refs[0][...])
        for left, right in zip(left_refs[1:], right_refs[1:]):
            block = block + over_rows(left[...], right[...])
        block = low(block)
        for row in range(row_tiles):
            for column in range(column_tiles):
                ready[slot, row * column_tiles + column] = block[
                    row * B : (row + 1) * B, column * B : (column + 1) * B
                ]

        def send(index, carry):
            where_to = place[first_tile + step * amount + index]
            for number, (begin, _, _) in enumerate(held):
                end = held[number + 1][0] if number + 1 < len(held) else 1 << 30
                copy = pltpu.make_async_copy(
                    ready.at[slot, index], outs[number].at[where_to - begin], sem.at[slot]
                )
                if len(held) == 1:
                    copy.start()
                else:
                    pl.when((where_to >= begin) & (where_to < end))(copy.start)
            return carry

        lax.fori_loop(0, amount, send, 0)

        @pl.when(step == steps - 1)
        def _():
            drain(slot)
            if steps > 1:
                drain(1 - slot)

    rows = [left.shape[0] for left in lefts]
    anywhere = pl.BlockSpec(memory_space=pl.ANY)
    in_specs = [
        pl.BlockSpec((size, height // steps), lambda step, place: (0, step)) for size in rows
    ] + [
        pl.BlockSpec((size, breadth), lambda step, place: (0, 0), pipeline_mode=pl.Buffered(1))
        for size in rows
    ]
    in_specs += [anywhere] * len(given)
    operands = [places, *lefts, *rights, *given]
    aliases = {}
    for number, (_, _, array) in enumerate(held):
        if array is not None:
            aliases[1 + 2 * count + len(aliases)] = number
    results = pl.pallas_call(
        kernel,
        grid_spec=pltpu.PrefetchScalarGridSpec(
            num_scalar_prefetch=1,
            grid=(steps,),
            in_specs=in_specs,
            out_specs=[anywhere] * len(held),
            scratch_shapes=[
                pltpu.VMEM((2, amount, B, B), jnp.bfloat16),
                pltpu.SemaphoreType.DMA((2,)),
            ],
        ),
        out_shape=[
            jax.ShapeDtypeStruct((places_here, B, B), jnp.bfloat16) for _, places_here, _ in held
        ],
        input_output_aliases=aliases,
        compiler_params=params(),
        cost_estimate=pl.CostEstimate(
            flops=2 * sum(rows) * height * breadth,
            bytes_accessed=2 * (sum(rows) * (height + breadth) + height * breadth),
            transcendentals=0,
        ),
    )(*operands)
    return [
        (begin, places_here, array) for (begin, places_here, _), array in zip(held, results)
    ]


def place_call(pieces, targets, held, earlier=()):
    count = len(pieces)
    given = [array for _, _, array in held if array is not None]

    def kernel(target, *refs):
        begin_outs = count + len(given) + len(earlier)
        outs = refs[begin_outs : begin_outs + len(held)]
        token = refs[begin_outs + len(held)]
        buffers, loaded, stored = refs[-2 - count : -2], refs[-2], refs[-1]
        token[...] = jnp.zeros_like(token)
        for number in range(count):
            pltpu.make_async_copy(refs[number], buffers[number], loaded.at[number]).start()
        for number, (piece, begin) in enumerate(pieces):
            pltpu.make_async_copy(refs[number], buffers[number], loaded.at[number]).wait()

            def send(index, carry):
                where_to = target[begin + index]
                left = True
                for out_number, (first, amount, _) in enumerate(held):
                    last = out_number == len(held) - 1
                    inside = (where_to >= first) & (where_to < first + amount - 1)
                    at = where_to - first
                    if last:
                        at = jnp.where(inside, at, amount - 1)
                        inside = left
                    else:
                        left = jnp.logical_not(inside)
                    copy = pltpu.make_async_copy(
                        buffers[number].at[index], outs[out_number].at[at], stored.at[number]
                    )
                    if len(held) == 1:
                        copy.start()
                    else:
                        pl.when(inside)(copy.start)
                return carry

            lax.fori_loop(0, piece.shape[0], send, 0)
        for number, (piece, begin) in enumerate(pieces):
            pltpu.make_async_copy(
                buffers[number], outs[0].at[pl.ds(0, piece.shape[0])], stored.at[number]
            ).wait()

    anywhere = pl.BlockSpec(memory_space=pl.ANY)
    operands = [targets] + [piece for piece, _ in pieces] + given + list(earlier)
    aliases = {}
    for number, (_, _, array) in enumerate(held):
        if array is not None:
            aliases[1 + count + len(aliases)] = number
    results = pl.pallas_call(
        kernel,
        grid_spec=pltpu.PrefetchScalarGridSpec(
            num_scalar_prefetch=1,
            grid=(1,),
            in_specs=[anywhere] * (len(operands) - 1),
            out_specs=[anywhere] * len(held) + [pl.BlockSpec((8, B), lambda step, target: (0, 0))],
            scratch_shapes=[pltpu.VMEM(piece.shape, jnp.bfloat16) for piece, _ in pieces]
            + [pltpu.SemaphoreType.DMA((count,))] * 2,
        ),
        out_shape=[jax.ShapeDtypeStruct((amount, B, B), jnp.bfloat16) for _, amount, _ in held]
        + [jax.ShapeDtypeStruct((8, B), jnp.int32)],
        input_output_aliases=aliases,
        compiler_params=params(),
        cost_estimate=pl.CostEstimate(
            flops=0,
            bytes_accessed=sum(4 * piece.shape[0] * B * B for piece, _ in pieces),
            transcendentals=0,
        ),
    )(*operands)
    return [(first, amount, array) for (first, amount, _), array in zip(held, results)], results[-1]


def chips_sum(value):
    for swap in (swap_y, swap_x, lambda part: swap_f(part, 2), lambda part: swap_f(part, 4)):
        value = value + swap(value)
    return value


LOT = 8


def lots(count):
    return (count + LOT - 1) // LOT


def bring_strays(store, strays, count, owned_tiles, ordering, slots, me, tp_parts):
    def body(state):
        lot, held = state
        tiles = lax.dynamic_slice_in_dim(strays, lot * LOT, LOT, 0)
        valid = lot * LOT + jnp.arange(LOT) < count
        here = ordering[tiles]
        mine = valid & (here // slots == me)
        sent = jnp.where(mine[:, None, None], owned_tiles[here % slots], 0)
        sent = chips_sum(sent)
        at = jnp.where(valid, store_of_tile(tiles, tp_parts), held.shape[0])
        return lot + 1, held.at[at].set(sent, mode="drop")

    return lax.while_loop(lambda state: state[0] < lots(count), body, (0, store))[1]


def sum_strays(owned, parts, strays, count, ordering, slots, me):
    def body(state):
        lot, held = state
        tiles = lax.dynamic_slice_in_dim(strays, lot * LOT, LOT, 0)
        valid = lot * LOT + jnp.arange(LOT) < count
        summed = chips_sum(wide(lax.dynamic_slice_in_dim(parts, lot * LOT, LOT, 0)))
        here = ordering[tiles]
        at = jnp.where(valid & (here // slots == me), here % slots, slots)
        return lot + 1, held.at[at].set(summed, mode="drop")

    return lax.while_loop(lambda state: state[0] < lots(count), body, (0, owned))[1]


def normed_value(stream):
    centred = stream - jnp.mean(stream, -1, keepdims=True)
    rate = lax.rsqrt(jnp.mean(centred * centred, -1, keepdims=True) + EPS_NORM)
    return centred * rate, rate


def rows_kernel_call(kernel, wide_ins, mode_ins, outs, earlier=()):
    count = len(wide_ins) + len(mode_ins)

    def body(*refs):
        kernel(*refs[:count], *refs[count + len(earlier) :])

    own, group = wide_ins[0].shape[:2]
    rows = pl.BlockSpec((1, group, D), lambda step: (step, 0, 0))
    few = lambda count: pl.BlockSpec((1, count, D), lambda step: (step, 0, 0))
    return pl.pallas_call(
        body,
        grid=(own,),
        in_specs=[rows] * len(wide_ins)
        + [few(modes.shape[1]) for modes in mode_ins]
        + [pl.BlockSpec(memory_space=pl.ANY)] * len(earlier),
        out_specs=[rows if count is None else few(count) for count, _ in outs],
        out_shape=[
            jax.ShapeDtypeStruct((own, group if count is None else count, D), kind)
            for count, kind in outs
        ],
        compiler_params=params(),
        cost_estimate=pl.CostEstimate(
            flops=own * group * D * 20,
            bytes_accessed=own * group * D * 4 * (len(wide_ins) + len(outs)),
            transcendentals=own * group,
        ),
    )(*wide_ins, *mode_ins, *earlier)


def modulate_call(stream, modes, shift, scale):
    def kernel(values, mode, out):
        out[0] = low(
            normed_value(values[0])[0] * (1.0 + mode[0, scale : scale + 1, :])
            + mode[0, shift : shift + 1, :]
        )

    return rows_kernel_call(kernel, [stream], [modes], [(None, jnp.bfloat16)])[0]


def residual_call(stream, terms, modes, gate, next_modes, shift, scale, earlier=()):
    def kernel(*refs):
        values, term_refs = refs[0], refs[1 : 1 + len(terms)]
        mode, mode_next, branch, stream_new, out = refs[1 + len(terms) :]
        summed = term_refs[0][0]
        for term in term_refs[1:]:
            summed = summed + term[0]
        branch[0] = summed
        result = values[0] + mode[0, gate : gate + 1, :] * summed
        stream_new[0] = result
        out[0] = low(
            normed_value(result)[0] * (1.0 + mode_next[0, scale : scale + 1, :])
            + mode_next[0, shift : shift + 1, :]
        )

    shape = stream.shape
    return rows_kernel_call(
        kernel,
        [stream] + [term.reshape(shape) for term in terms],
        [modes, next_modes],
        [(None, jnp.float32), (None, jnp.float32), (None, jnp.bfloat16)],
        earlier,
    )


def back_call(stream, terms, upstream, modes, scale, below, earlier=()):
    shape = stream.shape
    wide_ins = [stream] + [term.reshape(shape) for term in terms]
    if upstream is not None:
        wide_ins.append(upstream)
    mode_ins = [modes]
    outs = [(None, jnp.float32), (3 if below else 2, jnp.float32)]
    if below:
        branch, branch_modes, gate = below
        wide_ins.append(branch)
        mode_ins.append(branch_modes)
        outs.append((None, jnp.bfloat16))

    def kernel(*refs):
        ins, modes_in = refs[: len(wide_ins)], refs[len(wide_ins) : len(wide_ins) + len(mode_ins)]
        results = refs[len(wide_ins) + len(mode_ins) :]
        grad = ins[1][0]
        for term in ins[2 : 1 + len(terms)]:
            grad = grad + term[0]
        normal, rate = normed_value(ins[0][0])
        results[1][0, 0:1, :] = jnp.sum(grad, 0, keepdims=True)
        results[1][0, 1:2, :] = jnp.sum(grad * normal, 0, keepdims=True)
        grad = grad * (1.0 + modes_in[0][0, scale : scale + 1, :])
        grad = rate * (
            grad
            - jnp.mean(grad, -1, keepdims=True)
            - normal * jnp.mean(grad * normal, -1, keepdims=True)
        )
        if upstream is not None:
            grad = grad + ins[1 + len(terms)][0]
        results[0][0] = grad
        if below:
            results[1][0, 2:3, :] = jnp.sum(grad * ins[-1][0], 0, keepdims=True)
            results[2][0] = low(modes_in[1][0, gate : gate + 1, :] * grad)

    return rows_kernel_call(kernel, wide_ins, mode_ins, outs, earlier)


def update_kernel(clip, grad, master, first, second, bases, master_out, first_out, second_out, low_out):
    eye = lax.broadcasted_iota(jnp.int32, (B, B), 0) == lax.broadcasted_iota(jnp.int32, (B, B), 1)
    left_row = bases[:, 0:1, :]
    right_row = bases[:, 1:2, :]
    left_col = jnp.sum(jnp.where(eye[None], left_row, 0.0), 2, keepdims=True)
    left_scaled = left_col * (2.0 / jnp.sum(left_row * left_row, 2, keepdims=True))
    right_scaled = right_row * (2.0 / jnp.sum(right_row * right_row, 2, keepdims=True))

    def turn(middle):
        middle = middle - left_scaled * jnp.sum(left_col * middle, 1, keepdims=True)
        return middle - jnp.sum(middle * right_row, 2, keepdims=True) * right_scaled

    turned = turn(clip[0, 0] * grad[...])
    first_new = 0.5 * first[...] + 0.5 * turned
    second_new = 0.5 * second[...] + 0.5 * turned * turned
    first_out[...] = first_new
    second_out[...] = second_new
    master_new = master[...] - RATE * turn(first_new / (jnp.sqrt(second_new) + 1e-08))
    master_out[...] = master_new
    low_out[...] = master_new.astype(jnp.bfloat16)


def update_tiles(clip_factor, grad, master, first, second, bases):
    slots = grad.shape[0]
    amount = max(count for count in (1, 2, 3, 4, 6, 8) if slots % count == 0)
    tile_spec = pl.BlockSpec((amount, B, B), lambda step: (step, 0, 0))
    whole = jax.ShapeDtypeStruct(grad.shape, jnp.float32)
    return pl.pallas_call(
        update_kernel,
        grid=(slots // amount,),
        in_specs=[pl.BlockSpec(memory_space=pltpu.SMEM)]
        + [tile_spec] * 4
        + [pl.BlockSpec((amount, 2, B), lambda step: (step, 0, 0))],
        out_specs=[tile_spec] * 4,
        out_shape=[whole, whole, whole, jax.ShapeDtypeStruct(grad.shape, jnp.bfloat16)],
        compiler_params=params(),
        cost_estimate=pl.CostEstimate(
            flops=slots * B * B * 30, bytes_accessed=slots * B * B * 30, transcendentals=slots * B * B
        ),
    )(clip_factor.reshape(1, 1), grad, master, first, second, bases)


def on_device(
    latents,
    noise,
    timesteps,
    labels,
    owners,
    tiles_low,
    tiles_master,
    tiles_first,
    tiles_second,
    bases,
    else_low,
    else_master,
    else_first,
    else_second,
):
    box = is_box()
    tp_parts = lax.axis_size("tp")
    tp_index = lax.axis_index("tp")
    ctx_parts = lax.axis_size("ctx")
    fsdp_parts = lax.axis_size("fsdp")
    images = latents.shape[0]
    local_len = latents.shape[1]
    slots = tiles_low.shape[1]
    sp_rows = images * local_len // tp_parts
    first_row = tp_index * sp_rows
    own = max(1, sp_rows // local_len)
    group = sp_rows // own
    first_image = first_row // local_len
    element_count = images * fsdp_parts * ctx_parts * local_len * P_SIZE
    ordering = jnp.argsort(owners, stable=True)
    inverse = jnp.argsort(ordering)
    all_tiles = inverse.shape[0]
    per_layer = all_tiles // L
    if box:
        early = early_slots(slots)
        me = lax.axis_index("fsdp") * ctx_parts + lax.axis_index("ctx")
        tile = jnp.arange(all_tiles, dtype=jnp.int32)
        owner, slot = inverse // slots, inverse % slots
        is_early = slot < early
        place_early = early_place(owner, slot, early)
        place_late = late_place(owner, slot - early, slots - early)
        gather_places = jnp.where(is_early, place_early, 16 * early + place_late)
        targets = store_of_tile(jnp.argsort(gather_places), tp_parts).astype(jnp.int32)
        is_stray = jnp.logical_not(is_early) & (tile < per_layer)
        stray_count = jnp.sum(is_stray.astype(jnp.int32))
        stray_rank = jnp.cumsum(is_stray.astype(jnp.int32)) - 1
        room = 16 * (slots - early)
        strays = jnp.argsort(jnp.where(is_stray, tile, all_tiles + tile)).astype(jnp.int32)
        strays = jnp.concatenate([strays, jnp.zeros((LOT,), jnp.int32)])
        places = jnp.where(
            is_stray,
            room + 16 * (early + 1) + stray_rank,
            jnp.where(is_early, room + early_place(owner, slot, early + 1), place_late),
        ).astype(jnp.int32)
        stores = [(0, per_layer + 1, None), (per_layer, per_layer + 1, None)]
        late_store = None

        def place_early_tiles(tile_group, *earlier):
            nonlocal stores
            stores, token = place_call(tile_group, targets, stores, earlier)
            return token

        def place_late_tiles(tile_group, *earlier):
            nonlocal late_store
            tile_group = [(piece, 16 * early + at) for piece, at in tile_group]
            if late_store is None:
                late_store = [stores[1]]
            late_store, token = place_call(tile_group, targets, late_store, earlier)
            return token

        late_store = None
        else_parts, finish_gather, arriving = gather_tiles(
            tiles_low[0], early, place_early_tiles, place_late_tiles, else_low, targets
        )
        store = [
            bring_strays(
                stores[0][2], strays, stray_count, tiles_low[0], inverse, slots, me, tp_parts
            ),
            None,
        ]
        held = [(0, room, None), (room, 16 * (slots + 1) + LOT, None)]
    else:
        places = jnp.arange(all_tiles, dtype=jnp.int32)
        tile_stored = jnp.argsort(store_of_tile(places, tp_parts))
        gathered = lax.all_gather(tiles_low, ("fsdp", "ctx"), axis=1, tiled=True)[0]
        gathered = gathered[inverse[tile_stored]]
        store = [gathered[:per_layer], gathered[per_layer:]]
        held = [(0, all_tiles, None)]
        else_parts = cut_else(lax.all_gather(else_low, ("fsdp", "ctx", "tp"), axis=0, tiled=True))
    (patch_weight, class_table, time_first, time_second), final_rows, head_weight = else_parts
    features_low = low(time_features(timesteps))
    onehot = low(labels[:, None] == jnp.arange(NCLS)[None, :])
    time_hidden = product(features_low, time_first)
    time_act = low(jax.nn.silu(time_hidden))
    condition = product(time_act, time_second) + product(onehot, class_table)
    cond_act = low(jax.nn.silu(condition))
    def modes_of(layer_no):
        return lax.dynamic_slice_in_dim(
            columns_in(modes_call(cond_act, store[layer_no], tp_parts)), first_image, own, 0
        ).reshape(own, 6, D)

    modes = [modes_of(0)]
    final_modes = lax.dynamic_slice_in_dim(
        final_product(cond_act, final_rows), first_image, own, 0
    )
    row_index = first_row + jnp.arange(sp_rows)
    signal = signal_level(timesteps)
    noisy_input = (
        jnp.sqrt(signal)[:, None, None] * latents + jnp.sqrt(1.0 - signal)[:, None, None] * noise
    )
    noisy_rows = low(
        lax.dynamic_slice_in_dim(
            noisy_input.reshape(images * local_len, P_SIZE), first_row, sp_rows, 0
        )
    )
    target = lax.dynamic_slice_in_dim(
        noise.reshape(images * local_len, P_SIZE), first_row, sp_rows, 0
    )
    stream = (product(noisy_rows, patch_weight) + position_table(row_index % local_len)).reshape(
        own, group, D
    )
    normed_in = modulate_call(stream, modes[0], 0, 1)
    kept = []
    for layer_no in range(L):
        row_sets = rows_in(normed_in.reshape(sp_rows, D))
        halves, terms = each_half(
            lambda rows: attend_call(
                rows,
                store[layer_no],
                tp_parts,
                local_len,
                arriving if box and layer_no == 0 and rows is row_sets[0] else (),
            ),
            row_sets,
        )
        branch, middle, normed_mid = residual_call(
            stream,
            terms,
            modes[layer_no],
            2,
            modes[layer_no],
            3,
            4,
        )
        mid_sets = rows_in(normed_mid.reshape(sp_rows, D))
        hidden, terms = each_half(
            lambda rows: mlp_call(rows, store[layer_no], tp_parts, local_len), mid_sets
        )
        last = layer_no == L - 1
        if not last:
            if box:
                finish_gather(terms[0])
                store[1] = late_store[0][2]
            modes.append(modes_of(layer_no + 1))
        mlp_out, stream_new, normed_in = residual_call(
            middle,
            terms,
            modes[layer_no],
            5,
            final_modes if last else modes[layer_no + 1],
            0,
            1,
        )
        kept.append((stream, row_sets, halves, branch, middle, mid_sets, hidden, mlp_out))
        stream = stream_new
    head_low = normed_in.reshape(sp_rows, D)
    mismatch = product(head_low, head_weight) - target
    loss_part = jnp.sum(mismatch * mismatch) / element_count
    grad_pred = low(2.0 * mismatch / element_count)
    grad_head = over_rows(grad_pred, head_low)
    upstream, final_sums, grad_low = back_call(
        stream,
        [against(grad_pred, head_weight)],
        None,
        final_modes,
        1,
        (kept[-1][7], modes[-1], 5),
    )
    grad_final = final_sums[:, :2].reshape(own, 2 * D)
    gate_sum = final_sums[:, 2:]
    starts = [begin for _, begin in segments(tp_parts)]
    mode_width = 6 * D // tp_parts
    fill = (-3 * images) % 16
    conds = jnp.pad(jnp.concatenate([cond_act] * 3, 0), ((0, fill), (0, 0)))

    def all_images(values):
        return tp_sum(
            lax.dynamic_update_slice_in_dim(
                jnp.zeros((images, values.shape[1]), jnp.float32), values, first_image, 0
            )
        )

    grad_final = all_images(grad_final)
    cond_wide = wide(cond_act)

    def image_part(columns):
        packed = jnp.concatenate(columns, 1)
        packed = jnp.pad(packed, ((0, 0), (0, -packed.shape[1] % 256)))
        part = packed.shape[1] // 2
        return lax.dynamic_slice_in_dim(packed, tp_index * part, part, 1)

    label_column = jnp.broadcast_to(wide(labels)[:, None], (images, 128))
    early_columns = [label_column, wide(features_low), wide(time_act), cond_wide, grad_final]
    grad_cond_act = 0.0
    for layer_no in reversed(range(L)):
        stream, row_sets, halves, branch, middle, mid_sets, hidden, mlp_out = kept[layer_no]
        base = layer_no * per_layer
        grad_sets = rows_in(grad_low.reshape(sp_rows, D))
        results, terms = each_half(
            lambda pair: mlp_back_call(pair[0], pair[1], store[layer_no], tp_parts, local_len),
            [(rows, hidden_here[0]) for rows, hidden_here in zip(grad_sets, hidden)],
        )
        held = weight_grad_call(
            [result[0] for result in results], grad_sets, places, base + starts[3], held
        )
        held = weight_grad_call(
            mid_sets, [result[1] for result in results], places, base + starts[2], held
        )
        upstream, mlp_sums, grad_low = back_call(
            middle, terms, upstream, modes[layer_no], 4, (branch, modes[layer_no], 2)
        )
        if box and layer_no == 0:
            late_sums = scatter_late(
                late_parts,
                slots - early,
                lanes,
                late_first,
                tp_sum(grad_head),
                image_part(early_columns),
                upstream,
                grad_cond_early,
            )
        grad_sets = rows_in(grad_low.reshape(sp_rows, D))
        results, terms = each_half(
            lambda pair: attend_back_call(pair[0], pair[1], store[layer_no], tp_parts, local_len),
            [(rows, half[0]) for rows, half in zip(grad_sets, halves)],
        )
        held = weight_grad_call(
            [half[1] for half in halves], grad_sets, places, base + starts[1], held
        )
        held = weight_grad_call(
            row_sets, [result[0] for result in results], places, base + starts[0], held
        )
        below = None if layer_no == 0 else (kept[layer_no - 1][7], modes[layer_no - 1], 5)
        found = back_call(
            stream,
            terms,
            upstream,
            modes[layer_no],
            1,
            below,
            (late_sums[0][0],) if box and layer_no == 0 else (),
        )
        grad_modes = jnp.concatenate(
            [found[1][:, :2], mlp_sums[:, 2:], mlp_sums[:, :2], gate_sum], 1
        ).reshape(own, 6 * D)
        mode_image = lax.dynamic_slice_in_dim(
            all_images(grad_modes), tp_index * mode_width, mode_width, 1
        )
        held = weight_grad_call(
            [conds],
            [jnp.pad(three_parts(mode_image), ((0, fill), (0, 0)))],
            places,
            base + starts[4],
            held,
        )
        grad_cond_act = grad_cond_act + modes_back_call(mode_image, store[layer_no], tp_parts)
        upstream = found[0]
        if below:
            grad_low, gate_sum = found[2], found[1][:, 2:]
        if box and layer_no == L - 1:
            grad_low = after(grad_low, held[0][2], held[1][2])
            lanes = Lanes()
            late_parts = held[0][2]
            late_first = scatter_late_first(late_parts, slots - early, lanes)
            grad_cond_early = grad_cond_act
            held = held[1:]
    grad_patch = over_rows(noisy_rows, low(upstream).reshape(sp_rows, D))
    grad_cond_act = tp_sum(grad_cond_act) + final_product_back(grad_final, final_rows)
    grad_condition = jax.vjp(jax.nn.silu, condition)[1](grad_cond_act)[0]
    grad_time_hidden = jax.vjp(jax.nn.silu, time_hidden)[1](
        against_low(grad_condition, time_second)
    )[0]
    if box:
        patch_sum = tp_sum(grad_patch).reshape(1, B, B)
        patch_first = low(patch_sum)
        parts = lax.dynamic_update_slice_in_dim(
            held[0][2],
            jnp.where(tp_index == 0, patch_first, low(patch_sum - wide(patch_first))),
            early_place(0, early, early + 1),
            0,
        )
        owned, owned_late, late_images, head_sum, early_images = scatter_early(
            parts,
            early + 1,
            lanes,
            *late_sums,
            image_part([grad_time_hidden, grad_condition]),
        )
        late_images = columns_in(late_images)
        early_images = columns_in(early_images)
        head_rows = head_sum.T.reshape(P_SIZE, D)
        patch_rows = tp_sum(owned[early]).reshape(P_SIZE, D)
        owned = jnp.concatenate([owned[:early], owned_late], 0)
        owned = sum_strays(
            owned, parts[16 * (early + 1) :], strays, stray_count, inverse, slots, me
        )
    else:
        owned = lax.psum_scatter(
            wide(held[0][2])[ordering], ("fsdp", "ctx"), scatter_dimension=0, tiled=True
        )
        patch_rows = lax.psum(grad_patch, ("fsdp", "ctx", "tp"))
        head_rows = lax.psum(grad_head, ("fsdp", "ctx", "tp")).T.reshape(P_SIZE, D)
        late_images = gather_images(jnp.concatenate([grad_time_hidden, grad_condition], 1))
        early_images = gather_images(jnp.concatenate(early_columns, 1))
    all_hidden, all_condition = jnp.split(late_images, 2, 1)
    cuts = [128]
    for length in (TFREQ, D, D):
        cuts.append(cuts[-1] + length)
    all_labels, all_features, all_time, all_cond, all_final = jnp.split(early_images, cuts, 1)
    all_final = all_final[:, : 2 * D]
    all_onehot = wide(all_labels[:, :1] == jnp.arange(NCLS, dtype=jnp.float32)[None, :])
    share = else_low.shape[0]
    device = (lax.axis_index("fsdp") * ctx_parts + lax.axis_index("ctx")) * tp_parts + tp_index
    begin = device * share
    row_total = else_low.shape[0] * fsdp_parts * ctx_parts * tp_parts // D
    row_count = min(share // D + 2, row_total)
    begin_row = jnp.minimum(begin // D, row_total - row_count)
    row_ids = begin_row + jnp.arange(row_count)
    edge = jnp.zeros((all_cond.shape[0], P_SIZE), jnp.float32)
    factors = jnp.concatenate(
        [edge, all_onehot, all_features, all_time, jnp.repeat(all_cond, 2, axis=1), edge], 1
    )
    factors = lax.dynamic_slice_in_dim(factors, begin_row, row_count, 1)
    first_start = P_SIZE + NCLS
    second_start = first_start + TFREQ
    final_start = second_start + D

    def rows_of(chosen, right):
        return contract("ic,id->cd", jnp.where(chosen[None, :], factors, 0.0), right)

    in_first = (row_ids >= first_start) & (row_ids < second_start)
    in_final = row_ids >= final_start
    odd = (row_ids - final_start) % 2 == 1
    near = rows_of(in_first, all_hidden)
    near = near + rows_of(jnp.logical_not(in_first | in_final), all_condition)
    near = near + rows_of(in_final & jnp.logical_not(odd), all_final[:, :D])
    near = near + rows_of(in_final & odd, all_final[:, D:])
    for begin_here, token_rows in ((0, patch_rows), (row_total - P_SIZE, head_rows)):
        here = row_ids - begin_here
        inside = (here >= 0) & (here < P_SIZE)
        near = jnp.where(
            inside[:, None], token_rows[jnp.clip(here, 0, P_SIZE - 1)], near
        )
    else_grad = lax.dynamic_slice_in_dim(near.reshape(-1), begin - begin_row * D, share, 0)
    squares = jnp.sum(owned * owned) + jnp.sum(else_grad * else_grad)
    totals = total(jnp.stack([loss_part, squares]))
    loss_total = totals[0]
    grad_norm = jnp.sqrt(totals[1])
    clip_factor = jnp.minimum(1.0, 1.0 / grad_norm)
    master_new, first_new, second_new, low_new = update_tiles(
        clip_factor, owned, tiles_master[0], tiles_first[0], tiles_second[0], bases[0]
    )
    else_master_new, else_first_new, else_second_new = adamw_flat(
        clip_factor * else_grad, else_master, else_first, else_second
    )
    return (
        loss_total,
        grad_norm,
        master_new[None],
        first_new[None],
        second_new[None],
        low_new[None],
        else_master_new,
        else_first_new,
        else_second_new,
        low(else_master_new),
    )


def solution(mesh):
    return jax.shard_map(
        on_device,
        mesh=mesh,
        in_specs=(
            P(("fsdp", "ctx"), None, None),
            P(("fsdp", "ctx"), None, None),
            P(("fsdp", "ctx")),
            P(("fsdp", "ctx")),
            P(),
            P("tp", ("fsdp", "ctx"), None, None),
            P("tp", ("fsdp", "ctx"), None, None),
            P("tp", ("fsdp", "ctx"), None, None),
            P("tp", ("fsdp", "ctx"), None, None),
            P("tp", ("fsdp", "ctx"), None, None),
            P(("fsdp", "ctx", "tp")),
            P(("fsdp", "ctx", "tp")),
            P(("fsdp", "ctx", "tp")),
            P(("fsdp", "ctx", "tp")),
        ),
        out_specs=(
            P(),
            P(),
            P("tp", ("fsdp", "ctx"), None, None),
            P("tp", ("fsdp", "ctx"), None, None),
            P("tp", ("fsdp", "ctx"), None, None),
            P("tp", ("fsdp", "ctx"), None, None),
            P(("fsdp", "ctx", "tp")),
            P(("fsdp", "ctx", "tp")),
            P(("fsdp", "ctx", "tp")),
            P(("fsdp", "ctx", "tp")),
        ),
        check_vma=False,
    )
```

```python
import math

import jax
import jax.numpy as jnp
from jax import lax
from jax.experimental import pallas as pl
from jax.experimental.pallas import tpu as pltpu
from jax.sharding import PartitionSpec as P

D = 1024
HD = 64
F = 4096
P_SIZE = 16
TFREQ = 256
NCLS = 1000
GRID = 16
L = 2
B = 128


HIGHEST = lax.Precision.HIGHEST
EPS_NORM = 1e-06
RATE = 0.02
DECAY = 0.1


def matmul(left_op, right_op):
    return jnp.dot(left_op, right_op, precision=HIGHEST)


def contract(formula, left_op, right_op):
    return jnp.einsum(formula, left_op, right_op, precision=HIGHEST)


def product(left_op, right_op):
    return jnp.dot(left_op, right_op, preferred_element_type=jnp.float32)


def over_rows(left_op, right_op):
    return lax.dot_general(
        left_op, right_op, (((0,), (0,)), ((), ())), preferred_element_type=jnp.float32
    )


def against(left_op, right_op):
    return lax.dot_general(
        left_op, right_op, (((1,), (1,)), ((), ())), preferred_element_type=jnp.float32
    )


def normed(stream):
    centred = stream - jnp.mean(stream, -1, keepdims=True)
    return centred * lax.rsqrt(jnp.mean(centred * centred, -1, keepdims=True) + EPS_NORM)


def modulate(stream, offset, factor):
    return normed(stream) * (1.0 + factor) + offset


def gelu_tanh(values):
    return jax.nn.gelu(values, approximate=True)


def time_features(time_steps):
    half_count = TFREQ // 2
    freqs = jnp.exp(-math.log(10000.0) * jnp.arange(half_count, dtype=jnp.float32) / half_count)
    angles = time_steps.astype(jnp.float32)[:, None] * freqs[None, :]
    return jnp.concatenate([jnp.cos(angles), jnp.sin(angles)], -1)


def position_table(token_ids):
    quarter = D // 4
    omegas = 1.0 / 10000.0 ** (jnp.arange(quarter, dtype=jnp.float32) / quarter)
    row_angle = (token_ids // GRID).astype(jnp.float32)[:, None] * omegas[None, :]
    col_angle = (token_ids % GRID).astype(jnp.float32)[:, None] * omegas[None, :]
    return jnp.concatenate(
        [jnp.sin(row_angle), jnp.cos(row_angle), jnp.sin(col_angle), jnp.cos(col_angle)], -1
    )


def signal_level(time_steps):
    phase = (time_steps.astype(jnp.float32) / 1000.0 + 0.008) / 1.008 * (math.pi / 2)
    return jnp.cos(phase) ** 2


def shard_shapes(tp_parts):
    head_width = D // tp_parts
    hidden_width = F // tp_parts
    return [
        (D, 3 * head_width),
        (head_width, D),
        (D, hidden_width),
        (hidden_width, D),
        (D, 6 * head_width),
    ]


def untile(tile_set, height, breadth):
    block = tile_set.shape[-1]
    return (
        tile_set.reshape(height // block, breadth // block, block, block)
        .transpose(0, 2, 1, 3)
        .reshape(height, breadth)
    )


def retile(matrix):
    height, breadth = matrix.shape
    return matrix.reshape(height // B, B, breadth // B, B).transpose(0, 2, 1, 3).reshape(-1, B, B)


def unpack_layers(tile_set, tp_parts):
    layer_list = []
    cursor = 0
    for layer_no in range(L):
        matrices = []
        for height, breadth in shard_shapes(tp_parts):
            amount = height * breadth // (B * B)
            matrices.append(untile(tile_set[cursor : cursor + amount], height, breadth))
            cursor += amount
        layer_list.append(matrices)
    return layer_list


def pack_layers(layer_list):
    return jnp.concatenate([retile(matrix) for matrices in layer_list for matrix in matrices], 0)


def else_shapes():
    return [(P_SIZE, D), (NCLS, D), (TFREQ, D), (D, D), (D, 2 * D), (D, P_SIZE)]


def split_else(flat_params):
    components = []
    cursor = 0
    for height, breadth in else_shapes():
        components.append(flat_params[cursor : cursor + height * breadth].reshape(height, breadth))
        cursor += height * breadth
    return components


def reflection(vectors):
    outer_prod = vectors[..., :, None] * vectors[..., None, :]
    return (
        jnp.eye(vectors.shape[-1], dtype=jnp.float32)
        - 2.0 * outer_prod / jnp.sum(vectors * vectors, -1)[..., None, None]
    )


def rotate(left_basis, middle, right_basis):
    return contract(
        "...ab,...bc->...ac", contract("...ab,...bc->...ac", left_basis, middle), right_basis
    )


def adam_finish(turned, master_state, first_state, second_state, left_basis, right_basis):
    first_new = 0.5 * first_state + 0.5 * turned
    second_new = 0.5 * second_state + 0.5 * turned * turned
    direction = first_new / (jnp.sqrt(second_new) + 1e-08)
    return (master_state - RATE * rotate(left_basis, direction, right_basis), first_new, second_new)


def adamw_flat(grad_clipped, master_state, first_state, second_state):
    first_new = 0.5 * first_state + 0.5 * grad_clipped
    second_new = 0.5 * second_state + 0.5 * grad_clipped * grad_clipped
    master_new = master_state - RATE * (
        first_new / (jnp.sqrt(second_new) + 1e-08) + DECAY * master_state
    )
    return (master_new, first_new, second_new)


def is_box():
    return (lax.axis_size("fsdp"), lax.axis_size("ctx"), lax.axis_size("tp")) == (8, 2, 2)


def swap_tp(value):
    return lax.ppermute(value, "tp", [(0, 1), (1, 0)])


def swap_y(value):
    return lax.ppermute(value, "ctx", [(0, 1), (1, 0)])


def swap_f(value, bit):
    return lax.ppermute(value, "fsdp", [(place, place ^ bit) for place in range(8)])


def swap_x(value):
    return swap_f(value, 1)


def place_z():
    return lax.axis_index("fsdp") // 2


def low(value):
    return value.astype(jnp.bfloat16)


def wide(value):
    return value.astype(jnp.float32)


def after(value, *earlier):
    return lax.optimization_barrier((value, *earlier))[0]


class Lanes:
    def __init__(self):
        self.done = ()

    def step(self, sends, *earlier):
        values = lax.optimization_barrier(tuple(value for _, value in sends) + self.done + earlier)
        self.done = tuple(swap(value) for (swap, _), value in zip(sends, values))
        return list(self.done)


def move_z(step, sources):
    pairs = [(2 * z + x, 2 * (z + step) + x) for z in sources for x in range(2)]
    return lambda value: lax.ppermute(value, "fsdp", pairs)


def to_z(rel):
    return lambda value: swap_f(value, 2 * rel)


class ZLine:
    def __init__(self, own):
        self.above, self.below = [own], [own]

    def sends(self):
        hop = len(self.above)
        return [
            (move_z(1, range(hop - 1, 3)), self.above[-1]),
            (move_z(-1, range(1, 5 - hop)), self.below[-1]),
        ]

    def take(self, arrived):
        self.above.append(arrived[0])
        self.below.append(arrived[1])

    def block(self, rel, token=None):
        z = place_z()
        if token is not None:
            z = z + token[0, 0]
        above, below = self.above, self.below
        if rel == 0:
            return above[0]
        if rel == 1:
            return jnp.where(z % 2 == 1, above[1], below[1])
        if rel == 2:
            return jnp.where(z >= 2, above[2], below[2])
        return jnp.where(
            z == 0, below[3], jnp.where(z == 3, above[3], jnp.where(z == 1, below[1], above[1]))
        )


class ZSum:
    def __init__(self):
        self.last = None
        self.up = self.down = None

    def sends(self, rel, block):
        z = place_z()
        if rel == 3:
            self.last = block
            up, down = block, block
        elif rel == 2:
            up, down = block + self.up, block + self.down
        else:
            up = jnp.where(z == 1, self.last, block) + self.up
            down = jnp.where(z == 2, self.last, block) + self.down
        return [
            (move_z(1, range(0, 4 - rel)), low(up)),
            (move_z(-1, range(rel, 4)), low(down)),
        ]

    def take(self, arrived):
        self.up, self.down = arrived

    def total(self, block):
        return block + self.up + self.down


def early_slots(slots):
    return slots - slots * 25 // 72


def gather_tiles(own, early, place_early, place_late, else_low, targets):
    half = early // 2
    lanes = Lanes()
    line, late_line = ZLine(own[:early]), ZLine(own[early:])
    rest = whole = None
    tokens = []
    for rel in range(4):
        block = line.block(rel, tokens[rel - 2] if rel >= 2 else None)
        sends = [(swap_x, block), (swap_y, block)]
        waits = ()
        if rel == 3:
            waits = rest[0]
        going = line if rel < 3 else late_line
        sends += going.sends()
        if rel == 1:
            by_x, by_y, above, below, *both = lanes.step(sends + else_diagonal)
            whole = finish_else(else_line, both)
            rest = cut_else(whole)
        else:
            by_x, by_y, above, below = lanes.step(sends, *waits)
        going.take((above, below))
        sends = [(swap_y, by_x[:half]), (swap_x, by_y[half:])]
        if rel == 0:
            first, second, *arrived = lanes.step(
                sends + [(to_z(other), else_low.reshape(1, -1, 128)) for other in (1, 2, 3)],
                targets,
            )
            else_line, else_diagonal = start_else(else_low, lanes, arrived)
        elif rel < 3:
            first, second, *arrived = lanes.step(sends + late_line.sends())
            late_line.take(arrived)
        else:
            first, second = lanes.step(sends)
        at = 4 * rel * early
        group = [
            (block, at),
            (by_y, at + early),
            (by_x, at + 2 * early),
            (first, at + 3 * early),
            (second, at + 3 * early + half),
        ]
        earlier = ()
        if rel == 3:
            late = jnp.concatenate([late_line.block(other) for other in range(4)], 0)
            earlier = (late,)
        tokens.append(place_early(group, *earlier))
    line = late
    count = line.shape[0]
    half = count // 2
    by_x, by_y = lanes.step([(swap_x, line), (swap_y, line)])
    place_late([(line, 0)])

    def finish(*earlier):
        first, second = lanes.step([(swap_y, by_x[:half]), (swap_x, by_y[half:])])
        place_late([(by_y, count), (by_x, 2 * count)])
        place_late([(first, 3 * count), (second, 3 * count + half)], *earlier)

    return rest, finish, (by_x, by_y)


def relative(owner):
    rel_f = jnp.bitwise_xor(owner // 2, lax.axis_index("fsdp"))
    return rel_f // 2, rel_f % 2, jnp.bitwise_xor(owner % 2, lax.axis_index("ctx"))


def early_place(owner, slot, slots):
    rel_z, rel_x, rel_y = relative(owner)
    return ((rel_z * 2 + rel_x) * 2 + rel_y) * slots + slot


def late_place(owner, slot, slots):
    rel_z, rel_x, rel_y = relative(owner)
    return ((rel_x * 2 + rel_y) * 4 + rel_z) * slots + slot


def scatter_late_first(parts, slots, lanes):
    both = parts[12 * slots :]
    return lanes.step([(swap_y, both[: 2 * slots]), (swap_x, both[2 * slots :])])


def scatter_late(parts, slots, lanes, wait, head_sum, images_part, *earlier):
    count = 4 * slots
    half = count // 2
    keep, to_y, to_x, _ = (parts[part * count : (part + 1) * count] for part in range(4))
    by_y, by_x = wait
    to_x = jnp.concatenate([low(wide(to_x[:half]) + by_y), to_x[half:]], 0)
    to_y = jnp.concatenate([to_y[:half], low(wide(to_y[half:]) + by_x)], 0)
    from_x, from_y, head_y, *images = lanes.step(
        [(swap_x, to_x), (swap_y, to_y), (swap_y, head_sum)]
        + [(to_z(rel), images_part) for rel in (1, 2, 3)],
        *earlier,
    )
    keep = wide(keep) + from_x + from_y
    return (
        [keep[rel * slots : (rel + 1) * slots] for rel in range(4)],
        head_sum + head_y,
        jnp.concatenate([images_part] + images, 0),
    )


def scatter_early(parts, slots, lanes, late, head_sum, early_images, images_part):
    half = slots // 2

    def block(part, begin, end):
        return parts[part * slots + begin : part * slots + end]

    def diagonal(rel):
        return [
            (swap_y, block(4 * rel + 3, 0, half)),
            (swap_x, block(4 * rel + 3, half, slots)),
        ]

    def sides(rel, arrived):
        by_y, by_x = arrived
        return [
            (
                swap_x,
                jnp.concatenate(
                    [
                        low(wide(block(4 * rel + 2, 0, half)) + by_y),
                        block(4 * rel + 2, half, slots),
                    ],
                    0,
                ),
            ),
            (
                swap_y,
                jnp.concatenate(
                    [
                        block(4 * rel + 1, 0, half),
                        low(wide(block(4 * rel + 1, half, slots)) + by_x),
                    ],
                    0,
                ),
            ),
        ]

    def kept(rel, arrived):
        return wide(block(4 * rel, 0, slots)) + arrived[0] + arrived[1]

    line, late_line = ZSum(), ZSum()
    arrived = lanes.step(
        diagonal(3) + late_line.sends(3, late[3]) + [(swap_x, head_sum), (swap_y, early_images)]
    )
    diagonal_3 = arrived[:2]
    late_line.take(arrived[2:4])
    head_sum = head_sum + arrived[4]
    early_images = jnp.concatenate([early_images, arrived[5]], 0)
    arrived = lanes.step(
        diagonal(2) + late_line.sends(2, late[2]) + [(to_z(1), head_sum), (swap_x, early_images)]
    )
    diagonal_2 = arrived[:2]
    late_line.take(arrived[2:4])
    head_sum = head_sum + arrived[4]
    early_images = jnp.concatenate([early_images, arrived[5]], 0)
    arrived = lanes.step(sides(3, diagonal_3) + late_line.sends(1, late[1]))
    late_line.take(arrived[2:])
    owned_late = late_line.total(late[0])
    kept_3 = kept(3, arrived)
    arrived = lanes.step(
        diagonal(1) + [(to_z(rel), images_part) for rel in (1, 2, 3)] + [(to_z(2), head_sum)]
    )
    diagonal_1 = arrived[:2]
    images = jnp.concatenate([images_part] + arrived[2:5], 0)
    head_sum = head_sum + arrived[5]
    arrived = lanes.step(sides(2, diagonal_2) + line.sends(3, kept_3) + [(swap_y, images)])
    line.take(arrived[2:4])
    kept_2 = kept(2, arrived)
    images = jnp.concatenate([images, arrived[4]], 0)
    arrived = lanes.step(diagonal(0) + [(swap_x, images)])
    diagonal_0 = arrived[:2]
    images = jnp.concatenate([images, arrived[2]], 0)
    arrived = lanes.step(sides(1, diagonal_1) + line.sends(2, kept_2))
    line.take(arrived[2:4])
    arrived_0 = lanes.step(sides(0, diagonal_0) + line.sends(1, kept(1, arrived)))
    line.take(arrived_0[2:4])
    return line.total(kept(0, arrived_0)), owned_late, images, head_sum, early_images


def gather_images(value):
    if not is_box():
        return lax.all_gather(value, ("fsdp", "ctx"), axis=0, tiled=True)
    value = jnp.concatenate([value] + [swap_f(value, 2 * rel) for rel in (1, 2, 3)], 0)
    by_x, by_y = swap_x(value), swap_y(value)
    return jnp.concatenate([value, by_y, by_x, swap_x(by_y)], 0)


def start_else(flat, lanes, arrived):
    z = place_z()
    line = [flat.reshape(1, -1, 128)] + arrived
    line = [
        jnp.where(
            z == place,
            line[0],
            jnp.where(z == place ^ 1, line[1], jnp.where(z == place ^ 2, line[2], line[3])),
        )
        for place in range(4)
    ]
    line = jnp.concatenate(line, 0)
    by_x, by_y = lanes.step([(swap_x, line), (swap_y, line)])
    half = line.shape[1] // 2
    return (line, by_x, by_y), [(swap_y, by_x[:, :half]), (swap_x, by_y[:, half:])]


def finish_else(lines, both):
    x, y, core = lax.axis_index("fsdp") % 2, lax.axis_index("ctx"), lax.axis_index("tp")
    line, by_x, by_y = lines
    both = jnp.concatenate(both, 1)
    y_low = [jnp.where(y == 0, line, by_y), jnp.where(y == 0, by_x, both)]
    y_high = [jnp.where(y == 0, by_y, line), jnp.where(y == 0, both, by_x)]
    chip = jnp.stack(
        [
            jnp.stack([jnp.where(x == 0, y_low[0], y_low[1]), jnp.where(x == 0, y_high[0], y_high[1])], 1),
            jnp.stack([jnp.where(x == 0, y_low[1], y_low[0]), jnp.where(x == 0, y_high[1], y_high[0])], 1),
        ],
        1,
    )
    other = swap_tp(chip)
    return jnp.stack(
        [jnp.where(core == 0, chip, other), jnp.where(core == 0, other, chip)], 3
    )


def cut_else(whole):
    rows = whole.reshape(-1, D)
    counts = [P_SIZE, NCLS, TFREQ, D, 2 * D, P_SIZE]
    ends = [sum(counts[: place + 1]) for place in range(6)]
    parts = [rows[end - count : end] for end, count in zip(ends, counts)]
    return tuple(parts[:4]), parts[4], parts[5].reshape(D, P_SIZE)


def final_product(left_op, final_rows):
    rows = left_op.shape[0]
    nothing = jnp.zeros_like(left_op)
    spread = jnp.concatenate(
        [
            jnp.stack([left_op, nothing], -1).reshape(rows, 2 * D),
            jnp.stack([nothing, left_op], -1).reshape(rows, 2 * D),
        ],
        0,
    )
    found = product(spread, final_rows)
    return jnp.stack([found[:rows], found[rows:]], 1)


def final_product_back(grads, final_rows):
    rows = grads.shape[0]
    found = against_low(jnp.concatenate([grads[:, :D], grads[:, D:]], 0), final_rows)
    return found[:rows].reshape(rows, D, 2)[:, :, 0] + found[rows:].reshape(rows, D, 2)[:, :, 1]


def total(value):
    if not is_box():
        return lax.psum(value, ("fsdp", "ctx", "tp"))
    value = value + swap_tp(value)
    value = value + swap_y(value)
    for bit in (1, 2, 4):
        value = value + swap_f(value, bit)
    return value


def tp_sum(value):
    if lax.axis_size("tp") == 2:
        return value + swap_tp(value)
    return lax.psum(value, "tp")


def columns_in(value):
    if lax.axis_size("tp") == 2:
        other = swap_tp(value)
        at_zero = lax.axis_index("tp") == 0
        return jnp.concatenate(
            [jnp.where(at_zero, value, other), jnp.where(at_zero, other, value)], -1
        )
    return lax.all_gather(value, "tp", axis=value.ndim - 1, tiled=True)


def rows_in(value_low):
    if lax.axis_size("tp") == 2:
        return [value_low, swap_tp(value_low)]
    return [lax.all_gather(value_low, "tp", axis=0, tiled=True)]


def each_half(work, row_sets):
    if len(row_sets) == 2:
        other = work(row_sets[1])
        sent = swap_tp(other[-1])
        own = work(row_sets[0])
        return [own[:-1], other[:-1]], [own[-1], sent]
    whole = work(row_sets[0])
    return [whole[:-1]], [lax.psum_scatter(whole[-1], "tp", scatter_dimension=0, tiled=True)]


BIG = 56 * 1024 * 1024


def against_value(left_op, right_op):
    return lax.dot_general(
        left_op, right_op, (((1,), (1,)), ((), ())), preferred_element_type=jnp.float32
    )


def untile_into(matrix, tile_set):
    rows, columns = matrix.shape[0] // B, matrix.shape[1] // B
    for row in range(rows):
        for column in range(columns):
            matrix[row * B : (row + 1) * B, column * B : (column + 1) * B] = tile_set[
                row * columns + column
            ]


def segments(tp_parts):
    found = []
    begin = 0
    for height, breadth in shard_shapes(tp_parts):
        amount = height * breadth // (B * B)
        found.append((amount, begin))
        begin += amount
    return found


def weight_spec(kind, tp_parts):
    amount, begin = segments(tp_parts)[kind]
    return pl.BlockSpec(
        (amount, B, B), lambda *step: (begin // amount, 0, 0), pipeline_mode=pl.Buffered(1)
    )


def rows_spec(rows, breadth):
    return pl.BlockSpec((rows, breadth), lambda step: (step, 0))


def shaped(rows, breadth, kind):
    return jax.ShapeDtypeStruct((rows, breadth), kind)


def params():
    return pltpu.CompilerParams(vmem_limit_bytes=BIG)


def attend_kernel(normed_in, qkv_tiles, proj_tiles, *refs):
    projected, attended, partial, w_qkv, w_proj = refs[-5:]

    @pl.when(pl.program_id(0) == 0)
    def _():
        untile_into(w_qkv, qkv_tiles)
        untile_into(w_proj, proj_tiles)

    values = low(product(normed_in[...], w_qkv[...]))
    projected[...] = values
    width = values.shape[1] // 3
    results = []
    for head in range(width // HD):
        at = head * HD
        query = values[:, at : at + HD]
        key_rows = values[:, width + at : width + at + HD]
        value_rows = values[:, 2 * width + at : 2 * width + at + HD]
        scores = against_value(key_rows, query) * HD ** (-0.5)
        exponent = jnp.exp(scores - jnp.max(scores, 0, keepdims=True))
        probabilities = low(exponent * (1.0 / jnp.sum(exponent, 0, keepdims=True)))
        results.append(low(over_rows(probabilities, value_rows)))
    result = jnp.concatenate(results, 1)
    attended[...] = result
    partial[...] = product(result, w_proj[...])


def attend_call(normed_in, store, tp_parts, local_len, earlier=()):
    rows = normed_in.shape[0]
    width = D // tp_parts
    return pl.pallas_call(
        attend_kernel,
        grid=(rows // local_len,),
        in_specs=[
            rows_spec(local_len, D),
            weight_spec(0, tp_parts),
            weight_spec(1, tp_parts),
        ]
        + [pl.BlockSpec(memory_space=pl.ANY)] * len(earlier),
        out_specs=[
            rows_spec(local_len, 3 * width),
            rows_spec(local_len, width),
            rows_spec(local_len, D),
        ],
        out_shape=[
            shaped(rows, 3 * width, jnp.bfloat16),
            shaped(rows, width, jnp.bfloat16),
            shaped(rows, D, jnp.float32),
        ],
        scratch_shapes=[
            pltpu.VMEM((D, 3 * width), jnp.bfloat16),
            pltpu.VMEM((width, D), jnp.bfloat16),
        ],
        compiler_params=params(),
        cost_estimate=pl.CostEstimate(
            flops=rows * D * width * 8, bytes_accessed=rows * D * 8, transcendentals=rows * 2048
        ),
    )(normed_in, store, store, *earlier)


def attend_back_kernel(
    grad_branch, projected, qkv_tiles, proj_tiles, grad_qkv, partial, w_qkv, w_proj
):
    @pl.when(pl.program_id(0) == 0)
    def _():
        untile_into(w_qkv, qkv_tiles)
        untile_into(w_proj, proj_tiles)

    grad_attended = low(against_value(grad_branch[...], w_proj[...]))
    values = projected[...]
    width = values.shape[1] // 3
    grads = [[], [], []]
    for head in range(width // HD):
        at = head * HD
        query = values[:, at : at + HD]
        key_rows = values[:, width + at : width + at + HD]
        value_rows = values[:, 2 * width + at : 2 * width + at + HD]
        grad_here = grad_attended[:, at : at + HD]
        scores = against_value(key_rows, query) * HD ** (-0.5)
        exponent = jnp.exp(scores - jnp.max(scores, 0, keepdims=True))
        probabilities = exponent * (1.0 / jnp.sum(exponent, 0, keepdims=True))
        grad_prob = against_value(value_rows, grad_here)
        grad_scores = low(
            probabilities
            * (grad_prob - jnp.sum(probabilities * grad_prob, 0, keepdims=True))
        )
        grads[0].append(low(over_rows(grad_scores, key_rows) * HD ** (-0.5)))
        grads[1].append(low(product(grad_scores, query) * HD ** (-0.5)))
        grads[2].append(low(product(low(probabilities), grad_here)))
    result = jnp.concatenate(grads[0] + grads[1] + grads[2], 1)
    grad_qkv[...] = result
    partial[...] = against_value(result, w_qkv[...])


def attend_back_call(grad_branch, projected, store, tp_parts, local_len):
    rows = grad_branch.shape[0]
    width = D // tp_parts
    return pl.pallas_call(
        attend_back_kernel,
        grid=(rows // local_len,),
        in_specs=[
            rows_spec(local_len, D),
            rows_spec(local_len, 3 * width),
            weight_spec(0, tp_parts),
            weight_spec(1, tp_parts),
        ],
        out_specs=[rows_spec(local_len, 3 * width), rows_spec(local_len, D)],
        out_shape=[shaped(rows, 3 * width, jnp.bfloat16), shaped(rows, D, jnp.float32)],
        scratch_shapes=[
            pltpu.VMEM((D, 3 * width), jnp.bfloat16),
            pltpu.VMEM((width, D), jnp.bfloat16),
        ],
        compiler_params=params(),
        cost_estimate=pl.CostEstimate(
            flops=rows * D * width * 10, bytes_accessed=rows * D * 8, transcendentals=rows * 2048
        ),
    )(grad_branch, projected, store, store)


def mlp_chunk(tp_parts):
    return min(4 * B, F // tp_parts)


def chunk_specs(tp_parts):
    amount = D * mlp_chunk(tp_parts) // (B * B)
    up, down = (segments(tp_parts)[kind][1] // amount for kind in (2, 3))
    return [
        pl.BlockSpec((amount, B, B), lambda step: (up + step, 0, 0)),
        pl.BlockSpec((amount, B, B), lambda step: (down + step, 0, 0)),
    ]


def store_of_tile(tile, tp_parts):
    amount, begin = segments(tp_parts)[2]
    within = tile % sum(count for count, _ in segments(tp_parts)) - begin
    columns, wide_step = F // tp_parts // B, mlp_chunk(tp_parts) // B
    row, column = within // columns, within % columns
    moved = (column // wide_step * (D // B) + row) * wide_step + column % wide_step
    return jnp.where((within >= 0) & (within < amount), tile + moved - within, tile)


def add_to(total_ref, value):
    @pl.when(pl.program_id(0) == 0)
    def _():
        total_ref[...] = value

    @pl.when(pl.program_id(0) > 0)
    def _():
        total_ref[...] += value


def mlp_kernel(normed_mid, up_tiles, down_tiles, hidden, partial, w_up, w_down):
    untile_into(w_up, up_tiles)
    untile_into(w_down, down_tiles)
    values = product(normed_mid[...], w_up[...])
    hidden[...] = values
    add_to(partial, product(low(gelu_tanh(values)), w_down[...]))


def chunk_scratch(tp_parts):
    width = mlp_chunk(tp_parts)
    return [pltpu.VMEM((D, width), jnp.bfloat16), pltpu.VMEM((width, D), jnp.bfloat16)]


def all_rows(rows):
    return pl.BlockSpec((rows, D), lambda step: (0, 0))


def mlp_call(normed_mid, store, tp_parts, local_len):
    rows = normed_mid.shape[0]
    width, step_width = F // tp_parts, mlp_chunk(tp_parts)
    step_spec = pl.BlockSpec((rows, step_width), lambda step: (0, step))
    return pl.pallas_call(
        mlp_kernel,
        grid=(width // step_width,),
        in_specs=[all_rows(rows)] + chunk_specs(tp_parts),
        out_specs=[step_spec, all_rows(rows)],
        out_shape=[shaped(rows, width, jnp.float32), shaped(rows, D, jnp.float32)],
        scratch_shapes=chunk_scratch(tp_parts),
        compiler_params=params(),
        cost_estimate=pl.CostEstimate(
            flops=rows * D * width * 4,
            bytes_accessed=rows * D * 12 + 4 * D * width,
            transcendentals=rows * width,
        ),
    )(normed_mid, store, store)


def mlp_back_kernel(
    grad_mlp, hidden, up_tiles, down_tiles, activation, grad_hidden, partial, w_up, w_down
):
    untile_into(w_up, up_tiles)
    untile_into(w_down, down_tiles)
    values = hidden[...]
    factor = math.sqrt(2.0 / math.pi)
    square = values * values
    bent = jnp.tanh(factor * (values + 0.044715 * (square * values)))
    half_up = 0.5 * (1.0 + bent)
    activation[...] = low(values * half_up)
    slope = half_up + 0.5 * values * (1.0 - bent * bent) * (
        factor * (1.0 + 3.0 * 0.044715 * square)
    )
    grad = low(against_value(grad_mlp[...], w_down[...]) * slope)
    grad_hidden[...] = grad
    add_to(partial, against_value(grad, w_up[...]))


def mlp_back_call(grad_mlp, hidden, store, tp_parts, local_len):
    rows = grad_mlp.shape[0]
    width, step_width = F // tp_parts, mlp_chunk(tp_parts)
    step_spec = pl.BlockSpec((rows, step_width), lambda step: (0, step))
    return pl.pallas_call(
        mlp_back_kernel,
        grid=(width // step_width,),
        in_specs=[all_rows(rows), step_spec] + chunk_specs(tp_parts),
        out_specs=[step_spec, step_spec, all_rows(rows)],
        out_shape=[
            shaped(rows, width, jnp.bfloat16),
            shaped(rows, width, jnp.bfloat16),
            shaped(rows, D, jnp.float32),
        ],
        scratch_shapes=chunk_scratch(tp_parts),
        compiler_params=params(),
        cost_estimate=pl.CostEstimate(
            flops=rows * D * width * 4,
            bytes_accessed=rows * D * 16 + 4 * D * width,
            transcendentals=rows * width,
        ),
    )(grad_mlp, hidden, store, store)


def modes_call(cond_act, store, tp_parts):
    rows = cond_act.shape[0]
    width = 6 * D // tp_parts

    def kernel(left, tile_set, out):
        for column in range(width // B):
            total_here = 0.0
            for row in range(D // B):
                total_here = total_here + product(
                    left[:, row * B : (row + 1) * B], tile_set[row * (width // B) + column]
                )
            out[:, column * B : (column + 1) * B] = total_here

    return pl.pallas_call(
        kernel,
        grid=(1,),
        in_specs=[rows_spec(rows, D), weight_spec(4, tp_parts)],
        out_specs=rows_spec(rows, width),
        out_shape=shaped(rows, width, jnp.float32),
        compiler_params=params(),
    )(cond_act, store)


def three_parts(value):
    first = low(value)
    rest = value - wide(first)
    second = low(rest)
    return jnp.concatenate([first, second, low(rest - wide(second))], 0)


def against_low(value, weight):
    rows = value.shape[0]
    summed = against(three_parts(value), weight)
    return summed[:rows] + summed[rows : 2 * rows] + summed[2 * rows :]


def modes_back_call(grads, store, tp_parts):
    rows = grads.shape[0]
    width = 6 * D // tp_parts
    parts = three_parts(grads)

    def kernel(left, tile_set, out):
        for row in range(D // B):
            total_here = 0.0
            for column in range(width // B):
                total_here = total_here + against_value(
                    left[:, column * B : (column + 1) * B],
                    tile_set[row * (width // B) + column],
                )
            out[:, row * B : (row + 1) * B] = total_here

    summed = pl.pallas_call(
        kernel,
        grid=(1,),
        in_specs=[rows_spec(3 * rows, width), weight_spec(4, tp_parts)],
        out_specs=rows_spec(3 * rows, D),
        out_shape=shaped(3 * rows, D, jnp.float32),
        compiler_params=params(),
    )(parts, store)
    return summed[:rows] + summed[rows : 2 * rows] + summed[2 * rows :]


def weight_grad_call(lefts, rights, places, first_tile, held):
    height, breadth = lefts[0].shape[1], rights[0].shape[1]
    steps = min(4, height // B)
    count = len(lefts)
    row_tiles, column_tiles = height // B // steps, breadth // B
    amount = row_tiles * column_tiles
    given = [array for _, _, array in held if array is not None]

    def kernel(place, *refs):
        left_refs, right_refs = refs[:count], refs[count : 2 * count]
        outs = refs[2 * count + len(given) : 2 * count + len(given) + len(held)]
        ready, sem = refs[-2], refs[-1]
        step = pl.program_id(0)
        slot = lax.rem(step, 2)

        def drain(which):
            pltpu.make_async_copy(
                ready.at[which], outs[0].at[pl.ds(0, amount)], sem.at[which]
            ).wait()

        @pl.when(step >= 2)
        def _():
            drain(slot)

        block = over_rows(left_refs[0][...], right_refs[0][...])
        for left, right in zip(left_refs[1:], right_refs[1:]):
            block = block + over_rows(left[...], right[...])
        block = low(block)
        for row in range(row_tiles):
            for column in range(column_tiles):
                ready[slot, row * column_tiles + column] = block[
                    row * B : (row + 1) * B, column * B : (column + 1) * B
                ]

        def send(index, carry):
            where_to = place[first_tile + step * amount + index]
            for number, (begin, _, _) in enumerate(held):
                end = held[number + 1][0] if number + 1 < len(held) else 1 << 30
                copy = pltpu.make_async_copy(
                    ready.at[slot, index], outs[number].at[where_to - begin], sem.at[slot]
                )
                if len(held) == 1:
                    copy.start()
                else:
                    pl.when((where_to >= begin) & (where_to < end))(copy.start)
            return carry

        lax.fori_loop(0, amount, send, 0)

        @pl.when(step == steps - 1)
        def _():
            drain(slot)
            if steps > 1:
                drain(1 - slot)

    rows = [left.shape[0] for left in lefts]
    anywhere = pl.BlockSpec(memory_space=pl.ANY)
    in_specs = [
        pl.BlockSpec((size, height // steps), lambda step, place: (0, step)) for size in rows
    ] + [
        pl.BlockSpec((size, breadth), lambda step, place: (0, 0), pipeline_mode=pl.Buffered(1))
        for size in rows
    ]
    in_specs += [anywhere] * len(given)
    operands = [places, *lefts, *rights, *given]
    aliases = {}
    for number, (_, _, array) in enumerate(held):
        if array is not None:
            aliases[1 + 2 * count + len(aliases)] = number
    results = pl.pallas_call(
        kernel,
        grid_spec=pltpu.PrefetchScalarGridSpec(
            num_scalar_prefetch=1,
            grid=(steps,),
            in_specs=in_specs,
            out_specs=[anywhere] * len(held),
            scratch_shapes=[
                pltpu.VMEM((2, amount, B, B), jnp.bfloat16),
                pltpu.SemaphoreType.DMA((2,)),
            ],
        ),
        out_shape=[
            jax.ShapeDtypeStruct((places_here, B, B), jnp.bfloat16) for _, places_here, _ in held
        ],
        input_output_aliases=aliases,
        compiler_params=params(),
        cost_estimate=pl.CostEstimate(
            flops=2 * sum(rows) * height * breadth,
            bytes_accessed=2 * (sum(rows) * (height + breadth) + height * breadth),
            transcendentals=0,
        ),
    )(*operands)
    return [
        (begin, places_here, array) for (begin, places_here, _), array in zip(held, results)
    ]


def place_call(pieces, targets, held, earlier=()):
    count = len(pieces)
    given = [array for _, _, array in held if array is not None]

    def kernel(target, *refs):
        begin_outs = count + len(given) + len(earlier)
        outs = refs[begin_outs : begin_outs + len(held)]
        token = refs[begin_outs + len(held)]
        buffers, loaded, stored = refs[-2 - count : -2], refs[-2], refs[-1]
        token[...] = jnp.zeros_like(token)
        for number in range(count):
            pltpu.make_async_copy(refs[number], buffers[number], loaded.at[number]).start()
        for number, (piece, begin) in enumerate(pieces):
            pltpu.make_async_copy(refs[number], buffers[number], loaded.at[number]).wait()

            def send(index, carry):
                where_to = target[begin + index]
                left = True
                for out_number, (first, amount, _) in enumerate(held):
                    last = out_number == len(held) - 1
                    inside = (where_to >= first) & (where_to < first + amount - 1)
                    at = where_to - first
                    if last:
                        at = jnp.where(inside, at, amount - 1)
                        inside = left
                    else:
                        left = jnp.logical_not(inside)
                    copy = pltpu.make_async_copy(
                        buffers[number].at[index], outs[out_number].at[at], stored.at[number]
                    )
                    if len(held) == 1:
                        copy.start()
                    else:
                        pl.when(inside)(copy.start)
                return carry

            lax.fori_loop(0, piece.shape[0], send, 0)
        for number, (piece, begin) in enumerate(pieces):
            pltpu.make_async_copy(
                buffers[number], outs[0].at[pl.ds(0, piece.shape[0])], stored.at[number]
            ).wait()

    anywhere = pl.BlockSpec(memory_space=pl.ANY)
    operands = [targets] + [piece for piece, _ in pieces] + given + list(earlier)
    aliases = {}
    for number, (_, _, array) in enumerate(held):
        if array is not None:
            aliases[1 + count + len(aliases)] = number
    results = pl.pallas_call(
        kernel,
        grid_spec=pltpu.PrefetchScalarGridSpec(
            num_scalar_prefetch=1,
            grid=(1,),
            in_specs=[anywhere] * (len(operands) - 1),
            out_specs=[anywhere] * len(held) + [pl.BlockSpec((8, B), lambda step, target: (0, 0))],
            scratch_shapes=[pltpu.VMEM(piece.shape, jnp.bfloat16) for piece, _ in pieces]
            + [pltpu.SemaphoreType.DMA((count,))] * 2,
        ),
        out_shape=[jax.ShapeDtypeStruct((amount, B, B), jnp.bfloat16) for _, amount, _ in held]
        + [jax.ShapeDtypeStruct((8, B), jnp.int32)],
        input_output_aliases=aliases,
        compiler_params=params(),
        cost_estimate=pl.CostEstimate(
            flops=0,
            bytes_accessed=sum(4 * piece.shape[0] * B * B for piece, _ in pieces),
            transcendentals=0,
        ),
    )(*operands)
    return [(first, amount, array) for (first, amount, _), array in zip(held, results)], results[-1]


def chips_sum(value):
    for swap in (swap_y, swap_x, lambda part: swap_f(part, 2), lambda part: swap_f(part, 4)):
        value = value + swap(value)
    return value


LOT = 8


def lots(count):
    return (count + LOT - 1) // LOT


def bring_strays(store, strays, count, owned_tiles, ordering, slots, me, tp_parts):
    def body(state):
        lot, held = state
        tiles = lax.dynamic_slice_in_dim(strays, lot * LOT, LOT, 0)
        valid = lot * LOT + jnp.arange(LOT) < count
        here = ordering[tiles]
        mine = valid & (here // slots == me)
        sent = jnp.where(mine[:, None, None], owned_tiles[here % slots], 0)
        sent = chips_sum(sent)
        at = jnp.where(valid, store_of_tile(tiles, tp_parts), held.shape[0])
        return lot + 1, held.at[at].set(sent, mode="drop")

    return lax.while_loop(lambda state: state[0] < lots(count), body, (0, store))[1]


def sum_strays(owned, parts, strays, count, ordering, slots, me):
    def body(state):
        lot, held = state
        tiles = lax.dynamic_slice_in_dim(strays, lot * LOT, LOT, 0)
        valid = lot * LOT + jnp.arange(LOT) < count
        summed = chips_sum(wide(lax.dynamic_slice_in_dim(parts, lot * LOT, LOT, 0)))
        here = ordering[tiles]
        at = jnp.where(valid & (here // slots == me), here % slots, slots)
        return lot + 1, held.at[at].set(summed, mode="drop")

    return lax.while_loop(lambda state: state[0] < lots(count), body, (0, owned))[1]


def normed_value(stream):
    centred = stream - jnp.mean(stream, -1, keepdims=True)
    rate = lax.rsqrt(jnp.mean(centred * centred, -1, keepdims=True) + EPS_NORM)
    return centred * rate, rate


def rows_kernel_call(kernel, wide_ins, mode_ins, outs, earlier=()):
    count = len(wide_ins) + len(mode_ins)

    def body(*refs):
        kernel(*refs[:count], *refs[count + len(earlier) :])

    own, group = wide_ins[0].shape[:2]
    rows = pl.BlockSpec((1, group, D), lambda step: (step, 0, 0))
    few = lambda count: pl.BlockSpec((1, count, D), lambda step: (step, 0, 0))
    return pl.pallas_call(
        body,
        grid=(own,),
        in_specs=[rows] * len(wide_ins)
        + [few(modes.shape[1]) for modes in mode_ins]
        + [pl.BlockSpec(memory_space=pl.ANY)] * len(earlier),
        out_specs=[rows if count is None else few(count) for count, _ in outs],
        out_shape=[
            jax.ShapeDtypeStruct((own, group if count is None else count, D), kind)
            for count, kind in outs
        ],
        compiler_params=params(),
        cost_estimate=pl.CostEstimate(
            flops=own * group * D * 20,
            bytes_accessed=own * group * D * 4 * (len(wide_ins) + len(outs)),
            transcendentals=own * group,
        ),
    )(*wide_ins, *mode_ins, *earlier)


def modulate_call(stream, modes, shift, scale):
    def kernel(values, mode, out):
        out[0] = low(
            normed_value(values[0])[0] * (1.0 + mode[0, scale : scale + 1, :])
            + mode[0, shift : shift + 1, :]
        )

    return rows_kernel_call(kernel, [stream], [modes], [(None, jnp.bfloat16)])[0]


def residual_call(stream, terms, modes, gate, next_modes, shift, scale, earlier=()):
    def kernel(*refs):
        values, term_refs = refs[0], refs[1 : 1 + len(terms)]
        mode, mode_next, branch, stream_new, out = refs[1 + len(terms) :]
        summed = term_refs[0][0]
        for term in term_refs[1:]:
            summed = summed + term[0]
        branch[0] = summed
        result = values[0] + mode[0, gate : gate + 1, :] * summed
        stream_new[0] = result
        out[0] = low(
            normed_value(result)[0] * (1.0 + mode_next[0, scale : scale + 1, :])
            + mode_next[0, shift : shift + 1, :]
        )

    shape = stream.shape
    return rows_kernel_call(
        kernel,
        [stream] + [term.reshape(shape) for term in terms],
        [modes, next_modes],
        [(None, jnp.float32), (None, jnp.float32), (None, jnp.bfloat16)],
        earlier,
    )


def back_call(stream, terms, upstream, modes, scale, below, earlier=()):
    shape = stream.shape
    wide_ins = [stream] + [term.reshape(shape) for term in terms]
    if upstream is not None:
        wide_ins.append(upstream)
    mode_ins = [modes]
    outs = [(None, jnp.float32), (3 if below else 2, jnp.float32)]
    if below:
        branch, branch_modes, gate = below
        wide_ins.append(branch)
        mode_ins.append(branch_modes)
        outs.append((None, jnp.bfloat16))

    def kernel(*refs):
        ins, modes_in = refs[: len(wide_ins)], refs[len(wide_ins) : len(wide_ins) + len(mode_ins)]
        results = refs[len(wide_ins) + len(mode_ins) :]
        grad = ins[1][0]
        for term in ins[2 : 1 + len(terms)]:
            grad = grad + term[0]
        normal, rate = normed_value(ins[0][0])
        results[1][0, 0:1, :] = jnp.sum(grad, 0, keepdims=True)
        results[1][0, 1:2, :] = jnp.sum(grad * normal, 0, keepdims=True)
        grad = grad * (1.0 + modes_in[0][0, scale : scale + 1, :])
        grad = rate * (
            grad
            - jnp.mean(grad, -1, keepdims=True)
            - normal * jnp.mean(grad * normal, -1, keepdims=True)
        )
        if upstream is not None:
            grad = grad + ins[1 + len(terms)][0]
        results[0][0] = grad
        if below:
            results[1][0, 2:3, :] = jnp.sum(grad * ins[-1][0], 0, keepdims=True)
            results[2][0] = low(modes_in[1][0, gate : gate + 1, :] * grad)

    return rows_kernel_call(kernel, wide_ins, mode_ins, outs, earlier)


def update_kernel(clip, grad, master, first, second, bases, master_out, first_out, second_out, low_out):
    eye = lax.broadcasted_iota(jnp.int32, (B, B), 0) == lax.broadcasted_iota(jnp.int32, (B, B), 1)
    left_row = bases[:, 0:1, :]
    right_row = bases[:, 1:2, :]
    left_col = jnp.sum(jnp.where(eye[None], left_row, 0.0), 2, keepdims=True)
    left_scaled = left_col * (2.0 / jnp.sum(left_row * left_row, 2, keepdims=True))
    right_scaled = right_row * (2.0 / jnp.sum(right_row * right_row, 2, keepdims=True))

    def turn(middle):
        middle = middle - left_scaled * jnp.sum(left_col * middle, 1, keepdims=True)
        return middle - jnp.sum(middle * right_row, 2, keepdims=True) * right_scaled

    turned = turn(clip[0, 0] * grad[...])
    first_new = 0.5 * first[...] + 0.5 * turned
    second_new = 0.5 * second[...] + 0.5 * turned * turned
    first_out[...] = first_new
    second_out[...] = second_new
    master_new = master[...] - RATE * turn(first_new / (jnp.sqrt(second_new) + 1e-08))
    master_out[...] = master_new
    low_out[...] = master_new.astype(jnp.bfloat16)


def update_tiles(clip_factor, grad, master, first, second, bases):
    slots = grad.shape[0]
    amount = max(count for count in (1, 2, 3, 4, 6, 8) if slots % count == 0)
    tile_spec = pl.BlockSpec((amount, B, B), lambda step: (step, 0, 0))
    whole = jax.ShapeDtypeStruct(grad.shape, jnp.float32)
    return pl.pallas_call(
        update_kernel,
        grid=(slots // amount,),
        in_specs=[pl.BlockSpec(memory_space=pltpu.SMEM)]
        + [tile_spec] * 4
        + [pl.BlockSpec((amount, 2, B), lambda step: (step, 0, 0))],
        out_specs=[tile_spec] * 4,
        out_shape=[whole, whole, whole, jax.ShapeDtypeStruct(grad.shape, jnp.bfloat16)],
        compiler_params=params(),
        cost_estimate=pl.CostEstimate(
            flops=slots * B * B * 30, bytes_accessed=slots * B * B * 30, transcendentals=slots * B * B
        ),
    )(clip_factor.reshape(1, 1), grad, master, first, second, bases)


def on_device(
    latents,
    noise,
    timesteps,
    labels,
    owners,
    tiles_low,
    tiles_master,
    tiles_first,
    tiles_second,
    bases,
    else_low,
    else_master,
    else_first,
    else_second,
):
    box = is_box()
    tp_parts = lax.axis_size("tp")
    tp_index = lax.axis_index("tp")
    ctx_parts = lax.axis_size("ctx")
    fsdp_parts = lax.axis_size("fsdp")
    images = latents.shape[0]
    local_len = latents.shape[1]
    slots = tiles_low.shape[1]
    sp_rows = images * local_len // tp_parts
    first_row = tp_index * sp_rows
    own = max(1, sp_rows // local_len)
    group = sp_rows // own
    first_image = first_row // local_len
    element_count = images * fsdp_parts * ctx_parts * local_len * P_SIZE
    ordering = jnp.argsort(owners, stable=True)
    inverse = jnp.argsort(ordering)
    all_tiles = inverse.shape[0]
    per_layer = all_tiles // L
    if box:
        early = early_slots(slots)
        me = lax.axis_index("fsdp") * ctx_parts + lax.axis_index("ctx")
        tile = jnp.arange(all_tiles, dtype=jnp.int32)
        owner, slot = inverse // slots, inverse % slots
        is_early = slot < early
        place_early = early_place(owner, slot, early)
        place_late = late_place(owner, slot - early, slots - early)
        gather_places = jnp.where(is_early, place_early, 16 * early + place_late)
        targets = store_of_tile(jnp.argsort(gather_places), tp_parts).astype(jnp.int32)
        is_stray = jnp.logical_not(is_early) & (tile < per_layer)
        stray_count = jnp.sum(is_stray.astype(jnp.int32))
        stray_rank = jnp.cumsum(is_stray.astype(jnp.int32)) - 1
        room = 16 * (slots - early)
        strays = jnp.argsort(jnp.where(is_stray, tile, all_tiles + tile)).astype(jnp.int32)
        strays = jnp.concatenate([strays, jnp.zeros((LOT,), jnp.int32)])
        places = jnp.where(
            is_stray,
            room + 16 * (early + 1) + stray_rank,
            jnp.where(is_early, room + early_place(owner, slot, early + 1), place_late),
        ).astype(jnp.int32)
        stores = [(0, per_layer + 1, None), (per_layer, per_layer + 1, None)]
        late_store = None

        def place_early_tiles(tile_group, *earlier):
            nonlocal stores
            stores, token = place_call(tile_group, targets, stores, earlier)
            return token

        def place_late_tiles(tile_group, *earlier):
            nonlocal late_store
            tile_group = [(piece, 16 * early + at) for piece, at in tile_group]
            if late_store is None:
                late_store = [stores[1]]
            late_store, token = place_call(tile_group, targets, late_store, earlier)
            return token

        late_store = None
        else_parts, finish_gather, arriving = gather_tiles(
            tiles_low[0], early, place_early_tiles, place_late_tiles, else_low, targets
        )
        store = [
            bring_strays(
                stores[0][2], strays, stray_count, tiles_low[0], inverse, slots, me, tp_parts
            ),
            None,
        ]
        held = [(0, room, None), (room, 16 * (slots + 1) + LOT, None)]
    else:
        places = jnp.arange(all_tiles, dtype=jnp.int32)
        tile_stored = jnp.argsort(store_of_tile(places, tp_parts))
        gathered = lax.all_gather(tiles_low, ("fsdp", "ctx"), axis=1, tiled=True)[0]
        gathered = gathered[inverse[tile_stored]]
        store = [gathered[:per_layer], gathered[per_layer:]]
        held = [(0, all_tiles, None)]
        else_parts = cut_else(lax.all_gather(else_low, ("fsdp", "ctx", "tp"), axis=0, tiled=True))
    (patch_weight, class_table, time_first, time_second), final_rows, head_weight = else_parts
    features_low = low(time_features(timesteps))
    onehot = low(labels[:, None] == jnp.arange(NCLS)[None, :])
    time_hidden = product(features_low, time_first)
    time_act = low(jax.nn.silu(time_hidden))
    condition = product(time_act, time_second) + product(onehot, class_table)
    cond_act = low(jax.nn.silu(condition))
    def modes_of(layer_no):
        return lax.dynamic_slice_in_dim(
            columns_in(modes_call(cond_act, store[layer_no], tp_parts)), first_image, own, 0
        ).reshape(own, 6, D)

    modes = [modes_of(0)]
    final_modes = lax.dynamic_slice_in_dim(
        final_product(cond_act, final_rows), first_image, own, 0
    )
    row_index = first_row + jnp.arange(sp_rows)
    signal = signal_level(timesteps)
    noisy_input = (
        jnp.sqrt(signal)[:, None, None] * latents + jnp.sqrt(1.0 - signal)[:, None, None] * noise
    )
    noisy_rows = low(
        lax.dynamic_slice_in_dim(
            noisy_input.reshape(images * local_len, P_SIZE), first_row, sp_rows, 0
        )
    )
    target = lax.dynamic_slice_in_dim(
        noise.reshape(images * local_len, P_SIZE), first_row, sp_rows, 0
    )
    stream = (product(noisy_rows, patch_weight) + position_table(row_index % local_len)).reshape(
        own, group, D
    )
    normed_in = modulate_call(stream, modes[0], 0, 1)
    kept = []
    for layer_no in range(L):
        row_sets = rows_in(normed_in.reshape(sp_rows, D))
        halves, terms = each_half(
            lambda rows: attend_call(
                rows,
                store[layer_no],
                tp_parts,
                local_len,
                arriving if box and layer_no == 0 and rows is row_sets[0] else (),
            ),
            row_sets,
        )
        branch, middle, normed_mid = residual_call(
            stream,
            terms,
            modes[layer_no],
            2,
            modes[layer_no],
            3,
            4,
        )
        mid_sets = rows_in(normed_mid.reshape(sp_rows, D))
        hidden, terms = each_half(
            lambda rows: mlp_call(rows, store[layer_no], tp_parts, local_len), mid_sets
        )
        last = layer_no == L - 1
        if not last:
            if box:
                finish_gather(terms[0])
                store[1] = late_store[0][2]
            modes.append(modes_of(layer_no + 1))
        mlp_out, stream_new, normed_in = residual_call(
            middle,
            terms,
            modes[layer_no],
            5,
            final_modes if last else modes[layer_no + 1],
            0,
            1,
        )
        kept.append((stream, row_sets, halves, branch, middle, mid_sets, hidden, mlp_out))
        stream = stream_new
    head_low = normed_in.reshape(sp_rows, D)
    mismatch = product(head_low, head_weight) - target
    loss_part = jnp.sum(mismatch * mismatch) / element_count
    grad_pred = low(2.0 * mismatch / element_count)
    grad_head = over_rows(grad_pred, head_low)
    upstream, final_sums, grad_low = back_call(
        stream,
        [against(grad_pred, head_weight)],
        None,
        final_modes,
        1,
        (kept[-1][7], modes[-1], 5),
    )
    grad_final = final_sums[:, :2].reshape(own, 2 * D)
    gate_sum = final_sums[:, 2:]
    starts = [begin for _, begin in segments(tp_parts)]
    mode_width = 6 * D // tp_parts
    fill = (-3 * images) % 16
    conds = jnp.pad(jnp.concatenate([cond_act] * 3, 0), ((0, fill), (0, 0)))

    def all_images(values):
        return tp_sum(
            lax.dynamic_update_slice_in_dim(
                jnp.zeros((images, values.shape[1]), jnp.float32), values, first_image, 0
            )
        )

    grad_final = all_images(grad_final)
    cond_wide = wide(cond_act)

    def image_part(columns):
        packed = jnp.concatenate(columns, 1)
        packed = jnp.pad(packed, ((0, 0), (0, -packed.shape[1] % 256)))
        part = packed.shape[1] // 2
        return lax.dynamic_slice_in_dim(packed, tp_index * part, part, 1)

    label_column = jnp.broadcast_to(wide(labels)[:, None], (images, 128))
    early_columns = [label_column, wide(features_low), wide(time_act), cond_wide, grad_final]
    grad_cond_act = 0.0
    for layer_no in reversed(range(L)):
        stream, row_sets, halves, branch, middle, mid_sets, hidden, mlp_out = kept[layer_no]
        base = layer_no * per_layer
        grad_sets = rows_in(grad_low.reshape(sp_rows, D))
        results, terms = each_half(
            lambda pair: mlp_back_call(pair[0], pair[1], store[layer_no], tp_parts, local_len),
            [(rows, hidden_here[0]) for rows, hidden_here in zip(grad_sets, hidden)],
        )
        held = weight_grad_call(
            [result[0] for result in results], grad_sets, places, base + starts[3], held
        )
        held = weight_grad_call(
            mid_sets, [result[1] for result in results], places, base + starts[2], held
        )
        upstream, mlp_sums, grad_low = back_call(
            middle, terms, upstream, modes[layer_no], 4, (branch, modes[layer_no], 2)
        )
        if box and layer_no == 0:
            late_sums = scatter_late(
                late_parts,
                slots - early,
                lanes,
                late_first,
                tp_sum(grad_head),
                image_part(early_columns),
                upstream,
                grad_cond_early,
            )
        grad_sets = rows_in(grad_low.reshape(sp_rows, D))
        results, terms = each_half(
            lambda pair: attend_back_call(pair[0], pair[1], store[layer_no], tp_parts, local_len),
            [(rows, half[0]) for rows, half in zip(grad_sets, halves)],
        )
        held = weight_grad_call(
            [half[1] for half in halves], grad_sets, places, base + starts[1], held
        )
        held = weight_grad_call(
            row_sets, [result[0] for result in results], places, base + starts[0], held
        )
        below = None if layer_no == 0 else (kept[layer_no - 1][7], modes[layer_no - 1], 5)
        found = back_call(
            stream,
            terms,
            upstream,
            modes[layer_no],
            1,
            below,
            (late_sums[0][0],) if box and layer_no == 0 else (),
        )
        grad_modes = jnp.concatenate(
            [found[1][:, :2], mlp_sums[:, 2:], mlp_sums[:, :2], gate_sum], 1
        ).reshape(own, 6 * D)
        mode_image = lax.dynamic_slice_in_dim(
            all_images(grad_modes), tp_index * mode_width, mode_width, 1
        )
        held = weight_grad_call(
            [conds],
            [jnp.pad(three_parts(mode_image), ((0, fill), (0, 0)))],
            places,
            base + starts[4],
            held,
        )
        grad_cond_act = grad_cond_act + modes_back_call(mode_image, store[layer_no], tp_parts)
        upstream = found[0]
        if below:
            grad_low, gate_sum = found[2], found[1][:, 2:]
        if box and layer_no == L - 1:
            grad_low = after(grad_low, held[0][2], held[1][2])
            lanes = Lanes()
            late_parts = held[0][2]
            late_first = scatter_late_first(late_parts, slots - early, lanes)
            grad_cond_early = grad_cond_act
            held = held[1:]
    grad_patch = over_rows(noisy_rows, low(upstream).reshape(sp_rows, D))
    grad_cond_act = tp_sum(grad_cond_act) + final_product_back(grad_final, final_rows)
    grad_condition = jax.vjp(jax.nn.silu, condition)[1](grad_cond_act)[0]
    grad_time_hidden = jax.vjp(jax.nn.silu, time_hidden)[1](
        against_low(grad_condition, time_second)
    )[0]
    if box:
        patch_sum = tp_sum(grad_patch).reshape(1, B, B)
        patch_first = low(patch_sum)
        parts = lax.dynamic_update_slice_in_dim(
            held[0][2],
            jnp.where(tp_index == 0, patch_first, low(patch_sum - wide(patch_first))),
            early_place(0, early, early + 1),
            0,
        )
        owned, owned_late, late_images, head_sum, early_images = scatter_early(
            parts,
            early + 1,
            lanes,
            *late_sums,
            image_part([grad_time_hidden, grad_condition]),
        )
        late_images = columns_in(late_images)
        early_images = columns_in(early_images)
        head_rows = head_sum.T.reshape(P_SIZE, D)
        patch_rows = tp_sum(owned[early]).reshape(P_SIZE, D)
        owned = jnp.concatenate([owned[:early], owned_late], 0)
        owned = sum_strays(
            owned, parts[16 * (early + 1) :], strays, stray_count, inverse, slots, me
        )
    else:
        owned = lax.psum_scatter(
            wide(held[0][2])[ordering], ("fsdp", "ctx"), scatter_dimension=0, tiled=True
        )
        patch_rows = lax.psum(grad_patch, ("fsdp", "ctx", "tp"))
        head_rows = lax.psum(grad_head, ("fsdp", "ctx", "tp")).T.reshape(P_SIZE, D)
        late_images = gather_images(jnp.concatenate([grad_time_hidden, grad_condition], 1))
        early_images = gather_images(jnp.concatenate(early_columns, 1))
    all_hidden, all_condition = jnp.split(late_images, 2, 1)
    cuts = [128]
    for length in (TFREQ, D, D):
        cuts.append(cuts[-1] + length)
    all_labels, all_features, all_time, all_cond, all_final = jnp.split(early_images, cuts, 1)
    all_final = all_final[:, : 2 * D]
    all_onehot = wide(all_labels[:, :1] == jnp.arange(NCLS, dtype=jnp.float32)[None, :])
    share = else_low.shape[0]
    device = (lax.axis_index("fsdp") * ctx_parts + lax.axis_index("ctx")) * tp_parts + tp_index
    begin = device * share
    row_total = else_low.shape[0] * fsdp_parts * ctx_parts * tp_parts // D
    row_count = min(share // D + 2, row_total)
    begin_row = jnp.minimum(begin // D, row_total - row_count)
    row_ids = begin_row + jnp.arange(row_count)
    edge = jnp.zeros((all_cond.shape[0], P_SIZE), jnp.float32)
    factors = jnp.concatenate(
        [edge, all_onehot, all_features, all_time, jnp.repeat(all_cond, 2, axis=1), edge], 1
    )
    factors = lax.dynamic_slice_in_dim(factors, begin_row, row_count, 1)
    first_start = P_SIZE + NCLS
    second_start = first_start + TFREQ
    final_start = second_start + D

    def rows_of(chosen, right):
        return contract("ic,id->cd", jnp.where(chosen[None, :], factors, 0.0), right)

    in_first = (row_ids >= first_start) & (row_ids < second_start)
    in_final = row_ids >= final_start
    odd = (row_ids - final_start) % 2 == 1
    near = rows_of(in_first, all_hidden)
    near = near + rows_of(jnp.logical_not(in_first | in_final), all_condition)
    near = near + rows_of(in_final & jnp.logical_not(odd), all_final[:, :D])
    near = near + rows_of(in_final & odd, all_final[:, D:])
    for begin_here, token_rows in ((0, patch_rows), (row_total - P_SIZE, head_rows)):
        here = row_ids - begin_here
        inside = (here >= 0) & (here < P_SIZE)
        near = jnp.where(
            inside[:, None], token_rows[jnp.clip(here, 0, P_SIZE - 1)], near
        )
    else_grad = lax.dynamic_slice_in_dim(near.reshape(-1), begin - begin_row * D, share, 0)
    squares = jnp.sum(owned * owned) + jnp.sum(else_grad * else_grad)
    totals = total(jnp.stack([loss_part, squares]))
    loss_total = totals[0]
    grad_norm = jnp.sqrt(totals[1])
    clip_factor = jnp.minimum(1.0, 1.0 / grad_norm)
    master_new, first_new, second_new, low_new = update_tiles(
        clip_factor, owned, tiles_master[0], tiles_first[0], tiles_second[0], bases[0]
    )
    else_master_new, else_first_new, else_second_new = adamw_flat(
        clip_factor * else_grad, else_master, else_first, else_second
    )
    return (
        loss_total,
        grad_norm,
        master_new[None],
        first_new[None],
        second_new[None],
        low_new[None],
        else_master_new,
        else_first_new,
        else_second_new,
        low(else_master_new),
    )


def solution(mesh):
    return jax.shard_map(
        on_device,
        mesh=mesh,
        in_specs=(
            P(("fsdp", "ctx"), None, None),
            P(("fsdp", "ctx"), None, None),
            P(("fsdp", "ctx")),
            P(("fsdp", "ctx")),
            P(),
            P("tp", ("fsdp", "ctx"), None, None),
            P("tp", ("fsdp", "ctx"), None, None),
            P("tp", ("fsdp", "ctx"), None, None),
            P("tp", ("fsdp", "ctx"), None, None),
            P("tp", ("fsdp", "ctx"), None, None),
            P(("fsdp", "ctx", "tp")),
            P(("fsdp", "ctx", "tp")),
            P(("fsdp", "ctx", "tp")),
            P(("fsdp", "ctx", "tp")),
        ),
        out_specs=(
            P(),
            P(),
            P("tp", ("fsdp", "ctx"), None, None),
            P("tp", ("fsdp", "ctx"), None, None),
            P("tp", ("fsdp", "ctx"), None, None),
            P("tp", ("fsdp", "ctx"), None, None),
            P(("fsdp", "ctx", "tp")),
            P(("fsdp", "ctx", "tp")),
            P(("fsdp", "ctx", "tp")),
            P(("fsdp", "ctx", "tp")),
        ),
        check_vma=False,
    )
```
